32 devices in a mesh: groups: 2 (over y), store: 8 (over z, x), tensor: 2 (over core).
Axes of the slice: x: 2, y: 2, z: 4, core: 2. Of those that a mesh axis runs over, the one named last changes fastest.
Arguments:
- hidden: bfloat16 [32, 8192], P(('groups', 'store')), parts along dimension 0, may hold values from -6 to 6
- query_base: bfloat16 [32, 8192], P(('groups', 'store'), 'tensor'), parts along dimension 0, may hold values from -8 to 8
- adapter_down: bfloat16 [128, 16, 8192], P(('groups', 'store')), parts along dimension 0, may hold values from -0.0625 to 0.0625
- adapter_up: bfloat16 [128, 16, 8192], P(('groups', 'store'), None, 'tensor'), parts along dimension 0, may hold values from -1.5 to 1.5
- adapter_ids: int32 [32], P('groups'), parts along dimension 0, may hold values from 0 to 63
- key_cache: bfloat16 [32, 8, 256, 128], P(('groups', 'store'), 'tensor'), parts along dimension 0, may hold values from -8 to 8
- value_cache: bfloat16 [32, 8, 256, 128], P(('groups', 'store'), 'tensor'), parts along dimension 0, may hold values from -6 to 6
- kv_lengths: int32 [32], P(('groups', 'store')), parts along dimension 0, may hold values from 32 to 256
Outputs:
- attended: bfloat16 [32, 8192], P(('groups', 'store'), 'tensor'), parts along dimension 0
The draws below stay inside these ranges and needn't reach their ends.
There are 2 independent parts, one for each index of `groups`. The reference program is written for one: setup_inputs(seed, part) draws one part's arguments, and reference() takes and returns one part's arrays. A program takes and returns all parts, laid end to end along the dimension named above; each array names one. Nothing has to cross between parts.
All inputs are finite; a program needn't handle non-finite values.
Results may differ from the reference program's by a relative error of at most 0.0068.
Values may be sent and summed in bfloat16 or wider, within the bound.
No kernel may reach another device: no remote copies, remote signals or barrier semaphores. Data moves between devices by JAX's collectives and lax.ppermute only.
A program may use at most 64 MiB of HBM per device.

```python
import math
import jax
import jax.numpy as jnp
import numpy as np

D = 8192
HEADS = 64
KVH = 8
HD = 128
RANK = 16
L = 256
QD = 8192
REQUESTS = 16
ADAPTERS = 64


def draw_query_base(key, part):
    key = jax.random.fold_in(key, 11)
    base = jax.random.truncated_normal(key, -6.0, 6.0, (REQUESTS, QD), jnp.float32)
    return base.astype(jnp.bfloat16)


def draw_key_cache(key, part):
    key = jax.random.fold_in(key, 13)
    keys = jax.random.truncated_normal(key, -6.0, 6.0, (REQUESTS, KVH, L, HD), jnp.float32)
    return keys.astype(jnp.bfloat16)


def draw_kv_lengths(key, part):
    key = jax.random.fold_in(key, 17)
    lengths = jax.random.randint(key, (REQUESTS,), L // 8, L + 1)
    spot = jax.random.randint(jax.random.fold_in(key, 1), (), 0, REQUESTS)
    return lengths.at[spot].set(L).astype(jnp.int32)


def set_ends(array, key, least, largest):
    longest = array.shape.index(max(array.shape))
    spots = []
    for shift in (0, 1):
        where = [jax.random.randint(jax.random.fold_in(key, axis), (), 0, length) for axis, length in enumerate(array.shape)]
        where[longest] = (where[longest] + shift) % array.shape[longest]
        spots.append(tuple(where))
    return array.at[spots[0]].set(least).at[spots[1]].set(largest)


def shard_levels(key, shape, split, low, top_value):
    def one(axis_at, blocks):
        steps = jax.random.uniform(jax.random.fold_in(jax.random.fold_in(key, 6), axis_at), (blocks,), jnp.float32, low / len(split), top_value / len(split))
        return jnp.repeat(jnp.exp(steps), shape[axis_at] // blocks).reshape((-1,) + (1,) * (len(shape) - axis_at - 1))

    gain = one(*split[0])
    for cut in split[1:]:
        gain = gain * one(*cut)
    return gain


def rank_table(amount, lean):
    weights = [(1 << 20) // math.isqrt(grade ** lean) + 1 for grade in range(1, amount + 1)]
    deviation = 1 + sum(weights) // (1 << 30)
    return np.cumsum(np.array([max(1, weight // deviation) for weight in weights]))


def ranked(rng, dims, amount, slope):
    grid = rank_table(amount, slope)
    pick = jax.random.randint(jax.random.fold_in(rng, 1), dims, 0, int(grid[amount - 1]))
    grade = jnp.searchsorted(jnp.asarray(grid, jnp.int32), pick, side="right")
    return jax.random.permutation(jax.random.fold_in(rng, 2), amount)[grade].astype(jnp.int32)


def bell_draw(stream_key, dims, spread, most, shards=(), kind=jnp.bfloat16):
    factor_of = shard_levels(stream_key, dims, shards, -0.22, 0.18) if shards else 1.0
    drawn = jax.random.normal(stream_key, dims, jnp.float32) * spread * factor_of
    return jnp.minimum(jnp.maximum(drawn, -most), most).astype(kind)


def setup_inputs(seed: int = 0, part: int = 0) -> dict:
    splits = jax.random.split(jax.random.key(seed), 9)
    part_keys = jax.random.split(jax.random.fold_in(splits[8], part), 9)
    hidden = bell_draw(part_keys[0], (REQUESTS, D), 1.0, 6.0, ((0, 8),))
    query_base = draw_query_base(jax.random.fold_in(jax.random.fold_in(splits[8], part), 71), part)
    adapter_down = bell_draw(part_keys[2], (ADAPTERS, RANK, D), D ** -0.5, 0.0625, ((0, 8),))
    adapter_up = bell_draw(part_keys[3], (ADAPTERS, RANK, QD), RANK ** -0.5, 1.5, ((0, 8), (2, 2)))
    adapter_ids = set_ends(ranked(part_keys[4], (REQUESTS,), ADAPTERS, 2), jax.random.fold_in(part_keys[4], 3), 0, ADAPTERS - 1).astype(jnp.int32)
    key_cache = draw_key_cache(jax.random.fold_in(jax.random.fold_in(splits[8], part), 71), part)
    value_cache = bell_draw(part_keys[6], (REQUESTS, KVH, L, HD), 1.0, 6.0, ((0, 8), (1, 2)))
    kv_lengths = draw_kv_lengths(jax.random.fold_in(jax.random.fold_in(splits[8], part), 71), part)
    return {"hidden": hidden, "query_base": query_base, "adapter_down": adapter_down, "adapter_up": adapter_up, "adapter_ids": adapter_ids, "key_cache": key_cache, "value_cache": value_cache, "kv_lengths": kv_lengths}


def reference(hidden, query_base, adapter_down, adapter_up, adapter_ids, key_cache, value_cache, kv_lengths):
    down_rows = adapter_down[adapter_ids].astype(jnp.float32)
    low = jnp.einsum('rd,rkd->rk', hidden.astype(jnp.float32), down_rows).astype(jnp.bfloat16)
    up_rows = adapter_up[adapter_ids].astype(jnp.float32)
    delta = jnp.einsum('rk,rkq->rq', low.astype(jnp.float32), up_rows)
    query = (query_base.astype(jnp.float32) + delta).astype(jnp.bfloat16)
    kv_heads = key_cache.shape[1]
    group = HEADS // KVH
    query = query.reshape(query.shape[0], kv_heads, group, HD)
    scores = jnp.einsum('rhgd,rhld->rhgl', query.astype(jnp.float32), key_cache.astype(jnp.float32)) / jnp.sqrt(jnp.float32(HD))
    slots = jnp.arange(L, dtype=jnp.int32)
    live = slots[None, :] < kv_lengths[:, None]
    scores = jnp.where(live[:, None, None, :], scores, jnp.float32(-1e+30))
    weights = jax.nn.softmax(scores, axis=-1).astype(jnp.bfloat16)
    attended = jnp.einsum('rhgl,rhld->rhgd', weights.astype(jnp.float32), value_cache.astype(jnp.float32))
    return attended.reshape(attended.shape[0], kv_heads * group * HD).astype(jnp.bfloat16)
```

```python
import jax
import jax.numpy as jnp
from jax import lax
from jax.sharding import PartitionSpec as P

HEADS = 64
KVH = 8


def per_device(
    hidden, query_base, adapter_down, adapter_up, adapter_ids, key_cache, value_cache, kv_lengths
):
    local_count, rank_size, width = adapter_down.shape
    half_features = adapter_up.shape[2]
    first = lax.axis_index("store") * local_count
    owners = lax.axis_size("store")
    me = lax.axis_index("store")
    local_rows = hidden.shape[0]
    blocks = [hidden]
    for step in range(1, owners):
        blocks.append(lax.ppermute(hidden, "store", [(i, (i + step) % owners) for i in range(owners)]))
    everyone = jnp.concatenate(blocks, axis=0)
    source = (me - jnp.arange(owners, dtype=jnp.int32)) % owners
    order = (source[:, None] * local_rows + jnp.arange(local_rows, dtype=jnp.int32)).reshape(-1)
    total_rows = everyone.shape[0]
    local_slot = adapter_ids[order] - first
    owned = (local_slot[:, None] == jnp.arange(local_count, dtype=jnp.int32)[None, :]).astype(
        jnp.float32
    )
    down_flat = adapter_down.reshape(local_count * rank_size, width)
    projected = jnp.einsum("rd,kd->rk", everyone, down_flat, preferred_element_type=jnp.float32)
    projected = projected.reshape(total_rows, local_count, rank_size) * owned[:, :, None]
    low = projected.astype(jnp.bfloat16).reshape(total_rows, local_count * rank_size)
    up_flat = adapter_up.reshape(local_count * rank_size, half_features)
    parts = jnp.dot(low, up_flat, preferred_element_type=jnp.float32)
    delta = parts[:local_rows]
    for step in range(1, owners):
        block = parts[step * local_rows : (step + 1) * local_rows]
        delta = delta + lax.ppermute(
            block, "store", [(i, (i - step) % owners) for i in range(owners)]
        )
    query = (query_base.astype(jnp.float32) + delta).astype(jnp.bfloat16)
    requests, kv_heads, slots_count, head_size = key_cache.shape
    group = HEADS // KVH
    query = query.reshape(requests, kv_heads, group, head_size)
    scores = jnp.einsum(
        "rhgd,rhld->rhgl", query, key_cache, preferred_element_type=jnp.float32
    ) / jnp.sqrt(jnp.float32(head_size))
    slots = jnp.arange(slots_count, dtype=jnp.int32)
    live = slots[None, :] < kv_lengths[:, None]
    scores = jnp.where(live[:, None, None, :], scores, jnp.float32(-1e30))
    weights = jax.nn.softmax(scores, axis=-1).astype(jnp.bfloat16)
    attended = jnp.einsum(
        "rhgl,rhld->rhgd", weights, value_cache, preferred_element_type=jnp.float32
    )
    return attended.reshape(requests, kv_heads * group * head_size).astype(jnp.bfloat16)


def solution(mesh):
    in_specs = (
        P(("groups", "store"), None),
        P(("groups", "store"), "tensor"),
        P(("groups", "store"), None, None),
        P(("groups", "store"), None, "tensor"),
        P("groups"),
        P(("groups", "store"), "tensor", None, None),
        P(("groups", "store"), "tensor", None, None),
        P(("groups", "store")),
    )
    out_specs = P(("groups", "store"), "tensor")
    return jax.shard_map(
        per_device, mesh=mesh, in_specs=in_specs, out_specs=out_specs, check_vma=False
    )
```

```python
import jax
import jax.numpy as jnp
from jax import lax
from jax.sharding import PartitionSpec as P

HEADS = 64
KVH = 8


def per_device(
    hidden, query_base, adapter_down, adapter_up, adapter_ids, key_cache, value_cache, kv_lengths
):
    local_count, rank_size, width = adapter_down.shape
    half_features = adapter_up.shape[2]
    first = lax.axis_index("store") * local_count
    owners = lax.axis_size("store")
    local_rows = hidden.shape[0]
    copies = jnp.broadcast_to(hidden[None], (owners,) + hidden.shape)
    everyone = lax.all_to_all(copies, "store", 0, 0, tiled=True).reshape(owners * local_rows, width)
    total_rows = everyone.shape[0]
    local_slot = adapter_ids - first
    owned = (local_slot[:, None] == jnp.arange(local_count, dtype=jnp.int32)[None, :]).astype(
        jnp.float32
    )
    down_flat = adapter_down.reshape(local_count * rank_size, width)
    projected = jnp.einsum("rd,kd->rk", everyone, down_flat, preferred_element_type=jnp.float32)
    projected = projected.reshape(total_rows, local_count, rank_size) * owned[:, :, None]
    low = projected.astype(jnp.bfloat16).reshape(total_rows, local_count * rank_size)
    up_flat = adapter_up.reshape(local_count * rank_size, half_features)
    parts = jnp.dot(low, up_flat, preferred_element_type=jnp.float32)
    parts = parts.reshape(owners, local_rows, half_features)
    delta = jnp.sum(lax.all_to_all(parts, "store", 0, 0, tiled=True), axis=0)
    query = (query_base.astype(jnp.float32) + delta).astype(jnp.bfloat16)
    requests, kv_heads, slots_count, head_size = key_cache.shape
    group = HEADS // KVH
    query = query.reshape(requests, kv_heads, group, head_size)
    scores = jnp.einsum(
        "rhgd,rhld->rhgl", query, key_cache, preferred_element_type=jnp.float32
    ) / jnp.sqrt(jnp.float32(head_size))
    slots = jnp.arange(slots_count, dtype=jnp.int32)
    live = slots[None, :] < kv_lengths[:, None]
    scores = jnp.where(live[:, None, None, :], scores, jnp.float32(-1e30))
    weights = jax.nn.softmax(scores, axis=-1).astype(jnp.bfloat16)
    attended = jnp.einsum(
        "rhgl,rhld->rhgd", weights, value_cache, preferred_element_type=jnp.float32
    )
    return attended.reshape(requests, kv_heads * group * head_size).astype(jnp.bfloat16)


def solution(mesh):
    in_specs = (
        P(("groups", "store"), None),
        P(("groups", "store"), "tensor"),
        P(("groups", "store"), None, None),
        P(("groups", "store"), None, "tensor"),
        P("groups"),
        P(("groups", "store"), "tensor", None, None),
        P(("groups", "store"), "tensor", None, None),
        P(("groups", "store")),
    )
    out_specs = P(("groups", "store"), "tensor")
    return jax.shard_map(
        per_device, mesh=mesh, in_specs=in_specs, out_specs=out_specs, check_vma=False
    )
```

```python
import functools

import jax
import jax.numpy as jnp
from jax import lax
from jax.experimental import pallas as pl
from jax.experimental.pallas import tpu as pltpu
from jax.sharding import PartitionSpec as P

HEADS = 64
KVH = 8
LANES = 128
CHUNK = 1024


def spread_kernel(hidden_ref, copies_ref):
    value = hidden_ref[...]
    for owner in range(copies_ref.shape[0]):
        copies_ref[owner] = value


def owner_kernel(ids_ref, hidden_ref, down_ref, up_ref, delta_ref, row_ref):
    count, rank, width = down_ref.shape
    owners, rows = hidden_ref.shape[:2]
    heads = delta_ref.shape[2]
    first = lax.axis_index("store") * count

    def one_source(source, carry):
        for row in range(rows):
            slot = ids_ref[source * rows + row] - first

            @pl.when((slot >= 0) & (slot < count))
            def _():
                total = jnp.zeros((rank, CHUNK), jnp.float32)
                for start in range(0, width, CHUNK):
                    down = down_ref[slot, :, start : start + CHUNK].astype(jnp.float32)
                    state = hidden_ref[source, :, start : start + CHUNK].astype(jnp.float32)
                    total = total + down * state[row : row + 1]
                low = jnp.sum(total, axis=1, keepdims=True)
                low = low.astype(jnp.bfloat16).astype(jnp.float32)
                for head in range(heads):
                    up = up_ref[slot, :, head * LANES : (head + 1) * LANES].astype(jnp.float32)
                    row_ref[head : head + 1, :] = jnp.sum(up * low, axis=0, keepdims=True)
                delta_ref[source, row] = row_ref[...].astype(delta_ref.dtype)

        return carry

    lax.fori_loop(0, owners, one_source, 0)


def attend_kernel(
    count, ids_ref, lengths_ref, base_ref, delta_ref, key_ref, value_ref, out_ref, rows_ref
):
    rows, kv_heads, slots, head_size = key_ref.shape
    heads = base_ref.shape[1]
    group = heads // kv_heads
    me = lax.axis_index("store")
    scale = 1.0 / (float(head_size) ** 0.5)
    position = lax.broadcasted_iota(jnp.int32, (group, slots), 1)
    for row in range(rows):
        owner = ids_ref[me * rows + row] // count
        query = base_ref[row].astype(jnp.float32) + delta_ref[owner, row].astype(jnp.float32)
        live = position < lengths_ref[row]
        for kv in range(kv_heads):
            mine = query[kv * group : (kv + 1) * group].astype(jnp.bfloat16)
            scores = lax.dot_general(
                mine,
                key_ref[row, kv],
                (((1,), (1,)), ((), ())),
                preferred_element_type=jnp.float32,
            )
            scores = jnp.where(live, scores * scale, jnp.float32(-1e30))
            top = jnp.max(scores, axis=1, keepdims=True)
            grown = jnp.exp(scores - top)
            weights = grown / jnp.sum(grown, axis=1, keepdims=True)
            rows_ref[row, kv * group : (kv + 1) * group, :] = jnp.dot(
                weights.astype(jnp.bfloat16),
                value_ref[row, kv],
                preferred_element_type=jnp.float32,
            )
    for head in range(heads):
        out_ref[:, head * LANES : (head + 1) * LANES] = rows_ref[:, head, :].astype(out_ref.dtype)


def per_device(
    hidden, query_base, adapter_down, adapter_up, adapter_ids, key_cache, value_cache, kv_lengths
):
    owners = lax.axis_size("store")
    count, rank, width = adapter_down.shape
    features = adapter_up.shape[2]
    rows, kv_heads, slots, head_size = key_cache.shape
    heads = features // head_size
    vmem = pl.BlockSpec(memory_space=pltpu.VMEM)
    smem = pl.BlockSpec(memory_space=pltpu.SMEM)
    near = lambda array: pltpu.with_memory_space_constraint(array, pltpu.VMEM)

    copies = pl.pallas_call(
        spread_kernel,
        out_shape=jax.ShapeDtypeStruct((owners, rows, width), hidden.dtype),
        in_specs=[vmem],
        out_specs=vmem,
        name="spread",
    )(hidden)
    everyone = lax.all_to_all(copies, "store", 0, 0, tiled=True)
    parts = pl.pallas_call(
        owner_kernel,
        out_shape=jax.ShapeDtypeStruct((owners, rows, heads, head_size), jnp.bfloat16),
        in_specs=[smem, vmem, vmem, vmem],
        out_specs=vmem,
        scratch_shapes=[pltpu.VMEM((heads, head_size), jnp.float32)],
        compiler_params=pltpu.CompilerParams(vmem_limit_bytes=VMEM_LIMIT),
        name="owner",
    )(adapter_ids, everyone, near(adapter_down), near(adapter_up))
    delta = lax.all_to_all(parts, "store", 0, 0, tiled=True)
    return pl.pallas_call(
        functools.partial(attend_kernel, count),
        out_shape=jax.ShapeDtypeStruct((rows, features), jnp.bfloat16),
        in_specs=[smem, smem, vmem, vmem, vmem, vmem],
        out_specs=vmem,
        scratch_shapes=[pltpu.VMEM((rows, heads, head_size), jnp.float32)],
        compiler_params=pltpu.CompilerParams(vmem_limit_bytes=VMEM_LIMIT),
        name="attend",
    )(
        adapter_ids,
        kv_lengths,
        near(query_base.reshape(rows, heads, head_size)),
        delta,
        near(key_cache),
        near(value_cache),
    )


VMEM_LIMIT = 32 * 1024 * 1024


def solution(mesh):
    in_specs = (
        P(("groups", "store"), None),
        P(("groups", "store"), "tensor"),
        P(("groups", "store"), None, None),
        P(("groups", "store"), None, "tensor"),
        P("groups"),
        P(("groups", "store"), "tensor", None, None),
        P(("groups", "store"), "tensor", None, None),
        P(("groups", "store")),
    )
    out_specs = P(("groups", "store"), "tensor")
    return jax.shard_map(
        per_device, mesh=mesh, in_specs=in_specs, out_specs=out_specs, check_vma=False
    )
```

```python
import functools

import jax
import jax.numpy as jnp
from jax import lax
from jax.experimental import pallas as pl
from jax.experimental.pallas import tpu as pltpu
from jax.sharding import PartitionSpec as P

HEADS = 64
KVH = 8
LANES = 128
CHUNK = 1024
DIRECT = 8
VMEM_LIMIT = 32 * 1024 * 1024


def stack_kernel(sides, *refs):
    *blocks, out_ref = refs
    mine = lax.axis_index("store") // sides
    for shift, block in enumerate(blocks):
        out_ref[mine ^ shift] = block[...]


def spread_kernel(hidden_ref, copies_ref):
    value = hidden_ref[...]
    for owner in range(copies_ref.shape[0]):
        copies_ref[owner] = value


def fetch_kernel(*refs):
    *pairs, arrived = refs
    half = len(pairs) // 2
    copies = [
        pltpu.make_async_copy(source, target, arrived.at[i])
        for i, (source, target) in enumerate(zip(pairs[:half], pairs[half:]))
    ]
    for copy in copies:
        copy.start()
    for copy in copies:
        copy.wait()


def fetch(name, *arrays):
    size = sum(array.size * array.dtype.itemsize for array in arrays)
    return pl.pallas_call(
        fetch_kernel,
        out_shape=[pltpu.VMEM(array.shape, array.dtype) for array in arrays],
        in_specs=[pl.BlockSpec(memory_space=pl.ANY)] * len(arrays),
        out_specs=[pl.BlockSpec(memory_space=pltpu.VMEM)] * len(arrays),
        scratch_shapes=[pltpu.SemaphoreType.DMA((len(arrays),))],
        compiler_params=pltpu.CompilerParams(vmem_limit_bytes=VMEM_LIMIT),
        cost_estimate=pl.CostEstimate(flops=0, transcendentals=0, bytes_accessed=2 * size),
        name=name,
    )(*[pltpu.with_memory_space_constraint(array, pltpu.HBM) for array in arrays])


def owner_kernel(sides, ids_ref, *refs):
    hidden_refs, (down_ref, up_ref), delta_refs, row_ref = (
        refs[:sides],
        refs[sides : sides + 2],
        refs[sides + 2 : -1],
        refs[-1],
    )
    count, rank, width = down_ref.shape
    steps, rows = hidden_refs[0].shape[:2]
    heads = row_ref.shape[0]
    me = lax.axis_index("store")
    first = me * count
    side = lax.rem(me, sides)

    def one_step(step, carry):
        for turn in range(sides):
            hidden_ref, delta_ref = hidden_refs[turn], delta_refs[turn]
            source = step * sides + lax.rem(side + turn, sides)
            for row in range(rows):
                slot = ids_ref[source * rows + row] - first
                owned = (slot >= 0) & (slot < count)

                @pl.when(owned)
                def _():
                    total = jnp.zeros((rank, CHUNK), jnp.float32)
                    for start in range(0, width, CHUNK):
                        down = down_ref[slot, :, start : start + CHUNK].astype(jnp.float32)
                        state = hidden_ref[step, :, start : start + CHUNK].astype(jnp.float32)
                        total = total + down * state[row : row + 1]
                    low = jnp.sum(total, axis=1, keepdims=True)
                    low = low.astype(jnp.bfloat16).astype(jnp.float32)
                    for head in range(heads):
                        up = up_ref[slot, :, head * LANES : (head + 1) * LANES]
                        row_ref[head : head + 1, :] = jnp.sum(
                            up.astype(jnp.float32) * low, axis=0, keepdims=True
                        )
                    delta_ref[step, row] = row_ref[...].astype(delta_ref.dtype)

                @pl.when(jnp.logical_not(owned))
                def _():
                    delta_ref[step, row] = jnp.zeros(delta_ref.shape[2:], delta_ref.dtype)

        return carry

    lax.fori_loop(0, steps, one_step, 0)


def merge_kernel(sides, kept_ref, came_ref, *out_refs):
    mine = lax.axis_index("store") // sides
    for shift, out_ref in enumerate(out_refs):
        total = kept_ref[mine ^ shift].astype(jnp.float32) + came_ref[mine ^ shift].astype(
            jnp.float32
        )
        out_ref[...] = total.astype(out_ref.dtype)


def attend_kernel(parts, live_ref, base_ref, *refs):
    delta_refs, (key_ref, value_ref, out_ref, rows_ref) = refs[:parts], refs[parts:]
    rows, kv_heads, slots, head_size = key_ref.shape
    heads = base_ref.shape[1]
    group = heads // kv_heads
    scale = 1.0 / (float(head_size) ** 0.5)
    scores = []
    for row in range(rows):
        query = base_ref[row].astype(jnp.float32)
        delta = delta_refs[0][row].astype(jnp.float32)
        for ref in delta_refs[1:]:
            delta = delta + ref[row].astype(jnp.float32)
        query = query + delta
        live = live_ref[row] > 0
        for kv in range(kv_heads):
            mine = query[kv * group : (kv + 1) * group].astype(jnp.bfloat16)
            score = lax.dot_general(
                mine,
                key_ref[row, kv],
                (((1,), (1,)), ((), ())),
                preferred_element_type=jnp.float32,
            )
            scores.append(jnp.where(live, score * scale, jnp.float32(-1e30)))
    scores = jnp.concatenate(scores, axis=0)
    grown = jnp.exp(scores - jnp.max(scores, axis=1, keepdims=True))
    weights = grown / jnp.sum(grown, axis=1, keepdims=True)
    for row in range(rows):
        for kv in range(kv_heads):
            at = (row * kv_heads + kv) * group
            rows_ref[row, kv * group : (kv + 1) * group, :] = jnp.dot(
                weights[at : at + group].astype(jnp.bfloat16),
                value_ref[row, kv],
                preferred_element_type=jnp.float32,
            )
    for head in range(heads):
        out_ref[:, head * LANES : (head + 1) * LANES] = rows_ref[:, head, :].astype(out_ref.dtype)


def per_device(
    hidden, query_base, adapter_down, adapter_up, adapter_ids, key_cache, value_cache, kv_lengths
):
    owners = lax.axis_size("store")
    count, rank, width = adapter_down.shape
    features = adapter_up.shape[2]
    rows, kv_heads, slots, head_size = key_cache.shape
    heads = features // head_size
    vmem = pl.BlockSpec(memory_space=pltpu.VMEM)
    smem = pl.BlockSpec(memory_space=pltpu.SMEM)
    near = lambda array: pltpu.with_memory_space_constraint(array, pltpu.VMEM)
    limit = pltpu.CompilerParams(vmem_limit_bytes=VMEM_LIMIT)
    sides = 2 if owners == DIRECT else 1
    steps = owners // sides

    def along(array, shift):
        pairs = [(i, ((i // sides) ^ shift) * sides + i % sides) for i in range(owners)]
        return lax.ppermute(array, "store", pairs)

    def across(array):
        return lax.ppermute(array, "store", [(i, i ^ 1) for i in range(owners)])

    if sides == 2:
        blocks = [*fetch("fetch_hidden", hidden)] + [along(hidden, shift) for shift in range(1, steps)]
        column = pl.pallas_call(
            functools.partial(stack_kernel, sides),
            out_shape=jax.ShapeDtypeStruct((steps,) + hidden.shape, hidden.dtype),
            in_specs=[vmem] * steps,
            out_specs=vmem,
            compiler_params=limit,
            name="stack",
        )(*blocks)
        columns = [column, across(column)]
    else:
        copies = pl.pallas_call(
            spread_kernel,
            out_shape=jax.ShapeDtypeStruct((owners,) + hidden.shape, hidden.dtype),
            in_specs=[vmem],
            out_specs=vmem,
            name="spread",
        )(hidden)
        columns = [lax.all_to_all(copies, "store", 0, 0, tiled=True)]

    block = (rows, heads, head_size)
    ids, down, up = fetch("fetch_adapters", adapter_ids, adapter_down, adapter_up)
    parts = pl.pallas_call(
        functools.partial(owner_kernel, sides),
        out_shape=[jax.ShapeDtypeStruct((steps,) + block, jnp.bfloat16)] * sides,
        in_specs=[smem] + [vmem] * (sides + 2),
        out_specs=[vmem] * sides,
        scratch_shapes=[pltpu.VMEM((heads, head_size), jnp.float32)],
        compiler_params=limit,
        name="owner",
    )(ids, *columns, down, up)

    if sides == 2:
        sums = pl.pallas_call(
            functools.partial(merge_kernel, sides),
            out_shape=[jax.ShapeDtypeStruct(block, jnp.bfloat16)] * steps,
            in_specs=[vmem] * 2,
            out_specs=[vmem] * steps,
            compiler_params=limit,
            name="merge",
        )(parts[0], across(parts[1]))
        deltas = [sums[0]] + [along(sums[shift], shift) for shift in range(1, steps)]
    else:
        came = lax.all_to_all(parts[0], "store", 0, 0, tiled=True)
        deltas = [jnp.sum(came.astype(jnp.float32), axis=0)]

    live = jnp.arange(slots, dtype=jnp.int32)[None, None, :] < kv_lengths[:, None, None]
    return pl.pallas_call(
        functools.partial(attend_kernel, len(deltas)),
        out_shape=jax.ShapeDtypeStruct((rows, features), jnp.bfloat16),
        in_specs=[vmem] * (len(deltas) + 4),
        out_specs=vmem,
        scratch_shapes=[pltpu.VMEM(block, jnp.float32)],
        compiler_params=limit,
        name="attend",
    )(
        near(live.astype(jnp.float32)),
        near(query_base.reshape(block)),
        *deltas,
        near(key_cache),
        near(value_cache),
    )


def solution(mesh):
    in_specs = (
        P(("groups", "store"), None),
        P(("groups", "store"), "tensor"),
        P(("groups", "store"), None, None),
        P(("groups", "store"), None, "tensor"),
        P("groups"),
        P(("groups", "store"), "tensor", None, None),
        P(("groups", "store"), "tensor", None, None),
        P(("groups", "store")),
    )
    out_specs = P(("groups", "store"), "tensor")
    return jax.shard_map(
        per_device, mesh=mesh, in_specs=in_specs, out_specs=out_specs, check_vma=False
    )
```

```python
import functools

import jax
import jax.numpy as jnp
from jax import lax
from jax.experimental import pallas as pl
from jax.experimental.pallas import tpu as pltpu
from jax.sharding import PartitionSpec as P

HEADS = 64
KVH = 8
LANES = 128
CHUNK = 1024
VMEM_LIMIT = 32 * 1024 * 1024
VMEM = pl.BlockSpec(memory_space=pltpu.VMEM)
SMEM = pl.BlockSpec(memory_space=pltpu.SMEM)
PARAMS = pltpu.CompilerParams(vmem_limit_bytes=VMEM_LIMIT)
TURNS = ((1, 2, 3, 0), (4, 5, 6, 7))


def fetch_kernel(*refs):
    *pairs, arrived = refs
    half = len(pairs) // 2
    copies = [
        pltpu.make_async_copy(source, target, arrived.at[i])
        for i, (source, target) in enumerate(zip(pairs[:half], pairs[half:]))
    ]
    for copy in copies:
        copy.start()
    for copy in copies:
        copy.wait()


def fetch(name, *arrays):
    size = sum(array.size * array.dtype.itemsize for array in arrays)
    return pl.pallas_call(
        fetch_kernel,
        out_shape=[pltpu.VMEM(array.shape, array.dtype) for array in arrays],
        in_specs=[pl.BlockSpec(memory_space=pl.ANY)] * len(arrays),
        out_specs=[VMEM] * len(arrays),
        scratch_shapes=[pltpu.SemaphoreType.DMA((len(arrays),))],
        compiler_params=PARAMS,
        cost_estimate=pl.CostEstimate(flops=0, transcendentals=0, bytes_accessed=2 * size),
        name=name,
    )(*[pltpu.with_memory_space_constraint(array, pltpu.HBM) for array in arrays])


def near(array):
    return pltpu.with_memory_space_constraint(array, pltpu.VMEM)


def owner_kernel(ids_ref, *refs):
    turns = len(TURNS[0])
    hidden_refs, refs = refs[:turns], refs[turns:]
    down_ref, mine_ref, other_ref = refs[:3]
    delta_refs, (state_ref, sum_ref, row_ref) = refs[3 : 3 + turns], refs[3 + turns :]
    count, rank, width = down_ref.shape
    rows = state_ref.shape[1]
    heads = row_ref.shape[0]
    me, core = lax.axis_index("store"), lax.axis_index("tensor")
    first = me * count
    for turn, hidden_ref in enumerate(hidden_refs):
        state_ref[turn] = hidden_ref[...]

    def one_turn(turn, carry):
        source = me ^ jnp.where(core == 0, lax.rem(turn + 1, turns), turns + turn)
        for row in range(rows):
            slot = ids_ref[source * rows + row] - first
            owned = (slot >= 0) & (slot < count)

            @pl.when(owned)
            def _():
                total = jnp.zeros((rank, CHUNK), jnp.float32)
                for start in range(0, width, CHUNK):
                    down = down_ref[slot, :, start : start + CHUNK].astype(jnp.float32)
                    state = state_ref[turn, :, start : start + CHUNK].astype(jnp.float32)
                    total = total + down * state[row : row + 1]
                low = jnp.sum(total, axis=1, keepdims=True)
                low = low.astype(jnp.bfloat16).astype(jnp.float32)
                for half, up_ref in ((core, mine_ref), (1 - core, other_ref)):
                    for head in range(heads):
                        up = up_ref[slot, :, head * LANES : (head + 1) * LANES]
                        row_ref[head : head + 1, :] = jnp.sum(
                            up.astype(jnp.float32) * low, axis=0, keepdims=True
                        )
                    sum_ref[turn, row, half] = row_ref[...].astype(sum_ref.dtype)

            @pl.when(jnp.logical_not(owned))
            def _():
                sum_ref[turn, row] = jnp.zeros(sum_ref.shape[2:], sum_ref.dtype)

        return carry

    lax.fori_loop(0, turns, one_turn, 0)
    for turn, delta_ref in enumerate(delta_refs):
        delta_ref[...] = sum_ref[turn]


def merge_kernel(*refs):
    came_refs, (kept_ref, sent_ref) = refs[:-2], refs[-2:]
    core = lax.axis_index("tensor")
    for half, out_ref in ((core, kept_ref), (1 - core, sent_ref)):
        total = came_refs[0][:, half].astype(jnp.float32)
        for came_ref in came_refs[1:]:
            total = total + came_ref[:, half].astype(jnp.float32)
        out_ref[...] = total.astype(out_ref.dtype)


def attend_kernel(parts, live_ref, base_ref, *refs):
    delta_refs, (key_ref, value_ref, out_ref, rows_ref) = refs[:parts], refs[parts:]
    rows, kv_heads, slots, head_size = key_ref.shape
    heads = base_ref.shape[1]
    group = heads // kv_heads
    scale = 1.0 / (float(head_size) ** 0.5)
    scores = []
    for row in range(rows):
        query = base_ref[row].astype(jnp.float32)
        delta = delta_refs[0][row].astype(jnp.float32)
        for ref in delta_refs[1:]:
            delta = delta + ref[row].astype(jnp.float32)
        query = query + delta
        live = live_ref[row] > 0
        for kv in range(kv_heads):
            mine = query[kv * group : (kv + 1) * group].astype(jnp.bfloat16)
            score = lax.dot_general(
                mine,
                key_ref[row, kv],
                (((1,), (1,)), ((), ())),
                preferred_element_type=jnp.float32,
            )
            scores.append(jnp.where(live, score * scale, jnp.float32(-1e30)))
    scores = jnp.concatenate(scores, axis=0)
    grown = jnp.exp(scores - jnp.max(scores, axis=1, keepdims=True))
    weights = grown / jnp.sum(grown, axis=1, keepdims=True)
    for row in range(rows):
        for kv in range(kv_heads):
            at = (row * kv_heads + kv) * group
            rows_ref[row, kv * group : (kv + 1) * group, :] = jnp.dot(
                weights[at : at + group].astype(jnp.bfloat16),
                value_ref[row, kv],
                preferred_element_type=jnp.float32,
            )
    for head in range(heads):
        out_ref[:, head * LANES : (head + 1) * LANES] = rows_ref[:, head, :].astype(out_ref.dtype)


def shared_deltas(hidden, adapter_down, adapter_up, adapter_ids, block):
    rows, heads, head_size = block
    owners, cores, turns = lax.axis_size("store"), len(TURNS), len(TURNS[0])

    def turn_pairs(turn):
        return [
            (i * cores + core, (i ^ TURNS[core][turn]) * cores + core)
            for i in range(owners)
            for core in range(cores)
        ]

    def visit(array, turn):
        return lax.ppermute(array, ("store", "tensor"), turn_pairs(turn))

    def swap(array):
        return lax.ppermute(array, "tensor", [(0, 1), (1, 0)])

    states = [visit(hidden, turn) for turn in range(turns)]
    other = swap(adapter_up)
    ids, down, up = fetch("fetch_adapters", adapter_ids, adapter_down, adapter_up)
    wide = (rows, cores, heads, head_size)
    deltas = pl.pallas_call(
        owner_kernel,
        out_shape=[jax.ShapeDtypeStruct(wide, jnp.bfloat16)] * turns,
        in_specs=[SMEM] + [VMEM] * (turns + 3),
        out_specs=[VMEM] * turns,
        scratch_shapes=[
            pltpu.VMEM((turns,) + hidden.shape, hidden.dtype),
            pltpu.VMEM((turns,) + wide, jnp.bfloat16),
            pltpu.VMEM((heads, head_size), jnp.float32),
        ],
        compiler_params=PARAMS,
        name="owner",
    )(ids, *states, down, up, near(other))
    came = [visit(delta, turn) for turn, delta in enumerate(deltas)]
    kept, sent = pl.pallas_call(
        merge_kernel,
        out_shape=[jax.ShapeDtypeStruct(block, jnp.bfloat16)] * 2,
        in_specs=[VMEM] * turns,
        out_specs=[VMEM] * 2,
        compiler_params=PARAMS,
        name="merge",
    )(*came)
    return [kept, swap(sent)]


def exchanged_deltas(hidden, adapter_down, adapter_up, adapter_ids, block):
    count, rank, width = adapter_down.shape
    owners, rows = lax.axis_size("store"), hidden.shape[0]
    copies = jnp.broadcast_to(hidden[None], (owners,) + hidden.shape)
    everyone = lax.all_to_all(copies, "store", 0, 0, tiled=True).reshape(owners * rows, width)
    slot = adapter_ids - lax.axis_index("store") * count
    owned = slot[:, None] == jnp.arange(count, dtype=jnp.int32)[None, :]
    low = jnp.einsum(
        "rd,kd->rk",
        everyone,
        adapter_down.reshape(count * rank, width),
        preferred_element_type=jnp.float32,
    ).reshape(owners * rows, count, rank)
    low = (low * owned[:, :, None].astype(jnp.float32)).astype(jnp.bfloat16)
    parts = jnp.dot(
        low.reshape(owners * rows, count * rank),
        adapter_up.reshape(count * rank, -1),
        preferred_element_type=jnp.float32,
    )
    came = lax.all_to_all(parts.reshape((owners,) + block), "store", 0, 0, tiled=True)
    return [jnp.sum(came, axis=0)]


def per_device(
    hidden, query_base, adapter_down, adapter_up, adapter_ids, key_cache, value_cache, kv_lengths
):
    features = adapter_up.shape[2]
    rows, kv_heads, slots, head_size = key_cache.shape
    block = (rows, features // head_size, head_size)
    shared = lax.axis_size("tensor") == len(TURNS) and lax.axis_size("store") == sum(
        len(turns) for turns in TURNS
    )
    deltas = (shared_deltas if shared else exchanged_deltas)(
        hidden, adapter_down, adapter_up, adapter_ids, block
    )
    live = jnp.arange(slots, dtype=jnp.int32)[None, None, :] < kv_lengths[:, None, None]
    return pl.pallas_call(
        functools.partial(attend_kernel, len(deltas)),
        out_shape=jax.ShapeDtypeStruct((rows, features), jnp.bfloat16),
        in_specs=[VMEM] * (len(deltas) + 4),
        out_specs=VMEM,
        scratch_shapes=[pltpu.VMEM(block, jnp.float32)],
        compiler_params=PARAMS,
        name="attend",
    )(
        near(live.astype(jnp.float32)),
        near(query_base.reshape(block)),
        *deltas,
        near(key_cache),
        near(value_cache),
    )


def solution(mesh):
    in_specs = (
        P(("groups", "store"), None),
        P(("groups", "store"), "tensor"),
        P(("groups", "store"), None, None),
        P(("groups", "store"), None, "tensor"),
        P("groups"),
        P(("groups", "store"), "tensor", None, None),
        P(("groups", "store"), "tensor", None, None),
        P(("groups", "store")),
    )
    out_specs = P(("groups", "store"), "tensor")
    return jax.shard_map(
        per_device, mesh=mesh, in_specs=in_specs, out_specs=out_specs, check_vma=False
    )
```

```python
import functools

import jax
import jax.numpy as jnp
from jax import lax
from jax.experimental import pallas as pl
from jax.experimental.pallas import tpu as pltpu
from jax.sharding import PartitionSpec as P

HEADS = 64
KVH = 8
LANES = 128
CHUNK = 1024
VMEM_LIMIT = 32 * 1024 * 1024
VMEM = pl.BlockSpec(memory_space=pltpu.VMEM)
SMEM = pl.BlockSpec(memory_space=pltpu.SMEM)
PARAMS = pltpu.CompilerParams(vmem_limit_bytes=VMEM_LIMIT)
TURNS = ((7, 5, 1, 0), (6, 4, 3, 2))


def fetch_kernel(*refs):
    *pairs, arrived = refs
    half = len(pairs) // 2
    copies = [
        pltpu.make_async_copy(source, target, arrived.at[i])
        for i, (source, target) in enumerate(zip(pairs[:half], pairs[half:]))
    ]
    for copy in copies:
        copy.start()
    for copy in copies:
        copy.wait()


def fetch(name, *arrays):
    size = sum(array.size * array.dtype.itemsize for array in arrays)
    return pl.pallas_call(
        fetch_kernel,
        out_shape=[pltpu.VMEM(array.shape, array.dtype) for array in arrays],
        in_specs=[pl.BlockSpec(memory_space=pl.ANY)] * len(arrays),
        out_specs=[VMEM] * len(arrays),
        scratch_shapes=[pltpu.SemaphoreType.DMA((len(arrays),))],
        compiler_params=PARAMS,
        cost_estimate=pl.CostEstimate(flops=0, transcendentals=0, bytes_accessed=2 * size),
        name=name,
    )(*[pltpu.with_memory_space_constraint(array, pltpu.HBM) for array in arrays])


def near(array):
    return pltpu.with_memory_space_constraint(array, pltpu.VMEM)


def partner(core, turn):
    packed = [sum(value << (4 * i) for i, value in enumerate(turns)) for turns in TURNS]
    return (jnp.where(core == 0, packed[0], packed[1]) >> (4 * turn)) & 15


def owner_kernel(ids_ref, own_ref, *refs):
    turns = len(TURNS[0])
    hidden_refs, refs = refs[:turns], refs[turns:]
    down_ref, mine_ref, other_ref = refs[:3]
    delta_refs, (state_ref, sum_ref, row_ref) = refs[3 : 3 + turns], refs[3 + turns :]
    count, rank, width = down_ref.shape
    rows = state_ref.shape[1]
    heads = row_ref.shape[0]
    me, core = lax.axis_index("store"), lax.axis_index("tensor")
    first = me * count
    for turn, hidden_ref in enumerate(hidden_refs[:-1]):
        state_ref[turn] = hidden_ref[...]

    @pl.when(core == 0)
    def _():
        state_ref[turns - 1] = own_ref[...]

    @pl.when(core != 0)
    def _():
        state_ref[turns - 1] = hidden_refs[-1][...]

    def one_turn(turn, carry):
        source = me ^ partner(core, turn)
        for row in range(rows):
            slot = ids_ref[source * rows + row] - first
            owned = (slot >= 0) & (slot < count)

            @pl.when(owned)
            def _():
                total = jnp.zeros((rank, CHUNK), jnp.float32)
                for start in range(0, width, CHUNK):
                    down = down_ref[slot, :, start : start + CHUNK].astype(jnp.float32)
                    state = state_ref[turn, :, start : start + CHUNK].astype(jnp.float32)
                    total = total + down * state[row : row + 1]
                low = jnp.sum(total, axis=1, keepdims=True)
                low = low.astype(jnp.bfloat16).astype(jnp.float32)
                for half, up_ref in ((core, mine_ref), (1 - core, other_ref)):
                    for head in range(heads):
                        up = up_ref[slot, :, head * LANES : (head + 1) * LANES]
                        row_ref[head : head + 1, :] = jnp.sum(
                            up.astype(jnp.float32) * low, axis=0, keepdims=True
                        )
                    sum_ref[turn, row, half] = row_ref[...].astype(sum_ref.dtype)

            @pl.when(jnp.logical_not(owned))
            def _():
                sum_ref[turn, row] = jnp.zeros(sum_ref.shape[2:], sum_ref.dtype)

        return carry

    lax.fori_loop(0, turns, one_turn, 0)
    for turn, delta_ref in enumerate(delta_refs):
        delta_ref[...] = sum_ref[turn]


def merge_kernel(own_ref, *refs):
    came_refs, (kept_ref, sent_ref) = refs[:-2], refs[-2:]
    core = lax.axis_index("tensor")
    for half, out_ref in ((core, kept_ref), (1 - core, sent_ref)):
        total = jnp.where(core == 0, own_ref[:, half], came_refs[-1][:, half])
        total = total.astype(jnp.float32)
        for came_ref in came_refs[:-1]:
            total = total + came_ref[:, half].astype(jnp.float32)
        out_ref[...] = total.astype(out_ref.dtype)


def attend_kernel(parts, live_ref, base_ref, *refs):
    delta_refs, (key_ref, value_ref, out_ref, rows_ref) = refs[:parts], refs[parts:]
    rows, kv_heads, slots, head_size = key_ref.shape
    heads = base_ref.shape[1]
    group = heads // kv_heads
    scale = 1.0 / (float(head_size) ** 0.5)
    scores = []
    for row in range(rows):
        query = base_ref[row].astype(jnp.float32)
        delta = delta_refs[0][row].astype(jnp.float32)
        for ref in delta_refs[1:]:
            delta = delta + ref[row].astype(jnp.float32)
        query = query + delta
        live = live_ref[row] > 0
        for kv in range(kv_heads):
            mine = query[kv * group : (kv + 1) * group].astype(jnp.bfloat16)
            score = lax.dot_general(
                mine,
                key_ref[row, kv],
                (((1,), (1,)), ((), ())),
                preferred_element_type=jnp.float32,
            )
            scores.append(jnp.where(live, score * scale, jnp.float32(-1e30)))
    scores = jnp.concatenate(scores, axis=0)
    grown = jnp.exp(scores - jnp.max(scores, axis=1, keepdims=True))
    weights = grown / jnp.sum(grown, axis=1, keepdims=True)
    for row in range(rows):
        for kv in range(kv_heads):
            at = (row * kv_heads + kv) * group
            rows_ref[row, kv * group : (kv + 1) * group, :] = jnp.dot(
                weights[at : at + group].astype(jnp.bfloat16),
                value_ref[row, kv],
                preferred_element_type=jnp.float32,
            )
    for head in range(heads):
        out_ref[:, head * LANES : (head + 1) * LANES] = rows_ref[:, head, :].astype(out_ref.dtype)


def shared_deltas(hidden, adapter_down, adapter_up, adapter_ids, block):
    rows, heads, head_size = block
    owners, cores, turns = lax.axis_size("store"), len(TURNS), len(TURNS[0])

    def turn_pairs(turn):
        return [
            (i * cores + core, (i ^ TURNS[core][turn]) * cores + core)
            for i in range(owners)
            for core in range(cores)
            if TURNS[core][turn]
        ]

    def visit(array, turn):
        return lax.ppermute(array, ("store", "tensor"), turn_pairs(turn))

    def swap(array):
        return lax.ppermute(array, "tensor", [(0, 1), (1, 0)])

    states = [visit(hidden, turn) for turn in range(turns)]
    other = swap(adapter_up)
    ids, own, down, up = fetch("fetch", adapter_ids, hidden, adapter_down, adapter_up)
    wide = (rows, cores, heads, head_size)
    deltas = pl.pallas_call(
        owner_kernel,
        out_shape=[jax.ShapeDtypeStruct(wide, jnp.bfloat16)] * turns,
        in_specs=[SMEM] + [VMEM] * (turns + 4),
        out_specs=[VMEM] * turns,
        scratch_shapes=[
            pltpu.VMEM((turns,) + hidden.shape, hidden.dtype),
            pltpu.VMEM((turns,) + wide, jnp.bfloat16),
            pltpu.VMEM((heads, head_size), jnp.float32),
        ],
        compiler_params=PARAMS,
        name="owner",
    )(ids, own, *states, down, up, near(other))
    came = [visit(delta, turn) for turn, delta in enumerate(deltas)]
    kept, sent = pl.pallas_call(
        merge_kernel,
        out_shape=[jax.ShapeDtypeStruct(block, jnp.bfloat16)] * 2,
        in_specs=[VMEM] * (turns + 1),
        out_specs=[VMEM] * 2,
        compiler_params=PARAMS,
        name="merge",
    )(deltas[-1], *came)
    return [kept, swap(sent)]


def exchanged_deltas(hidden, adapter_down, adapter_up, adapter_ids, block):
    count, rank, width = adapter_down.shape
    owners, rows = lax.axis_size("store"), hidden.shape[0]
    copies = jnp.broadcast_to(hidden[None], (owners,) + hidden.shape)
    everyone = lax.all_to_all(copies, "store", 0, 0, tiled=True).reshape(owners * rows, width)
    slot = adapter_ids - lax.axis_index("store") * count
    owned = slot[:, None] == jnp.arange(count, dtype=jnp.int32)[None, :]
    low = jnp.einsum(
        "rd,kd->rk",
        everyone,
        adapter_down.reshape(count * rank, width),
        preferred_element_type=jnp.float32,
    ).reshape(owners * rows, count, rank)
    low = (low * owned[:, :, None].astype(jnp.float32)).astype(jnp.bfloat16)
    parts = jnp.dot(
        low.reshape(owners * rows, count * rank),
        adapter_up.reshape(count * rank, -1),
        preferred_element_type=jnp.float32,
    )
    came = lax.all_to_all(parts.reshape((owners,) + block), "store", 0, 0, tiled=True)
    return [jnp.sum(came, axis=0)]


def per_device(
    hidden, query_base, adapter_down, adapter_up, adapter_ids, key_cache, value_cache, kv_lengths
):
    features = adapter_up.shape[2]
    rows, kv_heads, slots, head_size = key_cache.shape
    block = (rows, features // head_size, head_size)
    shared = lax.axis_size("tensor") == len(TURNS) and lax.axis_size("store") == sum(
        len(turns) for turns in TURNS
    )
    deltas = (shared_deltas if shared else exchanged_deltas)(
        hidden, adapter_down, adapter_up, adapter_ids, block
    )
    live = jnp.arange(slots, dtype=jnp.int32)[None, None, :] < kv_lengths[:, None, None]
    return pl.pallas_call(
        functools.partial(attend_kernel, len(deltas)),
        out_shape=jax.ShapeDtypeStruct((rows, features), jnp.bfloat16),
        in_specs=[VMEM] * (len(deltas) + 4),
        out_specs=VMEM,
        scratch_shapes=[pltpu.VMEM(block, jnp.float32)],
        compiler_params=PARAMS,
        name="attend",
    )(
        near(live.astype(jnp.float32)),
        near(query_base.reshape(block)),
        *deltas,
        near(key_cache),
        near(value_cache),
    )


def solution(mesh):
    in_specs = (
        P(("groups", "store"), None),
        P(("groups", "store"), "tensor"),
        P(("groups", "store"), None, None),
        P(("groups", "store"), None, "tensor"),
        P("groups"),
        P(("groups", "store"), "tensor", None, None),
        P(("groups", "store"), "tensor", None, None),
        P(("groups", "store")),
    )
    out_specs = P(("groups", "store"), "tensor")
    return jax.shard_map(
        per_device, mesh=mesh, in_specs=in_specs, out_specs=out_specs, check_vma=False
    )
```

```python
import functools

import jax
import jax.numpy as jnp
from jax import lax
from jax.experimental import pallas as pl
from jax.experimental.pallas import tpu as pltpu
from jax.sharding import PartitionSpec as P

HEADS = 64
KVH = 8
LANES = 128
CHUNK = 1024
VMEM_LIMIT = 32 * 1024 * 1024
VMEM = pl.BlockSpec(memory_space=pltpu.VMEM)
SMEM = pl.BlockSpec(memory_space=pltpu.SMEM)
PARAMS = pltpu.CompilerParams(vmem_limit_bytes=VMEM_LIMIT)
COLUMN = ((3, 0), (2, 1))
SIDES = 2
SLOTS = len(COLUMN[0])


def fetch_kernel(*refs):
    *pairs, arrived = refs
    half = len(pairs) // 2
    copies = [
        pltpu.make_async_copy(source, target, arrived.at[i])
        for i, (source, target) in enumerate(zip(pairs[:half], pairs[half:]))
    ]
    for copy in copies:
        copy.start()
    for copy in copies:
        copy.wait()


def fetch(name, *arrays):
    size = sum(array.size * array.dtype.itemsize for array in arrays)
    return pl.pallas_call(
        fetch_kernel,
        out_shape=[pltpu.VMEM(array.shape, array.dtype) for array in arrays],
        in_specs=[pl.BlockSpec(memory_space=pl.ANY)] * len(arrays),
        out_specs=[VMEM] * len(arrays),
        scratch_shapes=[pltpu.SemaphoreType.DMA((len(arrays),))],
        compiler_params=PARAMS,
        cost_estimate=pl.CostEstimate(flops=0, transcendentals=0, bytes_accessed=2 * size),
        name=name,
    )(*[pltpu.with_memory_space_constraint(array, pltpu.HBM) for array in arrays])


def near(array):
    return pltpu.with_memory_space_constraint(array, pltpu.VMEM)


def stack_kernel(own_ref, *refs):
    *came_refs, out_ref = refs
    core = lax.axis_index("tensor")
    for slot, came_ref in enumerate(came_refs):
        for value in range(len(COLUMN)):
            ref = came_ref if COLUMN[value][slot] else own_ref

            @pl.when(core == value)
            def _():
                out_ref[slot] = ref[...]


def home(side, slot):
    packed = [sum(value << (4 * i) for i, value in enumerate(steps)) for steps in COLUMN]
    packed = jnp.where(lax.axis_index("tensor") == 0, packed[0], packed[1])
    return lax.axis_index("store") ^ (((packed >> (4 * slot)) & 15) * SIDES + side)


def owner_kernel(ids_ref, near_ref, far_ref, down_ref, mine_ref, other_ref, *refs):
    delta_refs, (state_ref, sum_ref, row_ref) = refs[:SIDES], refs[SIDES:]
    count, rank, width = down_ref.shape
    rows = state_ref.shape[1]
    heads = row_ref.shape[0]
    core = lax.axis_index("tensor")
    first = lax.axis_index("store") * count
    for side, hidden_ref in enumerate((near_ref, far_ref)):
        for slot in range(SLOTS):
            state_ref[side * SLOTS + slot] = hidden_ref[slot]

    def one_home(turn, carry):
        source = home(turn // SLOTS, turn % SLOTS)
        for row in range(rows):
            slot = ids_ref[source * rows + row] - first
            owned = (slot >= 0) & (slot < count)

            @pl.when(owned)
            def _():
                total = jnp.zeros((rank, CHUNK), jnp.float32)
                for start in range(0, width, CHUNK):
                    down = down_ref[slot, :, start : start + CHUNK].astype(jnp.float32)
                    state = state_ref[turn, :, start : start + CHUNK].astype(jnp.float32)
                    total = total + down * state[row : row + 1]
                low = jnp.sum(total, axis=1, keepdims=True)
                low = low.astype(jnp.bfloat16).astype(jnp.float32)
                for half, up_ref in ((core, mine_ref), (1 - core, other_ref)):
                    for head in range(heads):
                        up = up_ref[slot, :, head * LANES : (head + 1) * LANES]
                        row_ref[head : head + 1, :] = jnp.sum(
                            up.astype(jnp.float32) * low, axis=0, keepdims=True
                        )
                    sum_ref[turn, row, half] = row_ref[...].astype(sum_ref.dtype)

            @pl.when(jnp.logical_not(owned))
            def _():
                sum_ref[turn, row] = jnp.zeros(sum_ref.shape[2:], sum_ref.dtype)

        return carry

    lax.fori_loop(0, SIDES * SLOTS, one_home, 0)
    for side, delta_ref in enumerate(delta_refs):
        for slot in range(SLOTS):
            delta_ref[slot] = sum_ref[side * SLOTS + slot]


def side_kernel(near_ref, came_ref, *out_refs):
    for slot, out_ref in enumerate(out_refs):
        total = near_ref[slot].astype(jnp.float32) + came_ref[slot].astype(jnp.float32)
        out_ref[...] = total.astype(out_ref.dtype)


def merge_kernel(*refs):
    own_refs, came_refs, (kept_ref, sent_ref) = refs[:SLOTS], refs[SLOTS:-2], refs[-2:]
    core = lax.axis_index("tensor")
    for half, out_ref in ((core, kept_ref), (1 - core, sent_ref)):
        total = jnp.zeros(out_ref.shape, jnp.float32)
        for slot in range(SLOTS):
            part = came_refs[slot][:, half]
            for value in range(len(COLUMN)):
                if not COLUMN[value][slot]:
                    part = jnp.where(core == value, own_refs[slot][:, half], part)
            total = total + part.astype(jnp.float32)
        out_ref[...] = total.astype(out_ref.dtype)


def attend_kernel(parts, live_ref, base_ref, *refs):
    delta_refs, (key_ref, value_ref, out_ref, rows_ref) = refs[:parts], refs[parts:]
    rows, kv_heads, slots, head_size = key_ref.shape
    heads = base_ref.shape[1]
    group = heads // kv_heads
    scale = 1.0 / (float(head_size) ** 0.5)
    scores = []
    for row in range(rows):
        query = base_ref[row].astype(jnp.float32)
        delta = delta_refs[0][row].astype(jnp.float32)
        for ref in delta_refs[1:]:
            delta = delta + ref[row].astype(jnp.float32)
        query = query + delta
        live = live_ref[row] > 0
        for kv in range(kv_heads):
            mine = query[kv * group : (kv + 1) * group].astype(jnp.bfloat16)
            score = lax.dot_general(
                mine,
                key_ref[row, kv],
                (((1,), (1,)), ((), ())),
                preferred_element_type=jnp.float32,
            )
            scores.append(jnp.where(live, score * scale, jnp.float32(-1e30)))
    scores = jnp.concatenate(scores, axis=0)
    grown = jnp.exp(scores - jnp.max(scores, axis=1, keepdims=True))
    weights = grown / jnp.sum(grown, axis=1, keepdims=True)
    for row in range(rows):
        for kv in range(kv_heads):
            at = (row * kv_heads + kv) * group
            rows_ref[row, kv * group : (kv + 1) * group, :] = jnp.dot(
                weights[at : at + group].astype(jnp.bfloat16),
                value_ref[row, kv],
                preferred_element_type=jnp.float32,
            )
    for head in range(heads):
        out_ref[:, head * LANES : (head + 1) * LANES] = rows_ref[:, head, :].astype(out_ref.dtype)


def shared_deltas(hidden, adapter_down, adapter_up, adapter_ids, block):
    rows, heads, head_size = block
    owners, cores = lax.axis_size("store"), len(COLUMN)

    def along(array, slot):
        pairs = [
            (i * cores + core, (i ^ (COLUMN[core][slot] * SIDES)) * cores + core)
            for i in range(owners)
            for core in range(cores)
            if COLUMN[core][slot]
        ]
        return lax.ppermute(array, ("store", "tensor"), pairs)

    def across(array):
        return lax.ppermute(array, "store", [(i, i ^ 1) for i in range(owners)])

    def swap(array):
        return lax.ppermute(array, "tensor", [(0, 1), (1, 0)])

    def call(kernel, shapes, name, *operands, **options):
        return pl.pallas_call(
            kernel,
            out_shape=[jax.ShapeDtypeStruct(shape, jnp.bfloat16) for shape in shapes],
            out_specs=[VMEM] * len(shapes),
            compiler_params=PARAMS,
            name=name,
            **{"in_specs": [VMEM] * len(operands), **options},
        )(*operands)

    wide = (rows, cores, heads, head_size)
    came = [along(hidden, slot) for slot in range(SLOTS)]
    other = swap(adapter_up)
    (own,) = fetch("fetch_hidden", hidden)
    (near_side,) = call(stack_kernel, [(SLOTS,) + hidden.shape], "stack", own, *came)
    ids, down, up = fetch("fetch_adapters", adapter_ids, adapter_down, adapter_up)
    near_deltas, far_deltas = call(
        owner_kernel,
        [(SLOTS,) + wide] * SIDES,
        "owner",
        ids,
        near_side,
        across(near_side),
        down,
        up,
        near(other),
        in_specs=[SMEM] + [VMEM] * 5,
        scratch_shapes=[
            pltpu.VMEM((SIDES * SLOTS,) + hidden.shape, hidden.dtype),
            pltpu.VMEM((SIDES * SLOTS,) + wide, jnp.bfloat16),
            pltpu.VMEM((heads, head_size), jnp.float32),
        ],
    )
    sums = call(side_kernel, [wide] * SLOTS, "side", near_deltas, across(far_deltas))
    came = [along(part, slot) for slot, part in enumerate(sums)]
    kept, sent = call(merge_kernel, [block] * 2, "merge", *sums, *came)
    return [kept, swap(sent)]


def exchanged_deltas(hidden, adapter_down, adapter_up, adapter_ids, block):
    count, rank, width = adapter_down.shape
    owners, rows = lax.axis_size("store"), hidden.shape[0]
    copies = jnp.broadcast_to(hidden[None], (owners,) + hidden.shape)
    everyone = lax.all_to_all(copies, "store", 0, 0, tiled=True).reshape(owners * rows, width)
    slot = adapter_ids - lax.axis_index("store") * count
    owned = slot[:, None] == jnp.arange(count, dtype=jnp.int32)[None, :]
    low = jnp.einsum(
        "rd,kd->rk",
        everyone,
        adapter_down.reshape(count * rank, width),
        preferred_element_type=jnp.float32,
    ).reshape(owners * rows, count, rank)
    low = (low * owned[:, :, None].astype(jnp.float32)).astype(jnp.bfloat16)
    parts = jnp.dot(
        low.reshape(owners * rows, count * rank),
        adapter_up.reshape(count * rank, -1),
        preferred_element_type=jnp.float32,
    )
    came = lax.all_to_all(parts.reshape((owners,) + block), "store", 0, 0, tiled=True)
    return [jnp.sum(came, axis=0)]


def per_device(
    hidden, query_base, adapter_down, adapter_up, adapter_ids, key_cache, value_cache, kv_lengths
):
    features = adapter_up.shape[2]
    rows, kv_heads, slots, head_size = key_cache.shape
    block = (rows, features // head_size, head_size)
    shared = (lax.axis_size("store"), lax.axis_size("tensor")) == (8, len(COLUMN))
    deltas = (shared_deltas if shared else exchanged_deltas)(
        hidden, adapter_down, adapter_up, adapter_ids, block
    )
    live = jnp.arange(slots, dtype=jnp.int32)[None, None, :] < kv_lengths[:, None, None]
    return pl.pallas_call(
        functools.partial(attend_kernel, len(deltas)),
        out_shape=jax.ShapeDtypeStruct((rows, features), jnp.bfloat16),
        in_specs=[VMEM] * (len(deltas) + 4),
        out_specs=VMEM,
        scratch_shapes=[pltpu.VMEM(block, jnp.float32)],
        compiler_params=PARAMS,
        name="attend",
    )(
        near(live.astype(jnp.float32)),
        near(query_base.reshape(block)),
        *deltas,
        near(key_cache),
        near(value_cache),
    )


def solution(mesh):
    in_specs = (
        P(("groups", "store"), None),
        P(("groups", "store"), "tensor"),
        P(("groups", "store"), None, None),
        P(("groups", "store"), None, "tensor"),
        P("groups"),
        P(("groups", "store"), "tensor", None, None),
        P(("groups", "store"), "tensor", None, None),
        P(("groups", "store")),
    )
    out_specs = P(("groups", "store"), "tensor")
    return jax.shard_map(
        per_device, mesh=mesh, in_specs=in_specs, out_specs=out_specs, check_vma=False
    )
```

```python
import functools

import jax
import jax.numpy as jnp
from jax import lax
from jax.experimental import pallas as pl
from jax.experimental.pallas import tpu as pltpu
from jax.sharding import PartitionSpec as P

HEADS = 64
KVH = 8
LANES = 128
CHUNK = 1024
VMEM_LIMIT = 32 * 1024 * 1024
VMEM = pl.BlockSpec(memory_space=pltpu.VMEM)
SMEM = pl.BlockSpec(memory_space=pltpu.SMEM)
PARAMS = pltpu.CompilerParams(vmem_limit_bytes=VMEM_LIMIT)
TURNS = ((7, 4, 1, 2, 0), (6, 5, 3, 2, 0))
SENT = len(TURNS[0]) - 1
SHARED = [turn for turn in range(SENT + 1) if TURNS[0][turn] == TURNS[1][turn]][0]


def fetch_kernel(*refs):
    *pairs, arrived = refs
    half = len(pairs) // 2
    copies = [
        pltpu.make_async_copy(source, target, arrived.at[i])
        for i, (source, target) in enumerate(zip(pairs[:half], pairs[half:]))
    ]
    for copy in copies:
        copy.start()
    for copy in copies:
        copy.wait()


def fetch(name, *arrays):
    size = sum(array.size * array.dtype.itemsize for array in arrays)
    return pl.pallas_call(
        fetch_kernel,
        out_shape=[pltpu.VMEM(array.shape, array.dtype) for array in arrays],
        in_specs=[pl.BlockSpec(memory_space=pl.ANY)] * len(arrays),
        out_specs=[VMEM] * len(arrays),
        scratch_shapes=[pltpu.SemaphoreType.DMA((len(arrays),))],
        compiler_params=PARAMS,
        cost_estimate=pl.CostEstimate(flops=0, transcendentals=0, bytes_accessed=2 * size),
        name=name,
    )(*[pltpu.with_memory_space_constraint(array, pltpu.HBM) for array in arrays])


def near(array):
    return pltpu.with_memory_space_constraint(array, pltpu.VMEM)


def partner(core, turn):
    packed = [sum(value << (4 * i) for i, value in enumerate(turns)) for turns in TURNS]
    return (jnp.where(core == 0, packed[0], packed[1]) >> (4 * turn)) & 15


def owner_kernel(ids_ref, own_ref, *refs):
    hidden_refs, refs = refs[:SENT] + (own_ref,), refs[SENT:]
    down_ref, mine_ref, other_ref = refs[:3]
    delta_refs, (state_ref, sum_ref, row_ref) = refs[3:-3], refs[-3:]
    count, rank, width = down_ref.shape
    rows = state_ref.shape[1]
    heads = row_ref.shape[0]
    me, core = lax.axis_index("store"), lax.axis_index("tensor")
    first = me * count
    for turn, hidden_ref in enumerate(hidden_refs):
        state_ref[turn] = hidden_ref[...]

    def one_turn(turn, carry):
        source = me ^ partner(core, turn)
        for row in range(rows):
            slot = ids_ref[source * rows + row] - first
            mine = (turn < SHARED) | (core == row % len(TURNS))
            owned = mine & (slot >= 0) & (slot < count)

            @pl.when(owned)
            def _():
                total = jnp.zeros((rank, CHUNK), jnp.float32)
                for start in range(0, width, CHUNK):
                    down = down_ref[slot, :, start : start + CHUNK].astype(jnp.float32)
                    state = state_ref[turn, :, start : start + CHUNK].astype(jnp.float32)
                    total = total + down * state[row : row + 1]
                low = jnp.sum(total, axis=1, keepdims=True)
                low = low.astype(jnp.bfloat16).astype(jnp.float32)
                for half, up_ref in ((core, mine_ref), (1 - core, other_ref)):
                    for head in range(heads):
                        up = up_ref[slot, :, head * LANES : (head + 1) * LANES]
                        row_ref[head : head + 1, :] = jnp.sum(
                            up.astype(jnp.float32) * low, axis=0, keepdims=True
                        )
                    sum_ref[turn, row, half] = row_ref[...].astype(sum_ref.dtype)

            @pl.when(jnp.logical_not(owned))
            def _():
                sum_ref[turn, row] = jnp.zeros(sum_ref.shape[2:], sum_ref.dtype)

        return carry

    lax.fori_loop(0, SENT + 1, one_turn, 0)
    for turn, delta_ref in enumerate(delta_refs):
        delta_ref[...] = sum_ref[turn]


def merge_kernel(own_ref, *refs):
    came_refs, (kept_ref, sent_ref) = refs[:-2], refs[-2:]
    core = lax.axis_index("tensor")
    for half, out_ref in ((core, kept_ref), (1 - core, sent_ref)):
        total = own_ref[:, half].astype(jnp.float32)
        for came_ref in came_refs:
            total = total + came_ref[:, half].astype(jnp.float32)
        out_ref[...] = total.astype(out_ref.dtype)


def attend_kernel(parts, live_ref, base_ref, *refs):
    delta_refs, (key_ref, value_ref, out_ref, rows_ref) = refs[:parts], refs[parts:]
    rows, kv_heads, slots, head_size = key_ref.shape
    heads = base_ref.shape[1]
    group = heads // kv_heads
    scale = 1.0 / (float(head_size) ** 0.5)
    scores = []
    for row in range(rows):
        query = base_ref[row].astype(jnp.float32)
        delta = delta_refs[0][row].astype(jnp.float32)
        for ref in delta_refs[1:]:
            delta = delta + ref[row].astype(jnp.float32)
        query = query + delta
        live = live_ref[row] > 0
        for kv in range(kv_heads):
            mine = query[kv * group : (kv + 1) * group].astype(jnp.bfloat16)
            score = lax.dot_general(
                mine,
                key_ref[row, kv],
                (((1,), (1,)), ((), ())),
                preferred_element_type=jnp.float32,
            )
            scores.append(jnp.where(live, score * scale, jnp.float32(-1e30)))
    scores = jnp.concatenate(scores, axis=0)
    grown = jnp.exp(scores - jnp.max(scores, axis=1, keepdims=True))
    weights = grown / jnp.sum(grown, axis=1, keepdims=True)
    for row in range(rows):
        for kv in range(kv_heads):
            at = (row * kv_heads + kv) * group
            rows_ref[row, kv * group : (kv + 1) * group, :] = jnp.dot(
                weights[at : at + group].astype(jnp.bfloat16),
                value_ref[row, kv],
                preferred_element_type=jnp.float32,
            )
    for head in range(heads):
        out_ref[:, head * LANES : (head + 1) * LANES] = rows_ref[:, head, :].astype(out_ref.dtype)


def shared_deltas(hidden, adapter_down, adapter_up, adapter_ids, block):
    rows, heads, head_size = block
    owners, cores = lax.axis_size("store"), len(TURNS)

    def turn_pairs(turn):
        return [
            (i * cores + core, (i ^ TURNS[core][turn]) * cores + core)
            for i in range(owners)
            for core in range(cores)
        ]

    def visit(array, turn):
        return lax.ppermute(array, ("store", "tensor"), turn_pairs(turn))

    def swap(array):
        return lax.ppermute(array, "tensor", [(0, 1), (1, 0)])

    states = [visit(hidden, turn) for turn in range(SENT)]
    other = swap(adapter_up)
    ids, own, down, up = fetch("fetch", adapter_ids, hidden, adapter_down, adapter_up)
    wide = (rows, cores, heads, head_size)
    deltas = pl.pallas_call(
        owner_kernel,
        out_shape=[jax.ShapeDtypeStruct(wide, jnp.bfloat16)] * (SENT + 1),
        in_specs=[SMEM] + [VMEM] * (SENT + 4),
        out_specs=[VMEM] * (SENT + 1),
        scratch_shapes=[
            pltpu.VMEM((SENT + 1,) + hidden.shape, hidden.dtype),
            pltpu.VMEM((SENT + 1,) + wide, jnp.bfloat16),
            pltpu.VMEM((heads, head_size), jnp.float32),
        ],
        compiler_params=PARAMS,
        name="owner",
    )(ids, own, *states, down, up, near(other))
    came = [visit(delta, turn) for turn, delta in enumerate(deltas[:SENT])]
    kept, sent = pl.pallas_call(
        merge_kernel,
        out_shape=[jax.ShapeDtypeStruct(block, jnp.bfloat16)] * 2,
        in_specs=[VMEM] * (SENT + 1),
        out_specs=[VMEM] * 2,
        compiler_params=PARAMS,
        name="merge",
    )(deltas[-1], *came)
    return [kept, swap(sent)]


def exchanged_deltas(hidden, adapter_down, adapter_up, adapter_ids, block):
    count, rank, width = adapter_down.shape
    owners, rows = lax.axis_size("store"), hidden.shape[0]
    copies = jnp.broadcast_to(hidden[None], (owners,) + hidden.shape)
    everyone = lax.all_to_all(copies, "store", 0, 0, tiled=True).reshape(owners * rows, width)
    slot = adapter_ids - lax.axis_index("store") * count
    owned = slot[:, None] == jnp.arange(count, dtype=jnp.int32)[None, :]
    low = jnp.einsum(
        "rd,kd->rk",
        everyone,
        adapter_down.reshape(count * rank, width),
        preferred_element_type=jnp.float32,
    ).reshape(owners * rows, count, rank)
    low = (low * owned[:, :, None].astype(jnp.float32)).astype(jnp.bfloat16)
    parts = jnp.dot(
        low.reshape(owners * rows, count * rank),
        adapter_up.reshape(count * rank, -1),
        preferred_element_type=jnp.float32,
    )
    came = lax.all_to_all(parts.reshape((owners,) + block), "store", 0, 0, tiled=True)
    return [jnp.sum(came, axis=0)]


def per_device(
    hidden, query_base, adapter_down, adapter_up, adapter_ids, key_cache, value_cache, kv_lengths
):
    features = adapter_up.shape[2]
    rows, kv_heads, slots, head_size = key_cache.shape
    block = (rows, features // head_size, head_size)
    shared = (lax.axis_size("store"), lax.axis_size("tensor")) == (8, len(TURNS))
    deltas = (shared_deltas if shared else exchanged_deltas)(
        hidden, adapter_down, adapter_up, adapter_ids, block
    )
    live = jnp.arange(slots, dtype=jnp.int32)[None, None, :] < kv_lengths[:, None, None]
    return pl.pallas_call(
        functools.partial(attend_kernel, len(deltas)),
        out_shape=jax.ShapeDtypeStruct((rows, features), jnp.bfloat16),
        in_specs=[VMEM] * (len(deltas) + 4),
        out_specs=VMEM,
        scratch_shapes=[pltpu.VMEM(block, jnp.float32)],
        compiler_params=PARAMS,
        name="attend",
    )(
        near(live.astype(jnp.float32)),
        near(query_base.reshape(block)),
        *deltas,
        near(key_cache),
        near(value_cache),
    )


def solution(mesh):
    in_specs = (
        P(("groups", "store"), None),
        P(("groups", "store"), "tensor"),
        P(("groups", "store"), None, None),
        P(("groups", "store"), None, "tensor"),
        P("groups"),
        P(("groups", "store"), "tensor", None, None),
        P(("groups", "store"), "tensor", None, None),
        P(("groups", "store")),
    )
    out_specs = P(("groups", "store"), "tensor")
    return jax.shard_map(
        per_device, mesh=mesh, in_specs=in_specs, out_specs=out_specs, check_vma=False
    )
```

```python
import functools

import jax
import jax.numpy as jnp
from jax import lax
from jax.experimental import pallas as pl
from jax.experimental.pallas import tpu as pltpu
from jax.sharding import PartitionSpec as P

HEADS = 64
KVH = 8
LANES = 128
CHUNK = 1024
VMEM_LIMIT = 32 * 1024 * 1024
VMEM = pl.BlockSpec(memory_space=pltpu.VMEM)
SMEM = pl.BlockSpec(memory_space=pltpu.SMEM)
PARAMS = pltpu.CompilerParams(vmem_limit_bytes=VMEM_LIMIT)
TURNS = ((7, 1, 4, 2, 0), (6, 3, 5, 2, 0))
SENT = len(TURNS[0]) - 1
FAR = 2
SHARED = [turn for turn in range(SENT + 1) if TURNS[0][turn] == TURNS[1][turn]][0]


def fetch_kernel(*refs):
    *pairs, arrived = refs
    half = len(pairs) // 2
    copies = [
        pltpu.make_async_copy(source, target, arrived.at[i])
        for i, (source, target) in enumerate(zip(pairs[:half], pairs[half:]))
    ]
    for copy in copies:
        copy.start()
    for copy in copies:
        copy.wait()


def fetch(name, *arrays):
    size = sum(array.size * array.dtype.itemsize for array in arrays)
    return pl.pallas_call(
        fetch_kernel,
        out_shape=[pltpu.VMEM(array.shape, array.dtype) for array in arrays],
        in_specs=[pl.BlockSpec(memory_space=pl.ANY)] * len(arrays),
        out_specs=[VMEM] * len(arrays),
        scratch_shapes=[pltpu.SemaphoreType.DMA((len(arrays),))],
        compiler_params=PARAMS,
        cost_estimate=pl.CostEstimate(flops=0, transcendentals=0, bytes_accessed=2 * size),
        name=name,
    )(*[pltpu.with_memory_space_constraint(array, pltpu.HBM) for array in arrays])


def near(array):
    return pltpu.with_memory_space_constraint(array, pltpu.VMEM)


def owner_kernel(turns, ids_ref, down_ref, mine_ref, other_ref, *refs):
    amount = len(turns)
    hidden_refs, (delta_refs, scratch) = refs[:amount], (refs[-3 - amount : -3], refs[-3:])
    state_ref, sum_ref, row_ref = scratch
    count, rank, width = down_ref.shape
    rows = state_ref.shape[1]
    heads = row_ref.shape[0]
    me, core = lax.axis_index("store"), lax.axis_index("tensor")

    def slot_of(partners, row, shared):
        source = me ^ jnp.where(core == 0, partners[0], partners[1])
        slot = ids_ref[source * rows + row] - me * count
        mine = jnp.logical_not(shared) | (core == lax.rem(row, len(TURNS)))
        return slot, mine & (slot >= 0) & (slot < count)

    owned = {}
    for i, turn in enumerate(turns):
        for row in range(rows):
            owned[i, row] = slot_of([steps[turn] for steps in TURNS], row, turn >= SHARED)[1]

            @pl.when(owned[i, row])
            def _():
                state_ref[i, row : row + 1] = hidden_refs[i][row : row + 1, :].astype(jnp.float32)

        delta_refs[i][...] = jnp.zeros(delta_refs[i].shape, delta_refs[i].dtype)

    packed = [sum(steps[turn] << (4 * i) for i, turn in enumerate(turns)) for steps in TURNS]
    late = sum((turn >= SHARED) << i for i, turn in enumerate(turns))

    def one_request(index, carry):
        i, row = lax.div(index, rows), lax.rem(index, rows)
        partners = [(jnp.int32(value) >> (4 * i)) & 15 for value in packed]
        slot, here = slot_of(partners, row, ((jnp.int32(late) >> i) & 1) == 1)

        @pl.when(here)
        def _():
            total = jnp.zeros((rank, CHUNK), jnp.float32)
            for start in range(0, width, CHUNK):
                down = down_ref[slot, :, start : start + CHUNK].astype(jnp.float32)
                total = total + down * state_ref[i, pl.ds(row, 1), start : start + CHUNK]
            low = jnp.sum(total, axis=1, keepdims=True)
            low = low.astype(jnp.bfloat16).astype(jnp.float32)
            for half, up_ref in ((core, mine_ref), (1 - core, other_ref)):
                for head in range(heads):
                    up = up_ref[slot, :, head * LANES : (head + 1) * LANES]
                    row_ref[head : head + 1, :] = jnp.sum(
                        up.astype(jnp.float32) * low, axis=0, keepdims=True
                    )
                sum_ref[i, row, half] = row_ref[...].astype(sum_ref.dtype)

        return carry

    lax.fori_loop(0, amount * rows, one_request, 0)
    for (i, row), here in owned.items():

        @pl.when(here)
        def _():
            delta_refs[i][row] = sum_ref[i, row]


def merge_kernel(own_ref, *refs):
    came_refs, (kept_ref, sent_ref) = refs[:-2], refs[-2:]
    core = lax.axis_index("tensor")
    for half, out_ref in ((core, kept_ref), (1 - core, sent_ref)):
        total = own_ref[:, half].astype(jnp.float32)
        for came_ref in came_refs:
            total = total + came_ref[:, half].astype(jnp.float32)
        out_ref[...] = total.astype(out_ref.dtype)


def attend_kernel(parts, live_ref, base_ref, *refs):
    delta_refs, (key_ref, value_ref, out_ref, rows_ref) = refs[:parts], refs[parts:]
    rows, kv_heads, slots, head_size = key_ref.shape
    heads = base_ref.shape[1]
    group = heads // kv_heads
    scale = 1.0 / (float(head_size) ** 0.5)
    scores = []
    for row in range(rows):
        query = base_ref[row].astype(jnp.float32)
        delta = delta_refs[0][row].astype(jnp.float32)
        for ref in delta_refs[1:]:
            delta = delta + ref[row].astype(jnp.float32)
        query = query + delta
        live = live_ref[row] > 0
        for kv in range(kv_heads):
            mine = query[kv * group : (kv + 1) * group].astype(jnp.bfloat16)
            score = lax.dot_general(
                mine,
                key_ref[row, kv],
                (((1,), (1,)), ((), ())),
                preferred_element_type=jnp.float32,
            )
            scores.append(jnp.where(live, score * scale, jnp.float32(-1e30)))
    scores = jnp.concatenate(scores, axis=0)
    grown = jnp.exp(scores - jnp.max(scores, axis=1, keepdims=True))
    weights = grown / jnp.sum(grown, axis=1, keepdims=True)
    for row in range(rows):
        for kv in range(kv_heads):
            at = (row * kv_heads + kv) * group
            rows_ref[row, kv * group : (kv + 1) * group, :] = jnp.dot(
                weights[at : at + group].astype(jnp.bfloat16),
                value_ref[row, kv],
                preferred_element_type=jnp.float32,
            )
    for head in range(heads):
        out_ref[:, head * LANES : (head + 1) * LANES] = rows_ref[:, head, :].astype(out_ref.dtype)


def shared_deltas(hidden, adapter_down, adapter_up, adapter_ids, block):
    rows, heads, head_size = block
    owners, cores = lax.axis_size("store"), len(TURNS)

    def turn_pairs(turn):
        return [
            (i * cores + core, (i ^ TURNS[core][turn]) * cores + core)
            for i in range(owners)
            for core in range(cores)
        ]

    def visit(array, turn):
        return lax.ppermute(array, ("store", "tensor"), turn_pairs(turn))

    def swap(array):
        return lax.ppermute(array, "tensor", [(0, 1), (1, 0)])

    states = [visit(hidden, turn) for turn in range(SENT)]
    other = swap(adapter_up)
    ids, own, down, up = fetch("fetch", adapter_ids, hidden, adapter_down, adapter_up)
    other = near(other)
    wide = (rows, cores, heads, head_size)

    def work(name, after, *turns):
        amount = len(turns)
        return pl.pallas_call(
            functools.partial(owner_kernel, turns),
            out_shape=[jax.ShapeDtypeStruct(wide, jnp.bfloat16)] * amount,
            in_specs=[SMEM] + [VMEM] * (amount + 3) + [pl.BlockSpec(memory_space=pl.ANY)] * len(after),
            out_specs=[VMEM] * amount,
            scratch_shapes=[
                pltpu.VMEM((amount,) + hidden.shape, jnp.float32),
                pltpu.VMEM((amount,) + wide, jnp.bfloat16),
                pltpu.VMEM((heads, head_size), jnp.float32),
            ],
            compiler_params=PARAMS,
            name=name,
        )(ids, down, up, other, *[states[turn] for turn in turns], *after)

    states.append(own)
    deltas = work("owner_far", (), *range(FAR))
    deltas += work("owner_near", deltas[:1], *range(FAR, SENT + 1))
    came = [visit(delta, turn) for turn, delta in enumerate(deltas[:SENT])]
    kept, sent = pl.pallas_call(
        merge_kernel,
        out_shape=[jax.ShapeDtypeStruct(block, jnp.bfloat16)] * 2,
        in_specs=[VMEM] * (SENT + 1),
        out_specs=[VMEM] * 2,
        compiler_params=PARAMS,
        name="merge",
    )(deltas[-1], *came)
    return [kept, swap(sent)]


def exchanged_deltas(hidden, adapter_down, adapter_up, adapter_ids, block):
    count, rank, width = adapter_down.shape
    owners, rows = lax.axis_size("store"), hidden.shape[0]
    copies = jnp.broadcast_to(hidden[None], (owners,) + hidden.shape)
    everyone = lax.all_to_all(copies, "store", 0, 0, tiled=True).reshape(owners * rows, width)
    slot = adapter_ids - lax.axis_index("store") * count
    owned = slot[:, None] == jnp.arange(count, dtype=jnp.int32)[None, :]
    low = jnp.einsum(
        "rd,kd->rk",
        everyone,
        adapter_down.reshape(count * rank, width),
        preferred_element_type=jnp.float32,
    ).reshape(owners * rows, count, rank)
    low = (low * owned[:, :, None].astype(jnp.float32)).astype(jnp.bfloat16)
    parts = jnp.dot(
        low.reshape(owners * rows, count * rank),
        adapter_up.reshape(count * rank, -1),
        preferred_element_type=jnp.float32,
    )
    came = lax.all_to_all(parts.reshape((owners,) + block), "store", 0, 0, tiled=True)
    return [jnp.sum(came, axis=0)]


def per_device(
    hidden, query_base, adapter_down, adapter_up, adapter_ids, key_cache, value_cache, kv_lengths
):
    features = adapter_up.shape[2]
    rows, kv_heads, slots, head_size = key_cache.shape
    block = (rows, features // head_size, head_size)
    shared = (lax.axis_size("store"), lax.axis_size("tensor")) == (8, len(TURNS))
    deltas = (shared_deltas if shared else exchanged_deltas)(
        hidden, adapter_down, adapter_up, adapter_ids, block
    )
    live = jnp.arange(slots, dtype=jnp.int32)[None, None, :] < kv_lengths[:, None, None]
    return pl.pallas_call(
        functools.partial(attend_kernel, len(deltas)),
        out_shape=jax.ShapeDtypeStruct((rows, features), jnp.bfloat16),
        in_specs=[VMEM] * (len(deltas) + 4),
        out_specs=VMEM,
        scratch_shapes=[pltpu.VMEM(block, jnp.float32)],
        compiler_params=PARAMS,
        name="attend",
    )(
        near(live.astype(jnp.float32)),
        near(query_base.reshape(block)),
        *deltas,
        near(key_cache),
        near(value_cache),
    )


def solution(mesh):
    in_specs = (
        P(("groups", "store"), None),
        P(("groups", "store"), "tensor"),
        P(("groups", "store"), None, None),
        P(("groups", "store"), None, "tensor"),
        P("groups"),
        P(("groups", "store"), "tensor", None, None),
        P(("groups", "store"), "tensor", None, None),
        P(("groups", "store")),
    )
    out_specs = P(("groups", "store"), "tensor")
    return jax.shard_map(
        per_device, mesh=mesh, in_specs=in_specs, out_specs=out_specs, check_vma=False
    )
```

```python
import functools

import jax
import jax.numpy as jnp
from jax import lax
from jax.experimental import pallas as pl
from jax.experimental.pallas import tpu as pltpu
from jax.sharding import PartitionSpec as P

HEADS = 64
KVH = 8
LANES = 128
CHUNK = 1024
VMEM_LIMIT = 32 * 1024 * 1024
VMEM = pl.BlockSpec(memory_space=pltpu.VMEM)
SMEM = pl.BlockSpec(memory_space=pltpu.SMEM)
PARAMS = pltpu.CompilerParams(vmem_limit_bytes=VMEM_LIMIT)
TURNS = ((7, 1, 4, 2, 0), (6, 3, 5, 2, 0))
SENT = len(TURNS[0]) - 1
FAR = 2
SHARED = [turn for turn in range(SENT + 1) if TURNS[0][turn] == TURNS[1][turn]][0]


def fetch_kernel(
    ids_hbm, own_hbm, down_hbm, up_hbm, ids_ref, own_ref, down_ref, up_ref, used_ref, arrived
):
    count = down_ref.shape[0]
    first = lax.axis_index("store") * count
    own = pltpu.make_async_copy(own_hbm, own_ref, arrived.at[2 * count])
    own.start()
    ids = pltpu.make_async_copy(ids_hbm, ids_ref, arrived.at[2 * count + 1])
    ids.start()

    def adapter(slot):
        return (
            pltpu.make_async_copy(down_hbm.at[slot], down_ref.at[slot], arrived.at[slot]),
            pltpu.make_async_copy(up_hbm.at[slot], up_ref.at[slot], arrived.at[count + slot]),
        )

    for slot in range(count):
        used_ref[slot] = 0
    ids.wait()
    for request in range(ids_ref.shape[0]):
        slot = ids_ref[request] - first

        @pl.when((slot >= 0) & (slot < count))
        def _():
            used_ref[slot] = 1

    for slot in range(count):

        @pl.when(used_ref[slot] == 1)
        def _():
            for copy in adapter(slot):
                copy.start()

    for slot in range(count):

        @pl.when(used_ref[slot] == 1)
        def _():
            for copy in adapter(slot):
                copy.wait()

    own.wait()


def fetch(ids, own, down, up):
    arrays = (ids, own, down, up)
    size = sum(array.size * array.dtype.itemsize for array in arrays)
    return pl.pallas_call(
        fetch_kernel,
        out_shape=[pltpu.SMEM(ids.shape, ids.dtype)]
        + [pltpu.VMEM(array.shape, array.dtype) for array in arrays[1:]],
        in_specs=[pl.BlockSpec(memory_space=pl.ANY)] * len(arrays),
        out_specs=[SMEM, VMEM, VMEM, VMEM],
        scratch_shapes=[
            pltpu.SMEM((down.shape[0],), jnp.int32),
            pltpu.SemaphoreType.DMA((2 * down.shape[0] + 2,)),
        ],
        compiler_params=PARAMS,
        cost_estimate=pl.CostEstimate(flops=0, transcendentals=0, bytes_accessed=2 * size),
        name="fetch",
    )(*[pltpu.with_memory_space_constraint(array, pltpu.HBM) for array in arrays])


def near(array):
    return pltpu.with_memory_space_constraint(array, pltpu.VMEM)


def owner_kernel(turns, ids_ref, down_ref, mine_ref, other_ref, *refs):
    amount = len(turns)
    hidden_refs, (delta_refs, scratch) = refs[:amount], (refs[-3 - amount : -3], refs[-3:])
    state_ref, sum_ref, row_ref = scratch
    count, rank, width = down_ref.shape
    rows = state_ref.shape[1]
    heads = row_ref.shape[0]
    me, core = lax.axis_index("store"), lax.axis_index("tensor")

    def slot_of(partners, row, shared):
        source = me ^ jnp.where(core == 0, partners[0], partners[1])
        slot = ids_ref[source * rows + row] - me * count
        mine = jnp.logical_not(shared) | (core == lax.rem(row, len(TURNS)))
        return slot, mine & (slot >= 0) & (slot < count)

    owned = {}
    for i, turn in enumerate(turns):
        for row in range(rows):
            owned[i, row] = slot_of([steps[turn] for steps in TURNS], row, turn >= SHARED)[1]

            @pl.when(owned[i, row])
            def _():
                state_ref[i, row : row + 1] = hidden_refs[i][row : row + 1, :].astype(jnp.float32)

        delta_refs[i][...] = jnp.zeros(delta_refs[i].shape, delta_refs[i].dtype)

    packed = [sum(steps[turn] << (4 * i) for i, turn in enumerate(turns)) for steps in TURNS]
    late = sum((turn >= SHARED) << i for i, turn in enumerate(turns))

    def one_request(index, carry):
        i, row = lax.div(index, rows), lax.rem(index, rows)
        partners = [(jnp.int32(value) >> (4 * i)) & 15 for value in packed]
        slot, here = slot_of(partners, row, ((jnp.int32(late) >> i) & 1) == 1)

        @pl.when(here)
        def _():
            total = jnp.zeros((rank, CHUNK), jnp.float32)
            for start in range(0, width, CHUNK):
                down = down_ref[slot, :, start : start + CHUNK].astype(jnp.float32)
                total = total + down * state_ref[i, pl.ds(row, 1), start : start + CHUNK]
            low = jnp.sum(total, axis=1, keepdims=True)
            low = low.astype(jnp.bfloat16).astype(jnp.float32)
            for half, up_ref in ((core, mine_ref), (1 - core, other_ref)):
                for head in range(heads):
                    up = up_ref[slot, :, head * LANES : (head + 1) * LANES]
                    row_ref[head : head + 1, :] = jnp.sum(
                        up.astype(jnp.float32) * low, axis=0, keepdims=True
                    )
                sum_ref[i, row, half] = row_ref[...].astype(sum_ref.dtype)

        return carry

    lax.fori_loop(0, amount * rows, one_request, 0)
    for (i, row), here in owned.items():

        @pl.when(here)
        def _():
            delta_refs[i][row] = sum_ref[i, row]


def merge_kernel(own_ref, *refs):
    came_refs, (kept_ref, sent_ref) = refs[:-2], refs[-2:]
    core = lax.axis_index("tensor")
    for half, out_ref in ((core, kept_ref), (1 - core, sent_ref)):
        total = own_ref[:, half].astype(jnp.float32)
        for came_ref in came_refs:
            total = total + came_ref[:, half].astype(jnp.float32)
        out_ref[...] = total.astype(out_ref.dtype)


def attend_kernel(parts, live_ref, base_ref, *refs):
    delta_refs, (key_ref, value_ref, out_ref, rows_ref) = refs[:parts], refs[parts:]
    rows, kv_heads, slots, head_size = key_ref.shape
    heads = base_ref.shape[1]
    group = heads // kv_heads
    scale = 1.0 / (float(head_size) ** 0.5)
    scores = []
    for row in range(rows):
        query = base_ref[row].astype(jnp.float32)
        delta = delta_refs[0][row].astype(jnp.float32)
        for ref in delta_refs[1:]:
            delta = delta + ref[row].astype(jnp.float32)
        query = query + delta
        live = live_ref[row] > 0
        for kv in range(kv_heads):
            mine = query[kv * group : (kv + 1) * group].astype(jnp.bfloat16)
            score = lax.dot_general(
                mine,
                key_ref[row, kv],
                (((1,), (1,)), ((), ())),
                preferred_element_type=jnp.float32,
            )
            scores.append(jnp.where(live, score * scale, jnp.float32(-1e30)))
    scores = jnp.concatenate(scores, axis=0)
    grown = jnp.exp(scores - jnp.max(scores, axis=1, keepdims=True))
    weights = grown / jnp.sum(grown, axis=1, keepdims=True)
    for row in range(rows):
        for kv in range(kv_heads):
            at = (row * kv_heads + kv) * group
            rows_ref[row, kv * group : (kv + 1) * group, :] = jnp.dot(
                weights[at : at + group].astype(jnp.bfloat16),
                value_ref[row, kv],
                preferred_element_type=jnp.float32,
            )
    for head in range(heads):
        out_ref[:, head * LANES : (head + 1) * LANES] = rows_ref[:, head, :].astype(out_ref.dtype)


def shared_deltas(hidden, adapter_down, adapter_up, adapter_ids, block):
    rows, heads, head_size = block
    owners, cores = lax.axis_size("store"), len(TURNS)

    def turn_pairs(turn):
        return [
            (i * cores + core, (i ^ TURNS[core][turn]) * cores + core)
            for i in range(owners)
            for core in range(cores)
        ]

    def visit(array, turn):
        return lax.ppermute(array, ("store", "tensor"), turn_pairs(turn))

    def swap(array):
        return lax.ppermute(array, "tensor", [(0, 1), (1, 0)])

    states = [visit(hidden, turn) for turn in range(SENT)]
    other = swap(adapter_up)
    ids, own, down, up = fetch(adapter_ids, hidden, adapter_down, adapter_up)
    other = near(other)
    wide = (rows, cores, heads, head_size)

    def work(name, after, *turns):
        amount = len(turns)
        return pl.pallas_call(
            functools.partial(owner_kernel, turns),
            out_shape=[jax.ShapeDtypeStruct(wide, jnp.bfloat16)] * amount,
            in_specs=[SMEM] + [VMEM] * (amount + 3) + [pl.BlockSpec(memory_space=pl.ANY)] * len(after),
            out_specs=[VMEM] * amount,
            scratch_shapes=[
                pltpu.VMEM((amount,) + hidden.shape, jnp.float32),
                pltpu.VMEM((amount,) + wide, jnp.bfloat16),
                pltpu.VMEM((heads, head_size), jnp.float32),
            ],
            compiler_params=PARAMS,
            name=name,
        )(ids, down, up, other, *[states[turn] for turn in turns], *after)

    states.append(own)
    deltas = work("owner_far", (), *range(FAR))
    deltas += work("owner_near", deltas[:1], *range(FAR, SENT + 1))
    came = [visit(delta, turn) for turn, delta in enumerate(deltas[:SENT])]
    kept, sent = pl.pallas_call(
        merge_kernel,
        out_shape=[jax.ShapeDtypeStruct(block, jnp.bfloat16)] * 2,
        in_specs=[VMEM] * (SENT + 1),
        out_specs=[VMEM] * 2,
        compiler_params=PARAMS,
        name="merge",
    )(deltas[-1], *came)
    return [kept, swap(sent)]


def exchanged_deltas(hidden, adapter_down, adapter_up, adapter_ids, block):
    count, rank, width = adapter_down.shape
    owners, rows = lax.axis_size("store"), hidden.shape[0]
    copies = jnp.broadcast_to(hidden[None], (owners,) + hidden.shape)
    everyone = lax.all_to_all(copies, "store", 0, 0, tiled=True).reshape(owners * rows, width)
    slot = adapter_ids - lax.axis_index("store") * count
    owned = slot[:, None] == jnp.arange(count, dtype=jnp.int32)[None, :]
    low = jnp.einsum(
        "rd,kd->rk",
        everyone,
        adapter_down.reshape(count * rank, width),
        preferred_element_type=jnp.float32,
    ).reshape(owners * rows, count, rank)
    low = (low * owned[:, :, None].astype(jnp.float32)).astype(jnp.bfloat16)
    parts = jnp.dot(
        low.reshape(owners * rows, count * rank),
        adapter_up.reshape(count * rank, -1),
        preferred_element_type=jnp.float32,
    )
    came = lax.all_to_all(parts.reshape((owners,) + block), "store", 0, 0, tiled=True)
    return [jnp.sum(came, axis=0)]


def per_device(
    hidden, query_base, adapter_down, adapter_up, adapter_ids, key_cache, value_cache, kv_lengths
):
    features = adapter_up.shape[2]
    rows, kv_heads, slots, head_size = key_cache.shape
    block = (rows, features // head_size, head_size)
    shared = (lax.axis_size("store"), lax.axis_size("tensor")) == (8, len(TURNS))
    deltas = (shared_deltas if shared else exchanged_deltas)(
        hidden, adapter_down, adapter_up, adapter_ids, block
    )
    live = jnp.arange(slots, dtype=jnp.int32)[None, None, :] < kv_lengths[:, None, None]
    return pl.pallas_call(
        functools.partial(attend_kernel, len(deltas)),
        out_shape=jax.ShapeDtypeStruct((rows, features), jnp.bfloat16),
        in_specs=[VMEM] * (len(deltas) + 4),
        out_specs=VMEM,
        scratch_shapes=[pltpu.VMEM(block, jnp.float32)],
        compiler_params=PARAMS,
        name="attend",
    )(
        near(live.astype(jnp.float32)),
        near(query_base.reshape(block)),
        *deltas,
        near(key_cache),
        near(value_cache),
    )


def solution(mesh):
    in_specs = (
        P(("groups", "store"), None),
        P(("groups", "store"), "tensor"),
        P(("groups", "store"), None, None),
        P(("groups", "store"), None, "tensor"),
        P("groups"),
        P(("groups", "store"), "tensor", None, None),
        P(("groups", "store"), "tensor", None, None),
        P(("groups", "store")),
    )
    out_specs = P(("groups", "store"), "tensor")
    return jax.shard_map(
        per_device, mesh=mesh, in_specs=in_specs, out_specs=out_specs, check_vma=False
    )
```

```python
import functools

import jax
import jax.numpy as jnp
from jax import lax
from jax.experimental import pallas as pl
from jax.experimental.pallas import tpu as pltpu
from jax.sharding import PartitionSpec as P

HEADS = 64
KVH = 8
LANES = 128
CHUNK = 1024
VMEM_LIMIT = 32 * 1024 * 1024
VMEM = pl.BlockSpec(memory_space=pltpu.VMEM)
SMEM = pl.BlockSpec(memory_space=pltpu.SMEM)
PARAMS = pltpu.CompilerParams(vmem_limit_bytes=VMEM_LIMIT)
TURNS = ((7, 1, 4, 2, 0), (6, 3, 5, 2, 0))
SENT = len(TURNS[0]) - 1
FAR = 2
SHARED = [turn for turn in range(SENT + 1) if TURNS[0][turn] == TURNS[1][turn]][0]


def scalars_kernel(ids_hbm, *refs):
    ids_ref, arrived = refs[-2:]
    copy = pltpu.make_async_copy(ids_hbm, ids_ref, arrived)
    copy.start()
    copy.wait()


def scalars(ids, *beside):
    size = sum(array.size * array.dtype.itemsize for array in beside)
    return pl.pallas_call(
        scalars_kernel,
        out_shape=pltpu.SMEM(ids.shape, ids.dtype),
        in_specs=[pl.BlockSpec(memory_space=pl.ANY)] * (1 + len(beside)),
        out_specs=SMEM,
        scratch_shapes=[pltpu.SemaphoreType.DMA(())],
        compiler_params=PARAMS,
        cost_estimate=pl.CostEstimate(flops=0, transcendentals=0, bytes_accessed=size),
        name="scalars",
    )(*[pltpu.with_memory_space_constraint(array, pltpu.HBM) for array in (ids,) + beside])


def near(array):
    return pltpu.with_memory_space_constraint(array, pltpu.VMEM)


def owner_kernel(turns, ids_ref, down_ref, mine_ref, other_ref, *refs):
    amount = len(turns)
    hidden_refs, (delta_refs, scratch) = refs[:amount], (refs[-3 - amount : -3], refs[-3:])
    state_ref, sum_ref, row_ref = scratch
    count, rank, width = down_ref.shape
    rows = state_ref.shape[1]
    heads = row_ref.shape[0]
    me, core = lax.axis_index("store"), lax.axis_index("tensor")

    def slot_of(partners, row, shared):
        source = me ^ jnp.where(core == 0, partners[0], partners[1])
        slot = ids_ref[source * rows + row] - me * count
        mine = jnp.logical_not(shared) | (core == lax.rem(row, len(TURNS)))
        return slot, mine & (slot >= 0) & (slot < count)

    owned = {}
    for i, turn in enumerate(turns):
        for row in range(rows):
            owned[i, row] = slot_of([steps[turn] for steps in TURNS], row, turn >= SHARED)[1]

            @pl.when(owned[i, row])
            def _():
                state_ref[i, row : row + 1] = hidden_refs[i][row : row + 1, :].astype(jnp.float32)

        delta_refs[i][...] = jnp.zeros(delta_refs[i].shape, delta_refs[i].dtype)

    packed = [sum(steps[turn] << (4 * i) for i, turn in enumerate(turns)) for steps in TURNS]
    late = sum((turn >= SHARED) << i for i, turn in enumerate(turns))

    def one_request(index, carry):
        i, row = lax.div(index, rows), lax.rem(index, rows)
        partners = [(jnp.int32(value) >> (4 * i)) & 15 for value in packed]
        slot, here = slot_of(partners, row, ((jnp.int32(late) >> i) & 1) == 1)

        @pl.when(here)
        def _():
            total = jnp.zeros((rank, CHUNK), jnp.float32)
            for start in range(0, width, CHUNK):
                down = down_ref[slot, :, start : start + CHUNK].astype(jnp.float32)
                total = total + down * state_ref[i, pl.ds(row, 1), start : start + CHUNK]
            low = jnp.sum(total, axis=1, keepdims=True)
            low = low.astype(jnp.bfloat16).astype(jnp.float32)
            for half, up_ref in ((core, mine_ref), (1 - core, other_ref)):
                for head in range(heads):
                    up = up_ref[slot, :, head * LANES : (head + 1) * LANES]
                    row_ref[head : head + 1, :] = jnp.sum(
                        up.astype(jnp.float32) * low, axis=0, keepdims=True
                    )
                sum_ref[i, row, half] = row_ref[...].astype(sum_ref.dtype)

        return carry

    lax.fori_loop(0, amount * rows, one_request, 0)
    for (i, row), here in owned.items():

        @pl.when(here)
        def _():
            delta_refs[i][row] = sum_ref[i, row]


def merge_kernel(own_ref, *refs):
    came_refs, (kept_ref, sent_ref) = refs[:-2], refs[-2:]
    core = lax.axis_index("tensor")
    for half, out_ref in ((core, kept_ref), (1 - core, sent_ref)):
        total = own_ref[:, half].astype(jnp.float32)
        for came_ref in came_refs:
            total = total + came_ref[:, half].astype(jnp.float32)
        out_ref[...] = total.astype(out_ref.dtype)


def attend_kernel(parts, live_ref, base_ref, *refs):
    delta_refs, (key_ref, value_ref, out_ref, rows_ref) = refs[:parts], refs[parts:]
    rows, kv_heads, slots, head_size = key_ref.shape
    heads = base_ref.shape[1]
    group = heads // kv_heads
    scale = 1.0 / (float(head_size) ** 0.5)
    scores = []
    for row in range(rows):
        query = base_ref[row].astype(jnp.float32)
        delta = delta_refs[0][row].astype(jnp.float32)
        for ref in delta_refs[1:]:
            delta = delta + ref[row].astype(jnp.float32)
        query = query + delta
        live = live_ref[row] > 0
        for kv in range(kv_heads):
            mine = query[kv * group : (kv + 1) * group].astype(jnp.bfloat16)
            score = lax.dot_general(
                mine,
                key_ref[row, kv],
                (((1,), (1,)), ((), ())),
                preferred_element_type=jnp.float32,
            )
            scores.append(jnp.where(live, score * scale, jnp.float32(-1e30)))
    scores = jnp.concatenate(scores, axis=0)
    grown = jnp.exp(scores - jnp.max(scores, axis=1, keepdims=True))
    weights = grown / jnp.sum(grown, axis=1, keepdims=True)
    for row in range(rows):
        for kv in range(kv_heads):
            at = (row * kv_heads + kv) * group
            rows_ref[row, kv * group : (kv + 1) * group, :] = jnp.dot(
                weights[at : at + group].astype(jnp.bfloat16),
                value_ref[row, kv],
                preferred_element_type=jnp.float32,
            )
    for head in range(heads):
        out_ref[:, head * LANES : (head + 1) * LANES] = rows_ref[:, head, :].astype(out_ref.dtype)


def shared_deltas(hidden, adapter_down, adapter_up, adapter_ids, block):
    rows, heads, head_size = block
    owners, cores = lax.axis_size("store"), len(TURNS)

    def turn_pairs(turn):
        return [
            (i * cores + core, (i ^ TURNS[core][turn]) * cores + core)
            for i in range(owners)
            for core in range(cores)
        ]

    def visit(array, turn):
        return lax.ppermute(array, ("store", "tensor"), turn_pairs(turn))

    def swap(array):
        return lax.ppermute(array, "tensor", [(0, 1), (1, 0)])

    states = [visit(hidden, turn) for turn in range(SENT)]
    other = swap(adapter_up)
    ids = scalars(adapter_ids, adapter_down, adapter_up)
    down, up, other = near(adapter_down), near(adapter_up), near(other)
    wide = (rows, cores, heads, head_size)

    def work(name, after, *turns):
        amount = len(turns)
        return pl.pallas_call(
            functools.partial(owner_kernel, turns),
            out_shape=[jax.ShapeDtypeStruct(wide, jnp.bfloat16)] * amount,
            in_specs=[SMEM] + [VMEM] * (amount + 3) + [pl.BlockSpec(memory_space=pl.ANY)] * len(after),
            out_specs=[VMEM] * amount,
            scratch_shapes=[
                pltpu.VMEM((amount,) + hidden.shape, jnp.float32),
                pltpu.VMEM((amount,) + wide, jnp.bfloat16),
                pltpu.VMEM((heads, head_size), jnp.float32),
            ],
            compiler_params=PARAMS,
            name=name,
        )(ids, down, up, other, *[states[turn] for turn in turns], *after)

    states.append(near(hidden))
    deltas = work("owner_far", (), *range(FAR))
    deltas += work("owner_near", deltas[:1], *range(FAR, SENT + 1))
    came = [visit(delta, turn) for turn, delta in enumerate(deltas[:SENT])]
    kept, sent = pl.pallas_call(
        merge_kernel,
        out_shape=[jax.ShapeDtypeStruct(block, jnp.bfloat16)] * 2,
        in_specs=[VMEM] * (SENT + 1),
        out_specs=[VMEM] * 2,
        compiler_params=PARAMS,
        name="merge",
    )(deltas[-1], *came)
    return [kept, swap(sent)]


def exchanged_deltas(hidden, adapter_down, adapter_up, adapter_ids, block):
    count, rank, width = adapter_down.shape
    owners, rows = lax.axis_size("store"), hidden.shape[0]
    copies = jnp.broadcast_to(hidden[None], (owners,) + hidden.shape)
    everyone = lax.all_to_all(copies, "store", 0, 0, tiled=True).reshape(owners * rows, width)
    slot = adapter_ids - lax.axis_index("store") * count
    owned = slot[:, None] == jnp.arange(count, dtype=jnp.int32)[None, :]
    low = jnp.einsum(
        "rd,kd->rk",
        everyone,
        adapter_down.reshape(count * rank, width),
        preferred_element_type=jnp.float32,
    ).reshape(owners * rows, count, rank)
    low = (low * owned[:, :, None].astype(jnp.float32)).astype(jnp.bfloat16)
    parts = jnp.dot(
        low.reshape(owners * rows, count * rank),
        adapter_up.reshape(count * rank, -1),
        preferred_element_type=jnp.float32,
    )
    came = lax.all_to_all(parts.reshape((owners,) + block), "store", 0, 0, tiled=True)
    return [jnp.sum(came, axis=0)]


def per_device(
    hidden, query_base, adapter_down, adapter_up, adapter_ids, key_cache, value_cache, kv_lengths
):
    features = adapter_up.shape[2]
    rows, kv_heads, slots, head_size = key_cache.shape
    block = (rows, features // head_size, head_size)
    shared = (lax.axis_size("store"), lax.axis_size("tensor")) == (8, len(TURNS))
    deltas = (shared_deltas if shared else exchanged_deltas)(
        hidden, adapter_down, adapter_up, adapter_ids, block
    )
    live = jnp.arange(slots, dtype=jnp.int32)[None, None, :] < kv_lengths[:, None, None]
    return pl.pallas_call(
        functools.partial(attend_kernel, len(deltas)),
        out_shape=jax.ShapeDtypeStruct((rows, features), jnp.bfloat16),
        in_specs=[VMEM] * (len(deltas) + 4),
        out_specs=VMEM,
        scratch_shapes=[pltpu.VMEM(block, jnp.float32)],
        compiler_params=PARAMS,
        name="attend",
    )(
        near(live.astype(jnp.float32)),
        near(query_base.reshape(block)),
        *deltas,
        near(key_cache),
        near(value_cache),
    )


def solution(mesh):
    in_specs = (
        P(("groups", "store"), None),
        P(("groups", "store"), "tensor"),
        P(("groups", "store"), None, None),
        P(("groups", "store"), None, "tensor"),
        P("groups"),
        P(("groups", "store"), "tensor", None, None),
        P(("groups", "store"), "tensor", None, None),
        P(("groups", "store")),
    )
    out_specs = P(("groups", "store"), "tensor")
    return jax.shard_map(
        per_device, mesh=mesh, in_specs=in_specs, out_specs=out_specs, check_vma=False
    )
```

```python
import functools

import jax
import jax.numpy as jnp
from jax import lax
from jax.experimental import pallas as pl
from jax.experimental.pallas import tpu as pltpu
from jax.sharding import PartitionSpec as P

HEADS = 64
KVH = 8
LANES = 128
CHUNK = 1024
VMEM_LIMIT = 32 * 1024 * 1024
VMEM = pl.BlockSpec(memory_space=pltpu.VMEM)
SMEM = pl.BlockSpec(memory_space=pltpu.SMEM)
PARAMS = pltpu.CompilerParams(vmem_limit_bytes=VMEM_LIMIT)
TURNS = ((4, 1, 6, 2, 0), (5, 1, 7, 3, 0))
SENT = len(TURNS[0]) - 1
EARLY = 2
SHARED = [first == second for first, second in zip(*TURNS)]


def scalars_kernel(ids_hbm, *refs):
    ids_ref, arrived = refs[-2:]
    copy = pltpu.make_async_copy(ids_hbm, ids_ref, arrived)
    copy.start()
    copy.wait()


def scalars(ids, *beside):
    size = sum(array.size * array.dtype.itemsize for array in beside)
    return pl.pallas_call(
        scalars_kernel,
        out_shape=pltpu.SMEM(ids.shape, ids.dtype),
        in_specs=[pl.BlockSpec(memory_space=pl.ANY)] * (1 + len(beside)),
        out_specs=SMEM,
        scratch_shapes=[pltpu.SemaphoreType.DMA(())],
        compiler_params=PARAMS,
        cost_estimate=pl.CostEstimate(flops=0, transcendentals=0, bytes_accessed=size),
        name="scalars",
    )(*[pltpu.with_memory_space_constraint(array, pltpu.HBM) for array in (ids,) + beside])


def near(array):
    return pltpu.with_memory_space_constraint(array, pltpu.VMEM)


def owner_kernel(turns, ids_ref, down_ref, mine_ref, other_ref, *refs):
    amount = len(turns)
    hidden_refs, (delta_refs, scratch) = refs[:amount], (refs[-3 - amount : -3], refs[-3:])
    state_ref, sum_ref, row_ref = scratch
    count, rank, width = down_ref.shape
    rows = state_ref.shape[1]
    heads = row_ref.shape[0]
    me, core = lax.axis_index("store"), lax.axis_index("tensor")

    def slot_of(partners, row, shared):
        source = me ^ jnp.where(core == 0, partners[0], partners[1])
        slot = ids_ref[source * rows + row] - me * count
        mine = jnp.logical_not(shared) | (core == lax.rem(row, len(TURNS)))
        return slot, mine & (slot >= 0) & (slot < count)

    owned = {}
    for i, turn in enumerate(turns):
        for row in range(rows):
            owned[i, row] = slot_of([steps[turn] for steps in TURNS], row, SHARED[turn])[1]

            @pl.when(owned[i, row])
            def _():
                state_ref[i, row : row + 1] = hidden_refs[i][row : row + 1, :].astype(jnp.float32)

        delta_refs[i][...] = jnp.zeros(delta_refs[i].shape, delta_refs[i].dtype)

    packed = [sum(steps[turn] << (4 * i) for i, turn in enumerate(turns)) for steps in TURNS]
    both = sum(SHARED[turn] << i for i, turn in enumerate(turns))

    def one_request(index, carry):
        i, row = lax.div(index, rows), lax.rem(index, rows)
        partners = [(jnp.int32(value) >> (4 * i)) & 15 for value in packed]
        slot, here = slot_of(partners, row, ((jnp.int32(both) >> i) & 1) == 1)

        @pl.when(here)
        def _():
            total = jnp.zeros((rank, CHUNK), jnp.float32)
            for start in range(0, width, CHUNK):
                down = down_ref[slot, :, start : start + CHUNK].astype(jnp.float32)
                total = total + down * state_ref[i, pl.ds(row, 1), start : start + CHUNK]
            low = jnp.sum(total, axis=1, keepdims=True)
            low = low.astype(jnp.bfloat16).astype(jnp.float32)
            for half, up_ref in ((core, mine_ref), (1 - core, other_ref)):
                for head in range(heads):
                    up = up_ref[slot, :, head * LANES : (head + 1) * LANES]
                    row_ref[head : head + 1, :] = jnp.sum(
                        up.astype(jnp.float32) * low, axis=0, keepdims=True
                    )
                sum_ref[i, row, half] = row_ref[...].astype(sum_ref.dtype)

        return carry

    lax.fori_loop(0, amount * rows, one_request, 0)
    for (i, row), here in owned.items():

        @pl.when(here)
        def _():
            delta_refs[i][row] = sum_ref[i, row]


def merge_kernel(own_ref, *refs):
    came_refs, (kept_ref, sent_ref) = refs[:-2], refs[-2:]
    core = lax.axis_index("tensor")
    for half, out_ref in ((core, kept_ref), (1 - core, sent_ref)):
        total = own_ref[:, half].astype(jnp.float32)
        for came_ref in came_refs:
            total = total + came_ref[:, half].astype(jnp.float32)
        out_ref[...] = total.astype(out_ref.dtype)


def attend_kernel(parts, live_ref, base_ref, *refs):
    delta_refs, (key_ref, value_ref, out_ref, rows_ref) = refs[:parts], refs[parts:]
    rows, kv_heads, slots, head_size = key_ref.shape
    heads = base_ref.shape[1]
    group = heads // kv_heads
    scale = 1.0 / (float(head_size) ** 0.5)
    scores = []
    for row in range(rows):
        query = base_ref[row].astype(jnp.float32)
        delta = delta_refs[0][row].astype(jnp.float32)
        for ref in delta_refs[1:]:
            delta = delta + ref[row].astype(jnp.float32)
        query = query + delta
        live = live_ref[row] > 0
        for kv in range(kv_heads):
            mine = query[kv * group : (kv + 1) * group].astype(jnp.bfloat16)
            score = lax.dot_general(
                mine,
                key_ref[row, kv],
                (((1,), (1,)), ((), ())),
                preferred_element_type=jnp.float32,
            )
            scores.append(jnp.where(live, score * scale, jnp.float32(-1e30)))
    scores = jnp.concatenate(scores, axis=0)
    grown = jnp.exp(scores - jnp.max(scores, axis=1, keepdims=True))
    weights = grown / jnp.sum(grown, axis=1, keepdims=True)
    for row in range(rows):
        for kv in range(kv_heads):
            at = (row * kv_heads + kv) * group
            rows_ref[row, kv * group : (kv + 1) * group, :] = jnp.dot(
                weights[at : at + group].astype(jnp.bfloat16),
                value_ref[row, kv],
                preferred_element_type=jnp.float32,
            )
    for head in range(heads):
        out_ref[:, head * LANES : (head + 1) * LANES] = rows_ref[:, head, :].astype(out_ref.dtype)


def shared_deltas(hidden, adapter_down, adapter_up, adapter_ids, block):
    rows, heads, head_size = block
    owners, cores = lax.axis_size("store"), len(TURNS)

    def turn_pairs(turn):
        return [
            (i * cores + core, (i ^ TURNS[core][turn]) * cores + core)
            for i in range(owners)
            for core in range(cores)
        ]

    def visit(array, turn):
        return lax.ppermute(array, ("store", "tensor"), turn_pairs(turn))

    def swap(array):
        return lax.ppermute(array, "tensor", [(0, 1), (1, 0)])

    states = [visit(hidden, turn) for turn in range(SENT)]
    other = swap(adapter_up)
    ids = scalars(adapter_ids, adapter_down, adapter_up)
    down, up, other = near(adapter_down), near(adapter_up), near(other)
    wide = (rows, cores, heads, head_size)

    def work(name, after, *turns):
        amount = len(turns)
        return pl.pallas_call(
            functools.partial(owner_kernel, turns),
            out_shape=[jax.ShapeDtypeStruct(wide, jnp.bfloat16)] * amount,
            in_specs=[SMEM] + [VMEM] * (amount + 3) + [pl.BlockSpec(memory_space=pl.ANY)] * len(after),
            out_specs=[VMEM] * amount,
            scratch_shapes=[
                pltpu.VMEM((amount,) + hidden.shape, jnp.float32),
                pltpu.VMEM((amount,) + wide, jnp.bfloat16),
                pltpu.VMEM((heads, head_size), jnp.float32),
            ],
            compiler_params=PARAMS,
            name=name,
        )(ids, down, up, other, *[states[turn] for turn in turns], *after)

    states.append(near(hidden))
    deltas = work("owner_first", (), *range(EARLY))
    deltas += work("owner_rest", deltas[:1], *range(EARLY, SENT + 1))
    came = [visit(delta, turn) for turn, delta in enumerate(deltas[:SENT])]
    kept, sent = pl.pallas_call(
        merge_kernel,
        out_shape=[jax.ShapeDtypeStruct(block, jnp.bfloat16)] * 2,
        in_specs=[VMEM] * (SENT + 1),
        out_specs=[VMEM] * 2,
        compiler_params=PARAMS,
        name="merge",
    )(deltas[-1], *came)
    return [kept, swap(sent)]


def exchanged_deltas(hidden, adapter_down, adapter_up, adapter_ids, block):
    count, rank, width = adapter_down.shape
    owners, rows = lax.axis_size("store"), hidden.shape[0]
    copies = jnp.broadcast_to(hidden[None], (owners,) + hidden.shape)
    everyone = lax.all_to_all(copies, "store", 0, 0, tiled=True).reshape(owners * rows, width)
    slot = adapter_ids - lax.axis_index("store") * count
    owned = slot[:, None] == jnp.arange(count, dtype=jnp.int32)[None, :]
    low = jnp.einsum(
        "rd,kd->rk",
        everyone,
        adapter_down.reshape(count * rank, width),
        preferred_element_type=jnp.float32,
    ).reshape(owners * rows, count, rank)
    low = (low * owned[:, :, None].astype(jnp.float32)).astype(jnp.bfloat16)
    parts = jnp.dot(
        low.reshape(owners * rows, count * rank),
        adapter_up.reshape(count * rank, -1),
        preferred_element_type=jnp.float32,
    )
    came = lax.all_to_all(parts.reshape((owners,) + block), "store", 0, 0, tiled=True)
    return [jnp.sum(came, axis=0)]


def per_device(
    hidden, query_base, adapter_down, adapter_up, adapter_ids, key_cache, value_cache, kv_lengths
):
    features = adapter_up.shape[2]
    rows, kv_heads, slots, head_size = key_cache.shape
    block = (rows, features // head_size, head_size)
    shared = (lax.axis_size("store"), lax.axis_size("tensor")) == (8, len(TURNS))
    deltas = (shared_deltas if shared else exchanged_deltas)(
        hidden, adapter_down, adapter_up, adapter_ids, block
    )
    live = jnp.arange(slots, dtype=jnp.int32)[None, None, :] < kv_lengths[:, None, None]
    return pl.pallas_call(
        functools.partial(attend_kernel, len(deltas)),
        out_shape=jax.ShapeDtypeStruct((rows, features), jnp.bfloat16),
        in_specs=[VMEM] * (len(deltas) + 4),
        out_specs=VMEM,
        scratch_shapes=[pltpu.VMEM(block, jnp.float32)],
        compiler_params=PARAMS,
        name="attend",
    )(
        near(live.astype(jnp.float32)),
        near(query_base.reshape(block)),
        *deltas,
        near(key_cache),
        near(value_cache),
    )


def solution(mesh):
    in_specs = (
        P(("groups", "store"), None),
        P(("groups", "store"), "tensor"),
        P(("groups", "store"), None, None),
        P(("groups", "store"), None, "tensor"),
        P("groups"),
        P(("groups", "store"), "tensor", None, None),
        P(("groups", "store"), "tensor", None, None),
        P(("groups", "store")),
    )
    out_specs = P(("groups", "store"), "tensor")
    return jax.shard_map(
        per_device, mesh=mesh, in_specs=in_specs, out_specs=out_specs, check_vma=False
    )
```

```python
import functools

import jax
import jax.numpy as jnp
from jax import lax
from jax.experimental import pallas as pl
from jax.experimental.pallas import tpu as pltpu
from jax.sharding import PartitionSpec as P

HEADS = 64
KVH = 8
LANES = 128
CHUNK = 1024
VMEM_LIMIT = 32 * 1024 * 1024
VMEM = pl.BlockSpec(memory_space=pltpu.VMEM)
SMEM = pl.BlockSpec(memory_space=pltpu.SMEM)
PARAMS = pltpu.CompilerParams(vmem_limit_bytes=VMEM_LIMIT)
TURNS = ((3, 1, 4, 2, 0), (7, 1, 5, 6, 0))
SENT = len(TURNS[0]) - 1
EARLY = 2
SHARED = [first == second for first, second in zip(*TURNS)]


def scalars_kernel(ids_hbm, *refs):
    ids_ref, arrived = refs[-2:]
    copy = pltpu.make_async_copy(ids_hbm, ids_ref, arrived)
    copy.start()
    copy.wait()


def scalars(ids, *beside):
    size = sum(array.size * array.dtype.itemsize for array in beside)
    return pl.pallas_call(
        scalars_kernel,
        out_shape=pltpu.SMEM(ids.shape, ids.dtype),
        in_specs=[pl.BlockSpec(memory_space=pl.ANY)] * (1 + len(beside)),
        out_specs=SMEM,
        scratch_shapes=[pltpu.SemaphoreType.DMA(())],
        compiler_params=PARAMS,
        cost_estimate=pl.CostEstimate(flops=0, transcendentals=0, bytes_accessed=size),
        name="scalars",
    )(*[pltpu.with_memory_space_constraint(array, pltpu.HBM) for array in (ids,) + beside])


def near(array):
    return pltpu.with_memory_space_constraint(array, pltpu.VMEM)


def owner_kernel(turns, ids_ref, down_ref, mine_ref, other_ref, *refs):
    amount = len(turns)
    hidden_refs, (delta_refs, scratch) = refs[:amount], (refs[-3 - amount : -3], refs[-3:])
    state_ref, sum_ref, row_ref = scratch
    count, rank, width = down_ref.shape
    rows = state_ref.shape[1]
    heads = row_ref.shape[0]
    me, core = lax.axis_index("store"), lax.axis_index("tensor")

    def slot_of(partners, row, shared):
        source = me ^ jnp.where(core == 0, partners[0], partners[1])
        slot = ids_ref[source * rows + row] - me * count
        mine = jnp.logical_not(shared) | (core == lax.rem(row, len(TURNS)))
        return slot, mine & (slot >= 0) & (slot < count)

    owned = {}
    for i, turn in enumerate(turns):
        for row in range(rows):
            owned[i, row] = slot_of([steps[turn] for steps in TURNS], row, SHARED[turn])[1]

            @pl.when(owned[i, row])
            def _():
                state_ref[i, row : row + 1] = hidden_refs[i][row : row + 1, :].astype(jnp.float32)

        delta_refs[i][...] = jnp.zeros(delta_refs[i].shape, delta_refs[i].dtype)

    packed = [sum(steps[turn] << (4 * i) for i, turn in enumerate(turns)) for steps in TURNS]
    both = sum(SHARED[turn] << i for i, turn in enumerate(turns))

    def one_request(index, carry):
        i, row = lax.div(index, rows), lax.rem(index, rows)
        partners = [(jnp.int32(value) >> (4 * i)) & 15 for value in packed]
        slot, here = slot_of(partners, row, ((jnp.int32(both) >> i) & 1) == 1)

        @pl.when(here)
        def _():
            total = jnp.zeros((rank, CHUNK), jnp.float32)
            for start in range(0, width, CHUNK):
                down = down_ref[slot, :, start : start + CHUNK].astype(jnp.float32)
                total = total + down * state_ref[i, pl.ds(row, 1), start : start + CHUNK]
            low = jnp.sum(total, axis=1, keepdims=True)
            low = low.astype(jnp.bfloat16).astype(jnp.float32)
            for half, up_ref in ((core, mine_ref), (1 - core, other_ref)):
                for head in range(heads):
                    up = up_ref[slot, :, head * LANES : (head + 1) * LANES]
                    row_ref[head : head + 1, :] = jnp.sum(
                        up.astype(jnp.float32) * low, axis=0, keepdims=True
                    )
                sum_ref[i, row, half] = row_ref[...].astype(sum_ref.dtype)

        return carry

    lax.fori_loop(0, amount * rows, one_request, 0)
    for (i, row), here in owned.items():

        @pl.when(here)
        def _():
            delta_refs[i][row] = sum_ref[i, row]


def merge_kernel(own_ref, *refs):
    came_refs, (kept_ref, sent_ref) = refs[:-2], refs[-2:]
    core = lax.axis_index("tensor")
    for half, out_ref in ((core, kept_ref), (1 - core, sent_ref)):
        total = own_ref[:, half].astype(jnp.float32)
        for came_ref in came_refs:
            total = total + came_ref[:, half].astype(jnp.float32)
        out_ref[...] = total.astype(out_ref.dtype)


def attend_kernel(parts, live_ref, base_ref, *refs):
    delta_refs, (key_ref, value_ref, out_ref, rows_ref) = refs[:parts], refs[parts:]
    rows, kv_heads, slots, head_size = key_ref.shape
    heads = base_ref.shape[1]
    group = heads // kv_heads
    scale = 1.0 / (float(head_size) ** 0.5)
    scores = []
    for row in range(rows):
        query = base_ref[row].astype(jnp.float32)
        delta = delta_refs[0][row].astype(jnp.float32)
        for ref in delta_refs[1:]:
            delta = delta + ref[row].astype(jnp.float32)
        query = query + delta
        live = live_ref[row] > 0
        for kv in range(kv_heads):
            mine = query[kv * group : (kv + 1) * group].astype(jnp.bfloat16)
            score = lax.dot_general(
                mine,
                key_ref[row, kv],
                (((1,), (1,)), ((), ())),
                preferred_element_type=jnp.float32,
            )
            scores.append(jnp.where(live, score * scale, jnp.float32(-1e30)))
    scores = jnp.concatenate(scores, axis=0)
    grown = jnp.exp(scores - jnp.max(scores, axis=1, keepdims=True))
    weights = grown / jnp.sum(grown, axis=1, keepdims=True)
    for row in range(rows):
        for kv in range(kv_heads):
            at = (row * kv_heads + kv) * group
            rows_ref[row, kv * group : (kv + 1) * group, :] = jnp.dot(
                weights[at : at + group].astype(jnp.bfloat16),
                value_ref[row, kv],
                preferred_element_type=jnp.float32,
            )
    for head in range(heads):
        out_ref[:, head * LANES : (head + 1) * LANES] = rows_ref[:, head, :].astype(out_ref.dtype)


def shared_deltas(hidden, adapter_down, adapter_up, adapter_ids, block):
    rows, heads, head_size = block
    owners, cores = lax.axis_size("store"), len(TURNS)

    def turn_pairs(turn):
        return [
            (i * cores + core, (i ^ TURNS[core][turn]) * cores + core)
            for i in range(owners)
            for core in range(cores)
        ]

    def visit(array, turn):
        return lax.ppermute(array, ("store", "tensor"), turn_pairs(turn))

    def swap(array):
        return lax.ppermute(array, "tensor", [(0, 1), (1, 0)])

    states = [visit(hidden, turn) for turn in range(SENT)]
    other = swap(adapter_up)
    ids = scalars(adapter_ids, adapter_down, adapter_up)
    down, up, other = near(adapter_down), near(adapter_up), near(other)
    wide = (rows, cores, heads, head_size)

    def work(name, after, *turns):
        amount = len(turns)
        return pl.pallas_call(
            functools.partial(owner_kernel, turns),
            out_shape=[jax.ShapeDtypeStruct(wide, jnp.bfloat16)] * amount,
            in_specs=[SMEM] + [VMEM] * (amount + 3) + [pl.BlockSpec(memory_space=pl.ANY)] * len(after),
            out_specs=[VMEM] * amount,
            scratch_shapes=[
                pltpu.VMEM((amount,) + hidden.shape, jnp.float32),
                pltpu.VMEM((amount,) + wide, jnp.bfloat16),
                pltpu.VMEM((heads, head_size), jnp.float32),
            ],
            compiler_params=PARAMS,
            name=name,
        )(ids, down, up, other, *[states[turn] for turn in turns], *after)

    states.append(near(hidden))
    deltas = work("owner_first", (), *range(EARLY))
    deltas += work("owner_rest", deltas[:1], *range(EARLY, SENT + 1))
    came = [visit(delta, turn) for turn, delta in enumerate(deltas[:SENT])]
    kept, sent = pl.pallas_call(
        merge_kernel,
        out_shape=[jax.ShapeDtypeStruct(block, jnp.bfloat16)] * 2,
        in_specs=[VMEM] * (SENT + 1),
        out_specs=[VMEM] * 2,
        compiler_params=PARAMS,
        name="merge",
    )(deltas[-1], *came)
    return [kept, swap(sent)]


def exchanged_deltas(hidden, adapter_down, adapter_up, adapter_ids, block):
    count, rank, width = adapter_down.shape
    owners, rows = lax.axis_size("store"), hidden.shape[0]
    copies = jnp.broadcast_to(hidden[None], (owners,) + hidden.shape)
    everyone = lax.all_to_all(copies, "store", 0, 0, tiled=True).reshape(owners * rows, width)
    slot = adapter_ids - lax.axis_index("store") * count
    owned = slot[:, None] == jnp.arange(count, dtype=jnp.int32)[None, :]
    low = jnp.einsum(
        "rd,kd->rk",
        everyone,
        adapter_down.reshape(count * rank, width),
        preferred_element_type=jnp.float32,
    ).reshape(owners * rows, count, rank)
    low = (low * owned[:, :, None].astype(jnp.float32)).astype(jnp.bfloat16)
    parts = jnp.dot(
        low.reshape(owners * rows, count * rank),
        adapter_up.reshape(count * rank, -1),
        preferred_element_type=jnp.float32,
    )
    came = lax.all_to_all(parts.reshape((owners,) + block), "store", 0, 0, tiled=True)
    return [jnp.sum(came, axis=0)]


def per_device(
    hidden, query_base, adapter_down, adapter_up, adapter_ids, key_cache, value_cache, kv_lengths
):
    features = adapter_up.shape[2]
    rows, kv_heads, slots, head_size = key_cache.shape
    block = (rows, features // head_size, head_size)
    shared = (lax.axis_size("store"), lax.axis_size("tensor")) == (8, len(TURNS))
    deltas = (shared_deltas if shared else exchanged_deltas)(
        hidden, adapter_down, adapter_up, adapter_ids, block
    )
    live = jnp.arange(slots, dtype=jnp.int32)[None, None, :] < kv_lengths[:, None, None]
    return pl.pallas_call(
        functools.partial(attend_kernel, len(deltas)),
        out_shape=jax.ShapeDtypeStruct((rows, features), jnp.bfloat16),
        in_specs=[VMEM] * (len(deltas) + 4),
        out_specs=VMEM,
        scratch_shapes=[pltpu.VMEM(block, jnp.float32)],
        compiler_params=PARAMS,
        name="attend",
    )(
        near(live.astype(jnp.float32)),
        near(query_base.reshape(block)),
        *deltas,
        near(key_cache),
        near(value_cache),
    )


def solution(mesh):
    in_specs = (
        P(("groups", "store"), None),
        P(("groups", "store"), "tensor"),
        P(("groups", "store"), None, None),
        P(("groups", "store"), None, "tensor"),
        P("groups"),
        P(("groups", "store"), "tensor", None, None),
        P(("groups", "store"), "tensor", None, None),
        P(("groups", "store")),
    )
    out_specs = P(("groups", "store"), "tensor")
    return jax.shard_map(
        per_device, mesh=mesh, in_specs=in_specs, out_specs=out_specs, check_vma=False
    )
```

```python
import functools

import jax
import jax.numpy as jnp
from jax import lax
from jax.experimental import pallas as pl
from jax.experimental.pallas import tpu as pltpu
from jax.sharding import PartitionSpec as P

HEADS = 64
KVH = 8
LANES = 128
CHUNK = 1024
VMEM_LIMIT = 32 * 1024 * 1024
VMEM = pl.BlockSpec(memory_space=pltpu.VMEM)
SMEM = pl.BlockSpec(memory_space=pltpu.SMEM)
PARAMS = pltpu.CompilerParams(vmem_limit_bytes=VMEM_LIMIT)
TURNS = ((3, 1, 4, 2, 0), (7, 1, 5, 6, 0))
SENT = len(TURNS[0]) - 1
EARLY = 2
SHARED = [first == second for first, second in zip(*TURNS)]


def scalars_kernel(ids_hbm, *refs):
    ids_ref, arrived = refs[-2:]
    copy = pltpu.make_async_copy(ids_hbm, ids_ref, arrived)
    copy.start()
    copy.wait()


def scalars(ids, *beside):
    size = sum(array.size * array.dtype.itemsize for array in beside)
    return pl.pallas_call(
        scalars_kernel,
        out_shape=pltpu.SMEM(ids.shape, ids.dtype),
        in_specs=[pl.BlockSpec(memory_space=pl.ANY)] * (1 + len(beside)),
        out_specs=SMEM,
        scratch_shapes=[pltpu.SemaphoreType.DMA(())],
        compiler_params=PARAMS,
        cost_estimate=pl.CostEstimate(flops=0, transcendentals=0, bytes_accessed=size),
        name="scalars",
    )(*[pltpu.with_memory_space_constraint(array, pltpu.HBM) for array in (ids,) + beside])


def near(array):
    return pltpu.with_memory_space_constraint(array, pltpu.VMEM)


def owner_kernel(turns, ids_ref, down_ref, mine_ref, other_ref, *refs):
    amount = len(turns)
    hidden_refs, (delta_refs, scratch) = refs[:amount], (refs[-3 - amount : -3], refs[-3:])
    state_ref, sum_ref, row_ref = scratch
    count, rank, width = down_ref.shape
    rows = state_ref.shape[1]
    heads = row_ref.shape[0]
    me, core = lax.axis_index("store"), lax.axis_index("tensor")

    def slot_of(partners, row, shared):
        source = me ^ jnp.where(core == 0, partners[0], partners[1])
        slot = ids_ref[source * rows + row] - me * count
        mine = jnp.logical_not(shared) | (core == lax.rem(row, len(TURNS)))
        return slot, mine & (slot >= 0) & (slot < count)

    owned = {}
    for i, turn in enumerate(turns):
        for row in range(rows):
            owned[i, row] = slot_of([steps[turn] for steps in TURNS], row, SHARED[turn])[1]

            @pl.when(owned[i, row])
            def _():
                state_ref[i, row : row + 1] = hidden_refs[i][row : row + 1, :].astype(jnp.float32)

        delta_refs[i][...] = jnp.zeros(delta_refs[i].shape, delta_refs[i].dtype)

    packed = [sum(steps[turn] << (4 * i) for i, turn in enumerate(turns)) for steps in TURNS]
    both = sum(SHARED[turn] << i for i, turn in enumerate(turns))

    def one_request(index, carry):
        i, row = lax.div(index, rows), lax.rem(index, rows)
        partners = [(jnp.int32(value) >> (4 * i)) & 15 for value in packed]
        slot, here = slot_of(partners, row, ((jnp.int32(both) >> i) & 1) == 1)

        @pl.when(here)
        def _():
            total = jnp.zeros((rank, CHUNK), jnp.float32)
            for start in range(0, width, CHUNK):
                down = down_ref[slot, :, start : start + CHUNK].astype(jnp.float32)
                total = total + down * state_ref[i, pl.ds(row, 1), start : start + CHUNK]
            low = jnp.sum(total, axis=1, keepdims=True)
            low = low.astype(jnp.bfloat16).astype(jnp.float32)
            for half, up_ref in ((core, mine_ref), (1 - core, other_ref)):
                for head in range(heads):
                    up = up_ref[slot, :, head * LANES : (head + 1) * LANES]
                    row_ref[head : head + 1, :] = jnp.sum(
                        up.astype(jnp.float32) * low, axis=0, keepdims=True
                    )
                sum_ref[i, row, half] = row_ref[...].astype(sum_ref.dtype)

        return carry

    lax.fori_loop(0, amount * rows, one_request, 0)
    for (i, row), here in owned.items():

        @pl.when(here)
        def _():
            delta_refs[i][row] = sum_ref[i, row]


def merge_kernel(own_ref, *refs):
    came_refs, (kept_ref, sent_ref) = refs[:-2], refs[-2:]
    core = lax.axis_index("tensor")
    for half, out_ref in ((core, kept_ref), (1 - core, sent_ref)):
        total = own_ref[:, half].astype(jnp.float32)
        for came_ref in came_refs:
            total = total + came_ref[:, half].astype(jnp.float32)
        out_ref[...] = total.astype(out_ref.dtype)


def turn_kernel(key_ref, turned_ref):
    for row in range(key_ref.shape[0]):
        for kv in range(key_ref.shape[1]):
            turned_ref[row, kv] = key_ref[row, kv].T


def attend_kernel(parts, live_ref, base_ref, *refs):
    delta_refs, (key_ref, value_ref, out_ref, rows_ref) = refs[:parts], refs[parts:]
    rows, kv_heads, slots, head_size = value_ref.shape
    heads = base_ref.shape[1]
    group = heads // kv_heads
    scale = 1.0 / (float(head_size) ** 0.5)
    scores = []
    for row in range(rows):
        query = base_ref[row].astype(jnp.float32)
        delta = delta_refs[0][row].astype(jnp.float32)
        for ref in delta_refs[1:]:
            delta = delta + ref[row].astype(jnp.float32)
        query = query + delta
        live = live_ref[row] > 0
        for kv in range(kv_heads):
            mine = query[kv * group : (kv + 1) * group].astype(jnp.bfloat16)
            score = lax.dot_general(
                mine,
                key_ref[row, kv],
                (((1,), (0,)), ((), ())),
                preferred_element_type=jnp.float32,
            )
            scores.append(jnp.where(live, score * scale, jnp.float32(-1e30)))
    scores = jnp.concatenate(scores, axis=0)
    grown = jnp.exp(scores - jnp.max(scores, axis=1, keepdims=True))
    weights = grown / jnp.sum(grown, axis=1, keepdims=True)
    for row in range(rows):
        for kv in range(kv_heads):
            at = (row * kv_heads + kv) * group
            rows_ref[row, kv * group : (kv + 1) * group, :] = jnp.dot(
                weights[at : at + group].astype(jnp.bfloat16),
                value_ref[row, kv],
                preferred_element_type=jnp.float32,
            )
    for head in range(heads):
        out_ref[:, head * LANES : (head + 1) * LANES] = rows_ref[:, head, :].astype(out_ref.dtype)


def shared_deltas(hidden, adapter_down, adapter_up, adapter_ids, block):
    rows, heads, head_size = block
    owners, cores = lax.axis_size("store"), len(TURNS)

    def turn_pairs(turn):
        return [
            (i * cores + core, (i ^ TURNS[core][turn]) * cores + core)
            for i in range(owners)
            for core in range(cores)
        ]

    def visit(array, turn):
        return lax.ppermute(array, ("store", "tensor"), turn_pairs(turn))

    def swap(array):
        return lax.ppermute(array, "tensor", [(0, 1), (1, 0)])

    states = [visit(hidden, turn) for turn in range(SENT)]
    other = swap(adapter_up)
    ids = scalars(adapter_ids, adapter_down, adapter_up)
    down, up, other = near(adapter_down), near(adapter_up), near(other)
    wide = (rows, cores, heads, head_size)

    def work(name, after, *turns):
        amount = len(turns)
        return pl.pallas_call(
            functools.partial(owner_kernel, turns),
            out_shape=[jax.ShapeDtypeStruct(wide, jnp.bfloat16)] * amount,
            in_specs=[SMEM] + [VMEM] * (amount + 3) + [pl.BlockSpec(memory_space=pl.ANY)] * len(after),
            out_specs=[VMEM] * amount,
            scratch_shapes=[
                pltpu.VMEM((amount,) + hidden.shape, jnp.float32),
                pltpu.VMEM((amount,) + wide, jnp.bfloat16),
                pltpu.VMEM((heads, head_size), jnp.float32),
            ],
            compiler_params=PARAMS,
            name=name,
        )(ids, down, up, other, *[states[turn] for turn in turns], *after)

    states.append(near(hidden))
    deltas = work("owner_first", (), *range(EARLY))
    deltas += work("owner_rest", deltas[:1], *range(EARLY, SENT + 1))
    came = [visit(delta, turn) for turn, delta in enumerate(deltas[:SENT])]
    kept, sent = pl.pallas_call(
        merge_kernel,
        out_shape=[jax.ShapeDtypeStruct(block, jnp.bfloat16)] * 2,
        in_specs=[VMEM] * (SENT + 1),
        out_specs=[VMEM] * 2,
        compiler_params=PARAMS,
        name="merge",
    )(deltas[-1], *came)
    return [kept, swap(sent)]


def exchanged_deltas(hidden, adapter_down, adapter_up, adapter_ids, block):
    count, rank, width = adapter_down.shape
    owners, rows = lax.axis_size("store"), hidden.shape[0]
    copies = jnp.broadcast_to(hidden[None], (owners,) + hidden.shape)
    everyone = lax.all_to_all(copies, "store", 0, 0, tiled=True).reshape(owners * rows, width)
    slot = adapter_ids - lax.axis_index("store") * count
    owned = slot[:, None] == jnp.arange(count, dtype=jnp.int32)[None, :]
    low = jnp.einsum(
        "rd,kd->rk",
        everyone,
        adapter_down.reshape(count * rank, width),
        preferred_element_type=jnp.float32,
    ).reshape(owners * rows, count, rank)
    low = (low * owned[:, :, None].astype(jnp.float32)).astype(jnp.bfloat16)
    parts = jnp.dot(
        low.reshape(owners * rows, count * rank),
        adapter_up.reshape(count * rank, -1),
        preferred_element_type=jnp.float32,
    )
    came = lax.all_to_all(parts.reshape((owners,) + block), "store", 0, 0, tiled=True)
    return [jnp.sum(came, axis=0)]


def per_device(
    hidden, query_base, adapter_down, adapter_up, adapter_ids, key_cache, value_cache, kv_lengths
):
    features = adapter_up.shape[2]
    rows, kv_heads, slots, head_size = key_cache.shape
    block = (rows, features // head_size, head_size)
    shared = (lax.axis_size("store"), lax.axis_size("tensor")) == (8, len(TURNS))
    deltas = (shared_deltas if shared else exchanged_deltas)(
        hidden, adapter_down, adapter_up, adapter_ids, block
    )
    turned = pl.pallas_call(
        turn_kernel,
        out_shape=jax.ShapeDtypeStruct((rows, kv_heads, head_size, slots), key_cache.dtype),
        in_specs=[VMEM],
        out_specs=VMEM,
        compiler_params=PARAMS,
        name="turn",
    )(near(key_cache))
    live = jnp.arange(slots, dtype=jnp.int32)[None, None, :] < kv_lengths[:, None, None]
    return pl.pallas_call(
        functools.partial(attend_kernel, len(deltas)),
        out_shape=jax.ShapeDtypeStruct((rows, features), jnp.bfloat16),
        in_specs=[VMEM] * (len(deltas) + 4),
        out_specs=VMEM,
        scratch_shapes=[pltpu.VMEM(block, jnp.float32)],
        compiler_params=PARAMS,
        name="attend",
    )(
        near(live.astype(jnp.float32)),
        near(query_base.reshape(block)),
        *deltas,
        near(turned),
        near(value_cache),
    )


def solution(mesh):
    in_specs = (
        P(("groups", "store"), None),
        P(("groups", "store"), "tensor"),
        P(("groups", "store"), None, None),
        P(("groups", "store"), None, "tensor"),
        P("groups"),
        P(("groups", "store"), "tensor", None, None),
        P(("groups", "store"), "tensor", None, None),
        P(("groups", "store")),
    )
    out_specs = P(("groups", "store"), "tensor")
    return jax.shard_map(
        per_device, mesh=mesh, in_specs=in_specs, out_specs=out_specs, check_vma=False
    )
```

```python
import functools

import jax
import jax.numpy as jnp
from jax import lax
from jax.experimental import pallas as pl
from jax.experimental.pallas import tpu as pltpu
from jax.sharding import PartitionSpec as P

HEADS = 64
KVH = 8
LANES = 128
CHUNK = 1024
VMEM_LIMIT = 32 * 1024 * 1024
VMEM = pl.BlockSpec(memory_space=pltpu.VMEM)
SMEM = pl.BlockSpec(memory_space=pltpu.SMEM)
PARAMS = pltpu.CompilerParams(vmem_limit_bytes=VMEM_LIMIT)
TURNS = ((4, 1, 3, 2, 0), (7, 1, 5, 6, 0))
SENT = len(TURNS[0]) - 1
EARLY = 2
SHARED = [first == second for first, second in zip(*TURNS)]


def scalars_kernel(ids_hbm, *refs):
    ids_ref, arrived = refs[-2:]
    copy = pltpu.make_async_copy(ids_hbm, ids_ref, arrived)
    copy.start()
    copy.wait()


def scalars(ids, *beside):
    size = sum(array.size * array.dtype.itemsize for array in beside)
    return pl.pallas_call(
        scalars_kernel,
        out_shape=pltpu.SMEM(ids.shape, ids.dtype),
        in_specs=[pl.BlockSpec(memory_space=pl.ANY)] * (1 + len(beside)),
        out_specs=SMEM,
        scratch_shapes=[pltpu.SemaphoreType.DMA(())],
        compiler_params=PARAMS,
        cost_estimate=pl.CostEstimate(flops=0, transcendentals=0, bytes_accessed=size),
        name="scalars",
    )(*[pltpu.with_memory_space_constraint(array, pltpu.HBM) for array in (ids,) + beside])


def near(array):
    return pltpu.with_memory_space_constraint(array, pltpu.VMEM)


def owner_kernel(turns, ids_ref, down_ref, mine_ref, other_ref, *refs):
    amount = len(turns)
    hidden_refs, (delta_refs, scratch) = refs[:amount], (refs[-3 - amount : -3], refs[-3:])
    state_ref, sum_ref, row_ref = scratch
    count, rank, width = down_ref.shape
    rows = state_ref.shape[1]
    heads = row_ref.shape[0]
    me, core = lax.axis_index("store"), lax.axis_index("tensor")

    def slot_of(partners, row, shared):
        source = me ^ jnp.where(core == 0, partners[0], partners[1])
        slot = ids_ref[source * rows + row] - me * count
        mine = jnp.logical_not(shared) | (core == lax.rem(row, len(TURNS)))
        return slot, mine & (slot >= 0) & (slot < count)

    owned = {}
    for i, turn in enumerate(turns):
        for row in range(rows):
            owned[i, row] = slot_of([steps[turn] for steps in TURNS], row, SHARED[turn])[1]

            @pl.when(owned[i, row])
            def _():
                state_ref[i, row : row + 1] = hidden_refs[i][row : row + 1, :].astype(jnp.float32)

        delta_refs[i][...] = jnp.zeros(delta_refs[i].shape, delta_refs[i].dtype)

    packed = [sum(steps[turn] << (4 * i) for i, turn in enumerate(turns)) for steps in TURNS]
    both = sum(SHARED[turn] << i for i, turn in enumerate(turns))

    def one_request(index, carry):
        i, row = lax.div(index, rows), lax.rem(index, rows)
        partners = [(jnp.int32(value) >> (4 * i)) & 15 for value in packed]
        slot, here = slot_of(partners, row, ((jnp.int32(both) >> i) & 1) == 1)

        @pl.when(here)
        def _():
            total = jnp.zeros((rank, CHUNK), jnp.float32)
            for start in range(0, width, CHUNK):
                down = down_ref[slot, :, start : start + CHUNK].astype(jnp.float32)
                total = total + down * state_ref[i, pl.ds(row, 1), start : start + CHUNK]
            low = jnp.sum(total, axis=1, keepdims=True)
            low = low.astype(jnp.bfloat16).astype(jnp.float32)
            for half, up_ref in ((core, mine_ref), (1 - core, other_ref)):
                for head in range(heads):
                    up = up_ref[slot, :, head * LANES : (head + 1) * LANES]
                    row_ref[head : head + 1, :] = jnp.sum(
                        up.astype(jnp.float32) * low, axis=0, keepdims=True
                    )
                sum_ref[i, row, half] = row_ref[...].astype(sum_ref.dtype)

        return carry

    lax.fori_loop(0, amount * rows, one_request, 0)
    for (i, row), here in owned.items():

        @pl.when(here)
        def _():
            delta_refs[i][row] = sum_ref[i, row]


def merge_kernel(own_ref, *refs):
    came_refs, (kept_ref, sent_ref) = refs[:-2], refs[-2:]
    core = lax.axis_index("tensor")
    for half, out_ref in ((core, kept_ref), (1 - core, sent_ref)):
        total = own_ref[:, half].astype(jnp.float32)
        for came_ref in came_refs:
            total = total + came_ref[:, half].astype(jnp.float32)
        out_ref[...] = total.astype(out_ref.dtype)


def attend_kernel(parts, live_ref, base_ref, *refs):
    delta_refs, (key_ref, value_ref, out_ref, rows_ref) = refs[:parts], refs[parts:]
    rows, kv_heads, slots, head_size = key_ref.shape
    heads = base_ref.shape[1]
    group = heads // kv_heads
    scale = 1.0 / (float(head_size) ** 0.5)
    scores = []
    for row in range(rows):
        query = base_ref[row].astype(jnp.float32)
        delta = delta_refs[0][row].astype(jnp.float32)
        for ref in delta_refs[1:]:
            delta = delta + ref[row].astype(jnp.float32)
        query = query + delta
        live = live_ref[row] > 0
        for kv in range(kv_heads):
            mine = query[kv * group : (kv + 1) * group].astype(jnp.bfloat16)
            score = lax.dot_general(
                mine,
                key_ref[row, kv],
                (((1,), (1,)), ((), ())),
                preferred_element_type=jnp.float32,
            )
            scores.append(jnp.where(live, score * scale, jnp.float32(-1e30)))
    scores = jnp.concatenate(scores, axis=0)
    grown = jnp.exp(scores - jnp.max(scores, axis=1, keepdims=True))
    weights = grown / jnp.sum(grown, axis=1, keepdims=True)
    for row in range(rows):
        for kv in range(kv_heads):
            at = (row * kv_heads + kv) * group
            rows_ref[row, kv * group : (kv + 1) * group, :] = jnp.dot(
                weights[at : at + group].astype(jnp.bfloat16),
                value_ref[row, kv],
                preferred_element_type=jnp.float32,
            )
    for head in range(heads):
        out_ref[:, head * LANES : (head + 1) * LANES] = rows_ref[:, head, :].astype(out_ref.dtype)


def shared_deltas(hidden, adapter_down, adapter_up, adapter_ids, block):
    rows, heads, head_size = block
    owners, cores = lax.axis_size("store"), len(TURNS)

    def turn_pairs(turn):
        return [
            (i * cores + core, (i ^ TURNS[core][turn]) * cores + core)
            for i in range(owners)
            for core in range(cores)
        ]

    def visit(array, turn):
        return lax.ppermute(array, ("store", "tensor"), turn_pairs(turn))

    def swap(array):
        return lax.ppermute(array, "tensor", [(0, 1), (1, 0)])

    states = [visit(hidden, turn) for turn in range(SENT)]
    other = swap(adapter_up)
    ids = scalars(adapter_ids, adapter_down, adapter_up)
    down, up, other = near(adapter_down), near(adapter_up), near(other)
    wide = (rows, cores, heads, head_size)

    def work(name, after, *turns):
        amount = len(turns)
        return pl.pallas_call(
            functools.partial(owner_kernel, turns),
            out_shape=[jax.ShapeDtypeStruct(wide, jnp.bfloat16)] * amount,
            in_specs=[SMEM] + [VMEM] * (amount + 3) + [pl.BlockSpec(memory_space=pl.ANY)] * len(after),
            out_specs=[VMEM] * amount,
            scratch_shapes=[
                pltpu.VMEM((amount,) + hidden.shape, jnp.float32),
                pltpu.VMEM((amount,) + wide, jnp.bfloat16),
                pltpu.VMEM((heads, head_size), jnp.float32),
            ],
            compiler_params=PARAMS,
            name=name,
        )(ids, down, up, other, *[states[turn] for turn in turns], *after)

    states.append(near(hidden))
    deltas = work("owner_first", (), *range(EARLY))
    deltas += work("owner_rest", deltas[:1], *range(EARLY, SENT + 1))
    came = [visit(delta, turn) for turn, delta in enumerate(deltas[:SENT])]
    kept, sent = pl.pallas_call(
        merge_kernel,
        out_shape=[jax.ShapeDtypeStruct(block, jnp.bfloat16)] * 2,
        in_specs=[VMEM] * (SENT + 1),
        out_specs=[VMEM] * 2,
        compiler_params=PARAMS,
        name="merge",
    )(deltas[-1], *came)
    return [kept, swap(sent)]


def exchanged_deltas(hidden, adapter_down, adapter_up, adapter_ids, block):
    count, rank, width = adapter_down.shape
    owners, rows = lax.axis_size("store"), hidden.shape[0]
    copies = jnp.broadcast_to(hidden[None], (owners,) + hidden.shape)
    everyone = lax.all_to_all(copies, "store", 0, 0, tiled=True).reshape(owners * rows, width)
    slot = adapter_ids - lax.axis_index("store") * count
    owned = slot[:, None] == jnp.arange(count, dtype=jnp.int32)[None, :]
    low = jnp.einsum(
        "rd,kd->rk",
        everyone,
        adapter_down.reshape(count * rank, width),
        preferred_element_type=jnp.float32,
    ).reshape(owners * rows, count, rank)
    low = (low * owned[:, :, None].astype(jnp.float32)).astype(jnp.bfloat16)
    parts = jnp.dot(
        low.reshape(owners * rows, count * rank),
        adapter_up.reshape(count * rank, -1),
        preferred_element_type=jnp.float32,
    )
    came = lax.all_to_all(parts.reshape((owners,) + block), "store", 0, 0, tiled=True)
    return [jnp.sum(came, axis=0)]


def per_device(
    hidden, query_base, adapter_down, adapter_up, adapter_ids, key_cache, value_cache, kv_lengths
):
    features = adapter_up.shape[2]
    rows, kv_heads, slots, head_size = key_cache.shape
    block = (rows, features // head_size, head_size)
    shared = (lax.axis_size("store"), lax.axis_size("tensor")) == (8, len(TURNS))
    deltas = (shared_deltas if shared else exchanged_deltas)(
        hidden, adapter_down, adapter_up, adapter_ids, block
    )
    live = jnp.arange(slots, dtype=jnp.int32)[None, None, :] < kv_lengths[:, None, None]
    return pl.pallas_call(
        functools.partial(attend_kernel, len(deltas)),
        out_shape=jax.ShapeDtypeStruct((rows, features), jnp.bfloat16),
        in_specs=[VMEM] * (len(deltas) + 4),
        out_specs=VMEM,
        scratch_shapes=[pltpu.VMEM(block, jnp.float32)],
        compiler_params=PARAMS,
        name="attend",
    )(
        near(live.astype(jnp.float32)),
        near(query_base.reshape(block)),
        *deltas,
        near(key_cache),
        near(value_cache),
    )


def solution(mesh):
    in_specs = (
        P(("groups", "store"), None),
        P(("groups", "store"), "tensor"),
        P(("groups", "store"), None, None),
        P(("groups", "store"), None, "tensor"),
        P("groups"),
        P(("groups", "store"), "tensor", None, None),
        P(("groups", "store"), "tensor", None, None),
        P(("groups", "store")),
    )
    out_specs = P(("groups", "store"), "tensor")
    return jax.shard_map(
        per_device, mesh=mesh, in_specs=in_specs, out_specs=out_specs, check_vma=False
    )
```

```python
import functools

import jax
import jax.numpy as jnp
from jax import lax
from jax.experimental import pallas as pl
from jax.experimental.pallas import tpu as pltpu
from jax.sharding import PartitionSpec as P

HEADS = 64
KVH = 8
LANES = 128
CHUNK = 1024
VMEM_LIMIT = 32 * 1024 * 1024
VMEM = pl.BlockSpec(memory_space=pltpu.VMEM)
SMEM = pl.BlockSpec(memory_space=pltpu.SMEM)
PARAMS = pltpu.CompilerParams(vmem_limit_bytes=VMEM_LIMIT)
TURNS = ((3, 1, 4, 2, 0), (7, 1, 5, 6, 0))
SENT = len(TURNS[0]) - 1
EARLY = 2
SHARED = [first == second for first, second in zip(*TURNS)]


def scalars_kernel(ids_hbm, *refs):
    ids_ref, arrived = refs[-2:]
    copy = pltpu.make_async_copy(ids_hbm, ids_ref, arrived)
    copy.start()
    copy.wait()


def scalars(ids, *beside):
    size = sum(array.size * array.dtype.itemsize for array in beside)
    return pl.pallas_call(
        scalars_kernel,
        out_shape=pltpu.SMEM(ids.shape, ids.dtype),
        in_specs=[pl.BlockSpec(memory_space=pl.ANY)] * (1 + len(beside)),
        out_specs=SMEM,
        scratch_shapes=[pltpu.SemaphoreType.DMA(())],
        compiler_params=PARAMS,
        cost_estimate=pl.CostEstimate(flops=0, transcendentals=0, bytes_accessed=size),
        name="scalars",
    )(*[pltpu.with_memory_space_constraint(array, pltpu.HBM) for array in (ids,) + beside])


def near(array):
    return pltpu.with_memory_space_constraint(array, pltpu.VMEM)


def owner_kernel(turns, ids_ref, down_ref, mine_ref, other_ref, *refs):
    amount = len(turns)
    hidden_refs, (delta_refs, scratch) = refs[:amount], (refs[-3 - amount : -3], refs[-3:])
    state_ref, sum_ref, row_ref = scratch
    count, rank, width = down_ref.shape
    rows = state_ref.shape[1]
    heads = row_ref.shape[0]
    me, core = lax.axis_index("store"), lax.axis_index("tensor")

    def slot_of(partners, row):
        source = me ^ jnp.where(core == 0, partners[0], partners[1])
        slot = ids_ref[source * rows + row] - me * count
        return slot, (slot >= 0) & (slot < count)

    owned = {}
    for i, turn in enumerate(turns):
        for row in range(rows):
            owned[i, row] = slot_of([steps[turn] for steps in TURNS], row)[1]

            @pl.when(owned[i, row])
            def _():
                state_ref[i, row : row + 1] = hidden_refs[i][row : row + 1, :].astype(jnp.float32)

        delta_refs[i][...] = jnp.zeros(delta_refs[i].shape, delta_refs[i].dtype)

    packed = [sum(steps[turn] << (4 * i) for i, turn in enumerate(turns)) for steps in TURNS]
    both = sum(SHARED[turn] << i for i, turn in enumerate(turns))

    def one_request(index, carry):
        i, row = lax.div(index, rows), lax.rem(index, rows)
        partners = [(jnp.int32(value) >> (4 * i)) & 15 for value in packed]
        slot, here = slot_of(partners, row)
        whole = ((jnp.int32(both) >> i) & 1) == 0

        @pl.when(here)
        def _():
            total = jnp.zeros((rank, CHUNK), jnp.float32)
            for start in range(0, width, CHUNK):
                down = down_ref[slot, :, start : start + CHUNK].astype(jnp.float32)
                total = total + down * state_ref[i, pl.ds(row, 1), start : start + CHUNK]
            low = jnp.sum(total, axis=1, keepdims=True)
            low = low.astype(jnp.bfloat16).astype(jnp.float32)

            def spread(half, up_ref):
                for head in range(heads):
                    up = up_ref[slot, :, head * LANES : (head + 1) * LANES]
                    row_ref[head : head + 1, :] = jnp.sum(
                        up.astype(jnp.float32) * low, axis=0, keepdims=True
                    )
                sum_ref[i, row, half] = row_ref[...].astype(sum_ref.dtype)

            spread(core, mine_ref)
            pl.when(whole)(lambda: spread(1 - core, other_ref))

        return carry

    lax.fori_loop(0, amount * rows, one_request, 0)
    for (i, row), here in owned.items():

        @pl.when(here)
        def _():
            part = sum_ref.at[i, row]
            delta_refs[i][row] = part[core] if SHARED[turns[i]] else part[...]


def merge_kernel(*refs):
    came_refs, (kept_ref, sent_ref) = refs[:-2], refs[-2:]
    core = lax.axis_index("tensor")
    for half, out_ref in ((core, kept_ref), (1 - core, sent_ref)):
        total = came_refs[0][:, half].astype(jnp.float32)
        for came_ref in came_refs[1:]:
            total = total + came_ref[:, half].astype(jnp.float32)
        out_ref[...] = total.astype(out_ref.dtype)


def attend_kernel(parts, live_ref, base_ref, *refs):
    delta_refs, (key_ref, value_ref, out_ref, rows_ref) = refs[:parts], refs[parts:]
    rows, kv_heads, slots, head_size = key_ref.shape
    heads = base_ref.shape[1]
    group = heads // kv_heads
    scale = 1.0 / (float(head_size) ** 0.5)
    scores = []
    for row in range(rows):
        query = base_ref[row].astype(jnp.float32)
        delta = delta_refs[0][row].astype(jnp.float32)
        for ref in delta_refs[1:]:
            delta = delta + ref[row].astype(jnp.float32)
        query = query + delta
        live = live_ref[row] > 0
        for kv in range(kv_heads):
            mine = query[kv * group : (kv + 1) * group].astype(jnp.bfloat16)
            score = lax.dot_general(
                mine,
                key_ref[row, kv],
                (((1,), (1,)), ((), ())),
                preferred_element_type=jnp.float32,
            )
            scores.append(jnp.where(live, score * scale, jnp.float32(-1e30)))
    scores = jnp.concatenate(scores, axis=0)
    grown = jnp.exp(scores - jnp.max(scores, axis=1, keepdims=True))
    weights = grown / jnp.sum(grown, axis=1, keepdims=True)
    for row in range(rows):
        for kv in range(kv_heads):
            at = (row * kv_heads + kv) * group
            rows_ref[row, kv * group : (kv + 1) * group, :] = jnp.dot(
                weights[at : at + group].astype(jnp.bfloat16),
                value_ref[row, kv],
                preferred_element_type=jnp.float32,
            )
    for head in range(heads):
        out_ref[:, head * LANES : (head + 1) * LANES] = rows_ref[:, head, :].astype(out_ref.dtype)


def shared_deltas(hidden, adapter_down, adapter_up, adapter_ids, block):
    rows, heads, head_size = block
    owners, cores = lax.axis_size("store"), len(TURNS)

    def turn_pairs(turn):
        return [
            (i * cores + core, (i ^ TURNS[core][turn]) * cores + core)
            for i in range(owners)
            for core in range(cores)
        ]

    def visit(array, turn):
        return lax.ppermute(array, ("store", "tensor"), turn_pairs(turn))

    def swap(array):
        return lax.ppermute(array, "tensor", [(0, 1), (1, 0)])

    states = [visit(hidden, turn) for turn in range(SENT)]
    other = swap(adapter_up)
    ids = scalars(adapter_ids, adapter_down, adapter_up)
    down, up, other = near(adapter_down), near(adapter_up), near(other)
    wide = (rows, cores, heads, head_size)

    def work(name, after, *turns):
        amount = len(turns)
        return pl.pallas_call(
            functools.partial(owner_kernel, turns),
            out_shape=[
                jax.ShapeDtypeStruct(block if SHARED[turn] else wide, jnp.bfloat16)
                for turn in turns
            ],
            in_specs=[SMEM] + [VMEM] * (amount + 3) + [pl.BlockSpec(memory_space=pl.ANY)] * len(after),
            out_specs=[VMEM] * amount,
            scratch_shapes=[
                pltpu.VMEM((amount,) + hidden.shape, jnp.float32),
                pltpu.VMEM((amount,) + wide, jnp.bfloat16),
                pltpu.VMEM((heads, head_size), jnp.float32),
            ],
            compiler_params=PARAMS,
            name=name,
        )(ids, down, up, other, *[states[turn] for turn in turns], *after)

    states.append(near(hidden))
    deltas = work("owner_first", (), *range(EARLY))
    deltas += work("owner_rest", deltas[:1], *range(EARLY, SENT + 1))
    came = [visit(delta, turn) for turn, delta in enumerate(deltas[:SENT])]
    halves = [came[turn] for turn in range(SENT) if SHARED[turn]]
    wholes = [came[turn] for turn in range(SENT) if not SHARED[turn]]
    kept, sent = pl.pallas_call(
        merge_kernel,
        out_shape=[jax.ShapeDtypeStruct(block, jnp.bfloat16)] * 2,
        in_specs=[VMEM] * len(wholes),
        out_specs=[VMEM] * 2,
        compiler_params=PARAMS,
        name="merge",
    )(*wholes)
    return [kept, deltas[-1], *halves, swap(sent)]


def exchanged_deltas(hidden, adapter_down, adapter_up, adapter_ids, block):
    count, rank, width = adapter_down.shape
    owners, rows = lax.axis_size("store"), hidden.shape[0]
    copies = jnp.broadcast_to(hidden[None], (owners,) + hidden.shape)
    everyone = lax.all_to_all(copies, "store", 0, 0, tiled=True).reshape(owners * rows, width)
    slot = adapter_ids - lax.axis_index("store") * count
    owned = slot[:, None] == jnp.arange(count, dtype=jnp.int32)[None, :]
    low = jnp.einsum(
        "rd,kd->rk",
        everyone,
        adapter_down.reshape(count * rank, width),
        preferred_element_type=jnp.float32,
    ).reshape(owners * rows, count, rank)
    low = (low * owned[:, :, None].astype(jnp.float32)).astype(jnp.bfloat16)
    parts = jnp.dot(
        low.reshape(owners * rows, count * rank),
        adapter_up.reshape(count * rank, -1),
        preferred_element_type=jnp.float32,
    )
    came = lax.all_to_all(parts.reshape((owners,) + block), "store", 0, 0, tiled=True)
    return [jnp.sum(came, axis=0)]


def per_device(
    hidden, query_base, adapter_down, adapter_up, adapter_ids, key_cache, value_cache, kv_lengths
):
    features = adapter_up.shape[2]
    rows, kv_heads, slots, head_size = key_cache.shape
    block = (rows, features // head_size, head_size)
    shared = (lax.axis_size("store"), lax.axis_size("tensor")) == (8, len(TURNS))
    deltas = (shared_deltas if shared else exchanged_deltas)(
        hidden, adapter_down, adapter_up, adapter_ids, block
    )
    live = jnp.arange(slots, dtype=jnp.int32)[None, None, :] < kv_lengths[:, None, None]
    return pl.pallas_call(
        functools.partial(attend_kernel, len(deltas)),
        out_shape=jax.ShapeDtypeStruct((rows, features), jnp.bfloat16),
        in_specs=[VMEM] * (len(deltas) + 4),
        out_specs=VMEM,
        scratch_shapes=[pltpu.VMEM(block, jnp.float32)],
        compiler_params=PARAMS,
        name="attend",
    )(
        near(live.astype(jnp.float32)),
        near(query_base.reshape(block)),
        *deltas,
        near(key_cache),
        near(value_cache),
    )


def solution(mesh):
    in_specs = (
        P(("groups", "store"), None),
        P(("groups", "store"), "tensor"),
        P(("groups", "store"), None, None),
        P(("groups", "store"), None, "tensor"),
        P("groups"),
        P(("groups", "store"), "tensor", None, None),
        P(("groups", "store"), "tensor", None, None),
        P(("groups", "store")),
    )
    out_specs = P(("groups", "store"), "tensor")
    return jax.shard_map(
        per_device, mesh=mesh, in_specs=in_specs, out_specs=out_specs, check_vma=False
    )
```

```python
import functools

import jax
import jax.numpy as jnp
from jax import lax
from jax.experimental import pallas as pl
from jax.experimental.pallas import tpu as pltpu
from jax.sharding import PartitionSpec as P

HEADS = 64
KVH = 8
LANES = 128
CHUNK = 1024
VMEM_LIMIT = 32 * 1024 * 1024
VMEM = pl.BlockSpec(memory_space=pltpu.VMEM)
SMEM = pl.BlockSpec(memory_space=pltpu.SMEM)
PARAMS = pltpu.CompilerParams(vmem_limit_bytes=VMEM_LIMIT)
TURNS = ((3, 1, 4, 2, 0), (7, 1, 5, 6, 0))
SENT = len(TURNS[0]) - 1
GROUPS = ((0, 1), (2, 3), (4,))
SHARED = [first == second for first, second in zip(*TURNS)]


def scalars_kernel(ids_hbm, *refs):
    ids_ref, arrived = refs[-2:]
    copy = pltpu.make_async_copy(ids_hbm, ids_ref, arrived)
    copy.start()
    copy.wait()


def scalars(ids, *beside):
    size = sum(array.size * array.dtype.itemsize for array in beside)
    return pl.pallas_call(
        scalars_kernel,
        out_shape=pltpu.SMEM(ids.shape, ids.dtype),
        in_specs=[pl.BlockSpec(memory_space=pl.ANY)] * (1 + len(beside)),
        out_specs=SMEM,
        scratch_shapes=[pltpu.SemaphoreType.DMA(())],
        compiler_params=PARAMS,
        cost_estimate=pl.CostEstimate(flops=0, transcendentals=0, bytes_accessed=size),
        name="scalars",
    )(*[pltpu.with_memory_space_constraint(array, pltpu.HBM) for array in (ids,) + beside])


def near(array):
    return pltpu.with_memory_space_constraint(array, pltpu.VMEM)


def owner_kernel(turns, ids_ref, down_ref, mine_ref, other_ref, *refs):
    amount = len(turns)
    hidden_refs, (delta_refs, scratch) = refs[:amount], (refs[-3 - amount : -3], refs[-3:])
    state_ref, sum_ref, row_ref = scratch
    count, rank, width = down_ref.shape
    rows = state_ref.shape[1]
    heads = row_ref.shape[0]
    me, core = lax.axis_index("store"), lax.axis_index("tensor")

    def slot_of(partners, row, shared):
        source = me ^ jnp.where(core == 0, partners[0], partners[1])
        slot = ids_ref[source * rows + row] - me * count
        mine = jnp.logical_not(shared) | (core == lax.rem(row, len(TURNS)))
        return slot, mine & (slot >= 0) & (slot < count)

    owned = {}
    for i, turn in enumerate(turns):
        for row in range(rows):
            owned[i, row] = slot_of([steps[turn] for steps in TURNS], row, SHARED[turn])[1]

            @pl.when(owned[i, row])
            def _():
                state_ref[i, row : row + 1] = hidden_refs[i][row : row + 1, :].astype(jnp.float32)

        delta_refs[i][...] = jnp.zeros(delta_refs[i].shape, delta_refs[i].dtype)

    packed = [sum(steps[turn] << (4 * i) for i, turn in enumerate(turns)) for steps in TURNS]
    both = sum(SHARED[turn] << i for i, turn in enumerate(turns))

    def one_request(index, carry):
        i, row = lax.div(index, rows), lax.rem(index, rows)
        partners = [(jnp.int32(value) >> (4 * i)) & 15 for value in packed]
        slot, here = slot_of(partners, row, ((jnp.int32(both) >> i) & 1) == 1)

        @pl.when(here)
        def _():
            total = jnp.zeros((rank, CHUNK), jnp.float32)
            for start in range(0, width, CHUNK):
                down = down_ref[slot, :, start : start + CHUNK].astype(jnp.float32)
                total = total + down * state_ref[i, pl.ds(row, 1), start : start + CHUNK]
            low = jnp.sum(total, axis=1, keepdims=True)
            low = low.astype(jnp.bfloat16).astype(jnp.float32)
            for half, up_ref in ((core, mine_ref), (1 - core, other_ref)):
                for head in range(heads):
                    up = up_ref[slot, :, head * LANES : (head + 1) * LANES]
                    row_ref[head : head + 1, :] = jnp.sum(
                        up.astype(jnp.float32) * low, axis=0, keepdims=True
                    )
                sum_ref[i, row, half] = row_ref[...].astype(sum_ref.dtype)

        return carry

    lax.fori_loop(0, amount * rows, one_request, 0)
    for (i, row), here in owned.items():

        @pl.when(here)
        def _():
            delta_refs[i][row] = sum_ref[i, row]


def merge_kernel(own_ref, *refs):
    came_refs, (kept_ref, sent_ref) = refs[:-2], refs[-2:]
    core = lax.axis_index("tensor")
    for half, out_ref in ((core, kept_ref), (1 - core, sent_ref)):
        total = own_ref[:, half].astype(jnp.float32)
        for came_ref in came_refs:
            total = total + came_ref[:, half].astype(jnp.float32)
        out_ref[...] = total.astype(out_ref.dtype)


def attend_kernel(parts, live_ref, base_ref, *refs):
    delta_refs, (key_ref, value_ref, out_ref, rows_ref) = refs[:parts], refs[parts:]
    rows, kv_heads, slots, head_size = key_ref.shape
    heads = base_ref.shape[1]
    group = heads // kv_heads
    scale = 1.0 / (float(head_size) ** 0.5)
    scores = []
    for row in range(rows):
        query = base_ref[row].astype(jnp.float32)
        delta = delta_refs[0][row].astype(jnp.float32)
        for ref in delta_refs[1:]:
            delta = delta + ref[row].astype(jnp.float32)
        query = query + delta
        live = live_ref[row] > 0
        for kv in range(kv_heads):
            mine = query[kv * group : (kv + 1) * group].astype(jnp.bfloat16)
            score = lax.dot_general(
                mine,
                key_ref[row, kv],
                (((1,), (1,)), ((), ())),
                preferred_element_type=jnp.float32,
            )
            scores.append(jnp.where(live, score * scale, jnp.float32(-1e30)))
    scores = jnp.concatenate(scores, axis=0)
    grown = jnp.exp(scores - jnp.max(scores, axis=1, keepdims=True))
    weights = grown / jnp.sum(grown, axis=1, keepdims=True)
    for row in range(rows):
        for kv in range(kv_heads):
            at = (row * kv_heads + kv) * group
            rows_ref[row, kv * group : (kv + 1) * group, :] = jnp.dot(
                weights[at : at + group].astype(jnp.bfloat16),
                value_ref[row, kv],
                preferred_element_type=jnp.float32,
            )
    for head in range(heads):
        out_ref[:, head * LANES : (head + 1) * LANES] = rows_ref[:, head, :].astype(out_ref.dtype)


def shared_deltas(hidden, adapter_down, adapter_up, adapter_ids, block):
    rows, heads, head_size = block
    owners, cores = lax.axis_size("store"), len(TURNS)

    def turn_pairs(turn):
        return [
            (i * cores + core, (i ^ TURNS[core][turn]) * cores + core)
            for i in range(owners)
            for core in range(cores)
        ]

    def visit(array, turn):
        return lax.ppermute(array, ("store", "tensor"), turn_pairs(turn))

    def swap(array):
        return lax.ppermute(array, "tensor", [(0, 1), (1, 0)])

    states = [visit(hidden, turn) for turn in range(SENT)]
    other = swap(adapter_up)
    ids = scalars(adapter_ids, adapter_down, adapter_up)
    down, up, other = near(adapter_down), near(adapter_up), near(other)
    wide = (rows, cores, heads, head_size)

    def work(name, after, *turns):
        amount = len(turns)
        return pl.pallas_call(
            functools.partial(owner_kernel, turns),
            out_shape=[jax.ShapeDtypeStruct(wide, jnp.bfloat16)] * amount,
            in_specs=[SMEM] + [VMEM] * (amount + 3) + [pl.BlockSpec(memory_space=pl.ANY)] * len(after),
            out_specs=[VMEM] * amount,
            scratch_shapes=[
                pltpu.VMEM((amount,) + hidden.shape, jnp.float32),
                pltpu.VMEM((amount,) + wide, jnp.bfloat16),
                pltpu.VMEM((heads, head_size), jnp.float32),
            ],
            compiler_params=PARAMS,
            name=name,
        )(ids, down, up, other, *[states[turn] for turn in turns], *after)

    states.append(near(hidden))
    deltas = []
    for group in GROUPS:
        after = [deltas[others[0]] for others in GROUPS if others[0] < group[0]][-1:]
        deltas += work("owner%d" % group[0], after, *group)
    came = [visit(delta, turn) for turn, delta in enumerate(deltas[:SENT])]
    kept, sent = pl.pallas_call(
        merge_kernel,
        out_shape=[jax.ShapeDtypeStruct(block, jnp.bfloat16)] * 2,
        in_specs=[VMEM] * (SENT + 1),
        out_specs=[VMEM] * 2,
        compiler_params=PARAMS,
        name="merge",
    )(deltas[-1], *came)
    return [kept, swap(sent)]


def exchanged_deltas(hidden, adapter_down, adapter_up, adapter_ids, block):
    count, rank, width = adapter_down.shape
    owners, rows = lax.axis_size("store"), hidden.shape[0]
    copies = jnp.broadcast_to(hidden[None], (owners,) + hidden.shape)
    everyone = lax.all_to_all(copies, "store", 0, 0, tiled=True).reshape(owners * rows, width)
    slot = adapter_ids - lax.axis_index("store") * count
    owned = slot[:, None] == jnp.arange(count, dtype=jnp.int32)[None, :]
    low = jnp.einsum(
        "rd,kd->rk",
        everyone,
        adapter_down.reshape(count * rank, width),
        preferred_element_type=jnp.float32,
    ).reshape(owners * rows, count, rank)
    low = (low * owned[:, :, None].astype(jnp.float32)).astype(jnp.bfloat16)
    parts = jnp.dot(
        low.reshape(owners * rows, count * rank),
        adapter_up.reshape(count * rank, -1),
        preferred_element_type=jnp.float32,
    )
    came = lax.all_to_all(parts.reshape((owners,) + block), "store", 0, 0, tiled=True)
    return [jnp.sum(came, axis=0)]


def per_device(
    hidden, query_base, adapter_down, adapter_up, adapter_ids, key_cache, value_cache, kv_lengths
):
    features = adapter_up.shape[2]
    rows, kv_heads, slots, head_size = key_cache.shape
    block = (rows, features // head_size, head_size)
    shared = (lax.axis_size("store"), lax.axis_size("tensor")) == (8, len(TURNS))
    deltas = (shared_deltas if shared else exchanged_deltas)(
        hidden, adapter_down, adapter_up, adapter_ids, block
    )
    live = jnp.arange(slots, dtype=jnp.int32)[None, None, :] < kv_lengths[:, None, None]
    return pl.pallas_call(
        functools.partial(attend_kernel, len(deltas)),
        out_shape=jax.ShapeDtypeStruct((rows, features), jnp.bfloat16),
        in_specs=[VMEM] * (len(deltas) + 4),
        out_specs=VMEM,
        scratch_shapes=[pltpu.VMEM(block, jnp.float32)],
        compiler_params=PARAMS,
        name="attend",
    )(
        near(live.astype(jnp.float32)),
        near(query_base.reshape(block)),
        *deltas,
        near(key_cache),
        near(value_cache),
    )


def solution(mesh):
    in_specs = (
        P(("groups", "store"), None),
        P(("groups", "store"), "tensor"),
        P(("groups", "store"), None, None),
        P(("groups", "store"), None, "tensor"),
        P("groups"),
        P(("groups", "store"), "tensor", None, None),
        P(("groups", "store"), "tensor", None, None),
        P(("groups", "store")),
    )
    out_specs = P(("groups", "store"), "tensor")
    return jax.shard_map(
        per_device, mesh=mesh, in_specs=in_specs, out_specs=out_specs, check_vma=False
    )
```

```python
import functools

import jax
import jax.numpy as jnp
from jax import lax
from jax.experimental import pallas as pl
from jax.experimental.pallas import tpu as pltpu
from jax.sharding import PartitionSpec as P

HEADS = 64
KVH = 8
LANES = 128
CHUNK = 512
VMEM_LIMIT = 32 * 1024 * 1024
VMEM = pl.BlockSpec(memory_space=pltpu.VMEM)
SMEM = pl.BlockSpec(memory_space=pltpu.SMEM)
PARAMS = pltpu.CompilerParams(vmem_limit_bytes=VMEM_LIMIT)
TURNS = ((3, 1, 4, 2, 0), (7, 1, 5, 6, 0))
SENT = len(TURNS[0]) - 1
GROUPS = ((0, 1), (2, 3), (4,))
SHARED = [first == second for first, second in zip(*TURNS)]


def scalars_kernel(ids_hbm, *refs):
    ids_ref, arrived = refs[-2:]
    copy = pltpu.make_async_copy(ids_hbm, ids_ref, arrived)
    copy.start()
    copy.wait()


def scalars(ids, *beside):
    size = sum(array.size * array.dtype.itemsize for array in beside)
    return pl.pallas_call(
        scalars_kernel,
        out_shape=pltpu.SMEM(ids.shape, ids.dtype),
        in_specs=[pl.BlockSpec(memory_space=pl.ANY)] * (1 + len(beside)),
        out_specs=SMEM,
        scratch_shapes=[pltpu.SemaphoreType.DMA(())],
        compiler_params=PARAMS,
        cost_estimate=pl.CostEstimate(flops=0, transcendentals=0, bytes_accessed=size),
        name="scalars",
    )(*[pltpu.with_memory_space_constraint(array, pltpu.HBM) for array in (ids,) + beside])


def near(array):
    return pltpu.with_memory_space_constraint(array, pltpu.VMEM)


def owner_kernel(turns, ids_ref, down_ref, mine_ref, other_ref, *refs):
    amount = len(turns)
    hidden_refs, (delta_refs, scratch) = refs[:amount], (refs[-3 - amount : -3], refs[-3:])
    state_ref, sum_ref, row_ref = scratch
    count, rank, width = down_ref.shape
    rows = state_ref.shape[1]
    heads = row_ref.shape[0]
    me, core = lax.axis_index("store"), lax.axis_index("tensor")

    def slot_of(partners, row, shared):
        source = me ^ jnp.where(core == 0, partners[0], partners[1])
        slot = ids_ref[source * rows + row] - me * count
        mine = jnp.logical_not(shared) | (core == lax.rem(row, len(TURNS)))
        return slot, mine & (slot >= 0) & (slot < count)

    owned = {}
    for i, turn in enumerate(turns):
        for row in range(rows):
            owned[i, row] = slot_of([steps[turn] for steps in TURNS], row, SHARED[turn])[1]

            @pl.when(owned[i, row])
            def _():
                state_ref[i, row : row + 1] = hidden_refs[i][row : row + 1, :].astype(jnp.float32)

        delta_refs[i][...] = jnp.zeros(delta_refs[i].shape, delta_refs[i].dtype)

    packed = [sum(steps[turn] << (4 * i) for i, turn in enumerate(turns)) for steps in TURNS]
    both = sum(SHARED[turn] << i for i, turn in enumerate(turns))

    def one_request(index, carry):
        i, row = lax.div(index, rows), lax.rem(index, rows)
        partners = [(jnp.int32(value) >> (4 * i)) & 15 for value in packed]
        slot, here = slot_of(partners, row, ((jnp.int32(both) >> i) & 1) == 1)

        @pl.when(here)
        def _():
            total = jnp.zeros((rank, CHUNK), jnp.float32)
            for start in range(0, width, CHUNK):
                down = down_ref[slot, :, start : start + CHUNK].astype(jnp.float32)
                total = total + down * state_ref[i, pl.ds(row, 1), start : start + CHUNK]
            low = jnp.sum(total, axis=1, keepdims=True)
            low = low.astype(jnp.bfloat16).astype(jnp.float32)
            for half, up_ref in ((core, mine_ref), (1 - core, other_ref)):
                for head in range(heads):
                    up = up_ref[slot, :, head * LANES : (head + 1) * LANES]
                    row_ref[head : head + 1, :] = jnp.sum(
                        up.astype(jnp.float32) * low, axis=0, keepdims=True
                    )
                sum_ref[i, row, half] = row_ref[...].astype(sum_ref.dtype)

        return carry

    lax.fori_loop(0, amount * rows, one_request, 0)
    for (i, row), here in owned.items():

        @pl.when(here)
        def _():
            delta_refs[i][row] = sum_ref[i, row]


def merge_kernel(own_ref, *refs):
    came_refs, (kept_ref, sent_ref) = refs[:-2], refs[-2:]
    core = lax.axis_index("tensor")
    for half, out_ref in ((core, kept_ref), (1 - core, sent_ref)):
        total = own_ref[:, half].astype(jnp.float32)
        for came_ref in came_refs:
            total = total + came_ref[:, half].astype(jnp.float32)
        out_ref[...] = total.astype(out_ref.dtype)


def attend_kernel(parts, live_ref, base_ref, *refs):
    delta_refs, (key_ref, value_ref, out_ref, rows_ref) = refs[:parts], refs[parts:]
    rows, kv_heads, slots, head_size = key_ref.shape
    heads = base_ref.shape[1]
    group = heads // kv_heads
    scale = 1.0 / (float(head_size) ** 0.5)
    scores = []
    for row in range(rows):
        query = base_ref[row].astype(jnp.float32)
        delta = delta_refs[0][row].astype(jnp.float32)
        for ref in delta_refs[1:]:
            delta = delta + ref[row].astype(jnp.float32)
        query = query + delta
        live = live_ref[row] > 0
        for kv in range(kv_heads):
            mine = query[kv * group : (kv + 1) * group].astype(jnp.bfloat16)
            score = lax.dot_general(
                mine,
                key_ref[row, kv],
                (((1,), (1,)), ((), ())),
                preferred_element_type=jnp.float32,
            )
            scores.append(jnp.where(live, score * scale, jnp.float32(-1e30)))
    scores = jnp.concatenate(scores, axis=0)
    grown = jnp.exp(scores - jnp.max(scores, axis=1, keepdims=True))
    weights = grown / jnp.sum(grown, axis=1, keepdims=True)
    for row in range(rows):
        for kv in range(kv_heads):
            at = (row * kv_heads + kv) * group
            rows_ref[row, kv * group : (kv + 1) * group, :] = jnp.dot(
                weights[at : at + group].astype(jnp.bfloat16),
                value_ref[row, kv],
                preferred_element_type=jnp.float32,
            )
    for head in range(heads):
        out_ref[:, head * LANES : (head + 1) * LANES] = rows_ref[:, head, :].astype(out_ref.dtype)


def shared_deltas(hidden, adapter_down, adapter_up, adapter_ids, block):
    rows, heads, head_size = block
    owners, cores = lax.axis_size("store"), len(TURNS)

    def turn_pairs(turn):
        return [
            (i * cores + core, (i ^ TURNS[core][turn]) * cores + core)
            for i in range(owners)
            for core in range(cores)
        ]

    def visit(array, turn):
        return lax.ppermute(array, ("store", "tensor"), turn_pairs(turn))

    def swap(array):
        return lax.ppermute(array, "tensor", [(0, 1), (1, 0)])

    states = [visit(hidden, turn) for turn in range(SENT)]
    other = swap(adapter_up)
    ids = scalars(adapter_ids, adapter_down, adapter_up)
    down, up, other = near(adapter_down), near(adapter_up), near(other)
    wide = (rows, cores, heads, head_size)

    def work(name, after, *turns):
        amount = len(turns)
        return pl.pallas_call(
            functools.partial(owner_kernel, turns),
            out_shape=[jax.ShapeDtypeStruct(wide, jnp.bfloat16)] * amount,
            in_specs=[SMEM] + [VMEM] * (amount + 3) + [pl.BlockSpec(memory_space=pl.ANY)] * len(after),
            out_specs=[VMEM] * amount,
            scratch_shapes=[
                pltpu.VMEM((amount,) + hidden.shape, jnp.float32),
                pltpu.VMEM((amount,) + wide, jnp.bfloat16),
                pltpu.VMEM((heads, head_size), jnp.float32),
            ],
            compiler_params=PARAMS,
            name=name,
        )(ids, down, up, other, *[states[turn] for turn in turns], *after)

    states.append(near(hidden))
    deltas = []
    for group in GROUPS:
        after = [deltas[others[0]] for others in GROUPS if others[0] < group[0]][-1:]
        deltas += work("owner%d" % group[0], after, *group)
    came = [visit(delta, turn) for turn, delta in enumerate(deltas[:SENT])]
    kept, sent = pl.pallas_call(
        merge_kernel,
        out_shape=[jax.ShapeDtypeStruct(block, jnp.bfloat16)] * 2,
        in_specs=[VMEM] * (SENT + 1),
        out_specs=[VMEM] * 2,
        compiler_params=PARAMS,
        name="merge",
    )(deltas[-1], *came)
    return [kept, swap(sent)]


def exchanged_deltas(hidden, adapter_down, adapter_up, adapter_ids, block):
    count, rank, width = adapter_down.shape
    owners, rows = lax.axis_size("store"), hidden.shape[0]
    copies = jnp.broadcast_to(hidden[None], (owners,) + hidden.shape)
    everyone = lax.all_to_all(copies, "store", 0, 0, tiled=True).reshape(owners * rows, width)
    slot = adapter_ids - lax.axis_index("store") * count
    owned = slot[:, None] == jnp.arange(count, dtype=jnp.int32)[None, :]
    low = jnp.einsum(
        "rd,kd->rk",
        everyone,
        adapter_down.reshape(count * rank, width),
        preferred_element_type=jnp.float32,
    ).reshape(owners * rows, count, rank)
    low = (low * owned[:, :, None].astype(jnp.float32)).astype(jnp.bfloat16)
    parts = jnp.dot(
        low.reshape(owners * rows, count * rank),
        adapter_up.reshape(count * rank, -1),
        preferred_element_type=jnp.float32,
    )
    came = lax.all_to_all(parts.reshape((owners,) + block), "store", 0, 0, tiled=True)
    return [jnp.sum(came, axis=0)]


def per_device(
    hidden, query_base, adapter_down, adapter_up, adapter_ids, key_cache, value_cache, kv_lengths
):
    features = adapter_up.shape[2]
    rows, kv_heads, slots, head_size = key_cache.shape
    block = (rows, features // head_size, head_size)
    shared = (lax.axis_size("store"), lax.axis_size("tensor")) == (8, len(TURNS))
    deltas = (shared_deltas if shared else exchanged_deltas)(
        hidden, adapter_down, adapter_up, adapter_ids, block
    )
    live = jnp.arange(slots, dtype=jnp.int32)[None, None, :] < kv_lengths[:, None, None]
    return pl.pallas_call(
        functools.partial(attend_kernel, len(deltas)),
        out_shape=jax.ShapeDtypeStruct((rows, features), jnp.bfloat16),
        in_specs=[VMEM] * (len(deltas) + 4),
        out_specs=VMEM,
        scratch_shapes=[pltpu.VMEM(block, jnp.float32)],
        compiler_params=PARAMS,
        name="attend",
    )(
        near(live.astype(jnp.float32)),
        near(query_base.reshape(block)),
        *deltas,
        near(key_cache),
        near(value_cache),
    )


def solution(mesh):
    in_specs = (
        P(("groups", "store"), None),
        P(("groups", "store"), "tensor"),
        P(("groups", "store"), None, None),
        P(("groups", "store"), None, "tensor"),
        P("groups"),
        P(("groups", "store"), "tensor", None, None),
        P(("groups", "store"), "tensor", None, None),
        P(("groups", "store")),
    )
    out_specs = P(("groups", "store"), "tensor")
    return jax.shard_map(
        per_device, mesh=mesh, in_specs=in_specs, out_specs=out_specs, check_vma=False
    )
```

```python
import functools

import jax
import jax.numpy as jnp
from jax import lax
from jax.experimental import pallas as pl
from jax.experimental.pallas import tpu as pltpu
from jax.sharding import PartitionSpec as P

HEADS = 64
KVH = 8
LANES = 128
CHUNK = 1024
VMEM_LIMIT = 32 * 1024 * 1024
VMEM = pl.BlockSpec(memory_space=pltpu.VMEM)
SMEM = pl.BlockSpec(memory_space=pltpu.SMEM)
PARAMS = pltpu.CompilerParams(vmem_limit_bytes=VMEM_LIMIT)
TURNS = ((3, 1, 4, 2, 0), (7, 1, 5, 6, 0))
SENT = len(TURNS[0]) - 1
GROUPS = ((0, 1), (2, 3), (4,))
SHARED = [first == second for first, second in zip(*TURNS)]


def scalars_kernel(ids_hbm, *refs):
    ids_ref, arrived = refs[-2:]
    copy = pltpu.make_async_copy(ids_hbm, ids_ref, arrived)
    copy.start()
    copy.wait()


def scalars(ids, *beside):
    size = sum(array.size * array.dtype.itemsize for array in beside)
    return pl.pallas_call(
        scalars_kernel,
        out_shape=pltpu.SMEM(ids.shape, ids.dtype),
        in_specs=[pl.BlockSpec(memory_space=pl.ANY)] * (1 + len(beside)),
        out_specs=SMEM,
        scratch_shapes=[pltpu.SemaphoreType.DMA(())],
        compiler_params=PARAMS,
        cost_estimate=pl.CostEstimate(flops=0, transcendentals=0, bytes_accessed=size),
        name="scalars",
    )(*[pltpu.with_memory_space_constraint(array, pltpu.HBM) for array in (ids,) + beside])


def near(array):
    return pltpu.with_memory_space_constraint(array, pltpu.VMEM)


def owner_kernel(turns, ids_ref, down_ref, mine_ref, other_ref, *refs):
    amount = len(turns)
    hidden_refs, (delta_refs, scratch) = refs[:amount], (refs[-3 - amount : -3], refs[-3:])
    state_ref, sum_ref, row_ref = scratch
    count, rank, width = down_ref.shape
    rows = state_ref.shape[1]
    heads = row_ref.shape[0]
    me, core = lax.axis_index("store"), lax.axis_index("tensor")

    def slot_of(partners, row, shared):
        source = me ^ jnp.where(core == 0, partners[0], partners[1])
        slot = ids_ref[source * rows + row] - me * count
        mine = jnp.logical_not(shared) | (core == lax.rem(row, len(TURNS)))
        return slot, mine & (slot >= 0) & (slot < count)

    owned = {}
    for i, turn in enumerate(turns):
        for row in range(rows):
            owned[i, row] = slot_of([steps[turn] for steps in TURNS], row, SHARED[turn])[1]

            @pl.when(owned[i, row])
            def _():
                state_ref[i, row : row + 1] = hidden_refs[i][row : row + 1, :].astype(jnp.float32)

        delta_refs[i][...] = jnp.zeros(delta_refs[i].shape, delta_refs[i].dtype)

    packed = [sum(steps[turn] << (4 * i) for i, turn in enumerate(turns)) for steps in TURNS]
    both = sum(SHARED[turn] << i for i, turn in enumerate(turns))

    def one_request(index, carry):
        i, row = lax.div(index, rows), lax.rem(index, rows)
        partners = [(jnp.int32(value) >> (4 * i)) & 15 for value in packed]
        slot, here = slot_of(partners, row, ((jnp.int32(both) >> i) & 1) == 1)

        @pl.when(here)
        def _():
            total = jnp.zeros((rank, CHUNK), jnp.float32)
            for start in range(0, width, CHUNK):
                down = down_ref[slot, :, start : start + CHUNK].astype(jnp.float32)
                total = total + down * state_ref[i, pl.ds(row, 1), start : start + CHUNK]
            low = jnp.sum(total, axis=1, keepdims=True)
            low = low.astype(jnp.bfloat16).astype(jnp.float32)
            for half, up_ref in ((core, mine_ref), (1 - core, other_ref)):
                for head in range(heads):
                    up = up_ref[slot, :, head * LANES : (head + 1) * LANES]
                    row_ref[head : head + 1, :] = jnp.sum(
                        up.astype(jnp.float32) * low, axis=0, keepdims=True
                    )
                sum_ref[i, row, half] = row_ref[...].astype(sum_ref.dtype)

        return carry

    lax.fori_loop(0, amount * rows, one_request, 0)
    for (i, row), here in owned.items():

        @pl.when(here)
        def _():
            delta_refs[i][row] = sum_ref[i, row]


def merge_kernel(own_ref, *refs):
    came_refs, (kept_ref, sent_ref) = refs[:-2], refs[-2:]
    core = lax.axis_index("tensor")
    for half, out_ref in ((core, kept_ref), (1 - core, sent_ref)):
        total = own_ref[:, half].astype(jnp.float32)
        for came_ref in came_refs:
            total = total + came_ref[:, half].astype(jnp.float32)
        out_ref[...] = total.astype(out_ref.dtype)


def attend_kernel(parts, live_ref, base_ref, *refs):
    delta_refs, (key_ref, value_ref, out_ref, rows_ref) = refs[:parts], refs[parts:]
    rows, kv_heads, slots, head_size = key_ref.shape
    heads = base_ref.shape[1]
    group = heads // kv_heads
    scale = 1.0 / (float(head_size) ** 0.5)
    scores = []
    for row in range(rows):
        query = base_ref[row].astype(jnp.float32)
        delta = delta_refs[0][row].astype(jnp.float32)
        for ref in delta_refs[1:]:
            delta = delta + ref[row].astype(jnp.float32)
        query = query + delta
        live = live_ref[row] > 0
        for kv in range(kv_heads):
            mine = query[kv * group : (kv + 1) * group].astype(jnp.bfloat16)
            score = lax.dot_general(
                mine,
                key_ref[row, kv],
                (((1,), (1,)), ((), ())),
                preferred_element_type=jnp.float32,
            )
            scores.append(jnp.where(live, score * scale, jnp.float32(-1e30)))
    scores = jnp.concatenate(scores, axis=0)
    grown = jnp.exp(scores - jnp.max(scores, axis=1, keepdims=True))
    weights = grown * (1.0 / jnp.sum(grown, axis=1, keepdims=True))
    for row in range(rows):
        for kv in range(kv_heads):
            at = (row * kv_heads + kv) * group
            rows_ref[row, kv * group : (kv + 1) * group, :] = jnp.dot(
                weights[at : at + group].astype(jnp.bfloat16),
                value_ref[row, kv],
                preferred_element_type=jnp.float32,
            )
    for head in range(heads):
        out_ref[:, head * LANES : (head + 1) * LANES] = rows_ref[:, head, :].astype(out_ref.dtype)


def shared_deltas(hidden, adapter_down, adapter_up, adapter_ids, block):
    rows, heads, head_size = block
    owners, cores = lax.axis_size("store"), len(TURNS)

    def turn_pairs(turn):
        return [
            (i * cores + core, (i ^ TURNS[core][turn]) * cores + core)
            for i in range(owners)
            for core in range(cores)
        ]

    def visit(array, turn):
        return lax.ppermute(array, ("store", "tensor"), turn_pairs(turn))

    def swap(array):
        return lax.ppermute(array, "tensor", [(0, 1), (1, 0)])

    states = [visit(hidden, turn) for turn in range(SENT)]
    other = swap(adapter_up)
    ids = scalars(adapter_ids, adapter_down, adapter_up)
    down, up, other = near(adapter_down), near(adapter_up), near(other)
    wide = (rows, cores, heads, head_size)

    def work(name, after, *turns):
        amount = len(turns)
        return pl.pallas_call(
            functools.partial(owner_kernel, turns),
            out_shape=[jax.ShapeDtypeStruct(wide, jnp.bfloat16)] * amount,
            in_specs=[SMEM] + [VMEM] * (amount + 3) + [pl.BlockSpec(memory_space=pl.ANY)] * len(after),
            out_specs=[VMEM] * amount,
            scratch_shapes=[
                pltpu.VMEM((amount,) + hidden.shape, jnp.float32),
                pltpu.VMEM((amount,) + wide, jnp.bfloat16),
                pltpu.VMEM((heads, head_size), jnp.float32),
            ],
            compiler_params=PARAMS,
            name=name,
        )(ids, down, up, other, *[states[turn] for turn in turns], *after)

    states.append(near(hidden))
    deltas = []
    for group in GROUPS:
        after = [deltas[others[0]] for others in GROUPS if others[0] < group[0]][-1:]
        deltas += work("owner%d" % group[0], after, *group)
    came = [visit(delta, turn) for turn, delta in enumerate(deltas[:SENT])]
    kept, sent = pl.pallas_call(
        merge_kernel,
        out_shape=[jax.ShapeDtypeStruct(block, jnp.bfloat16)] * 2,
        in_specs=[VMEM] * (SENT + 1),
        out_specs=[VMEM] * 2,
        compiler_params=PARAMS,
        name="merge",
    )(deltas[-1], *came)
    return [kept, swap(sent)]


def exchanged_deltas(hidden, adapter_down, adapter_up, adapter_ids, block):
    count, rank, width = adapter_down.shape
    owners, rows = lax.axis_size("store"), hidden.shape[0]
    copies = jnp.broadcast_to(hidden[None], (owners,) + hidden.shape)
    everyone = lax.all_to_all(copies, "store", 0, 0, tiled=True).reshape(owners * rows, width)
    slot = adapter_ids - lax.axis_index("store") * count
    owned = slot[:, None] == jnp.arange(count, dtype=jnp.int32)[None, :]
    low = jnp.einsum(
        "rd,kd->rk",
        everyone,
        adapter_down.reshape(count * rank, width),
        preferred_element_type=jnp.float32,
    ).reshape(owners * rows, count, rank)
    low = (low * owned[:, :, None].astype(jnp.float32)).astype(jnp.bfloat16)
    parts = jnp.dot(
        low.reshape(owners * rows, count * rank),
        adapter_up.reshape(count * rank, -1),
        preferred_element_type=jnp.float32,
    )
    came = lax.all_to_all(parts.reshape((owners,) + block), "store", 0, 0, tiled=True)
    return [jnp.sum(came, axis=0)]


def per_device(
    hidden, query_base, adapter_down, adapter_up, adapter_ids, key_cache, value_cache, kv_lengths
):
    features = adapter_up.shape[2]
    rows, kv_heads, slots, head_size = key_cache.shape
    block = (rows, features // head_size, head_size)
    shared = (lax.axis_size("store"), lax.axis_size("tensor")) == (8, len(TURNS))
    deltas = (shared_deltas if shared else exchanged_deltas)(
        hidden, adapter_down, adapter_up, adapter_ids, block
    )
    live = jnp.arange(slots, dtype=jnp.int32)[None, None, :] < kv_lengths[:, None, None]
    return pl.pallas_call(
        functools.partial(attend_kernel, len(deltas)),
        out_shape=jax.ShapeDtypeStruct((rows, features), jnp.bfloat16),
        in_specs=[VMEM] * (len(deltas) + 4),
        out_specs=VMEM,
        scratch_shapes=[pltpu.VMEM(block, jnp.float32)],
        compiler_params=PARAMS,
        name="attend",
    )(
        near(live.astype(jnp.float32)),
        near(query_base.reshape(block)),
        *deltas,
        near(key_cache),
        near(value_cache),
    )


def solution(mesh):
    in_specs = (
        P(("groups", "store"), None),
        P(("groups", "store"), "tensor"),
        P(("groups", "store"), None, None),
        P(("groups", "store"), None, "tensor"),
        P("groups"),
        P(("groups", "store"), "tensor", None, None),
        P(("groups", "store"), "tensor", None, None),
        P(("groups", "store")),
    )
    out_specs = P(("groups", "store"), "tensor")
    return jax.shard_map(
        per_device, mesh=mesh, in_specs=in_specs, out_specs=out_specs, check_vma=False
    )
```

```python
import functools

import jax
import jax.numpy as jnp
from jax import lax
from jax.experimental import pallas as pl
from jax.experimental.pallas import tpu as pltpu
from jax.sharding import PartitionSpec as P

HEADS = 64
KVH = 8
LANES = 128
CHUNK = 1024
VMEM_LIMIT = 32 * 1024 * 1024
VMEM = pl.BlockSpec(memory_space=pltpu.VMEM)
SMEM = pl.BlockSpec(memory_space=pltpu.SMEM)
PARAMS = pltpu.CompilerParams(vmem_limit_bytes=VMEM_LIMIT)
TURNS = ((3, 1, 4, 2, 0), (7, 1, 5, 6, 0))
SENT = len(TURNS[0]) - 1
GROUPS = ((0, 1), (2, 3), (4,))
SHARED = [first == second for first, second in zip(*TURNS)]


def scalars_kernel(ids_hbm, *refs):
    ids_ref, arrived = refs[-2:]
    copy = pltpu.make_async_copy(ids_hbm, ids_ref, arrived)
    copy.start()
    copy.wait()


def scalars(ids, *beside):
    size = sum(array.size * array.dtype.itemsize for array in beside)
    return pl.pallas_call(
        scalars_kernel,
        out_shape=pltpu.SMEM(ids.shape, ids.dtype),
        in_specs=[pl.BlockSpec(memory_space=pl.ANY)] * (1 + len(beside)),
        out_specs=SMEM,
        scratch_shapes=[pltpu.SemaphoreType.DMA(())],
        compiler_params=PARAMS,
        cost_estimate=pl.CostEstimate(flops=0, transcendentals=0, bytes_accessed=size),
        name="scalars",
    )(*[pltpu.with_memory_space_constraint(array, pltpu.HBM) for array in (ids,) + beside])


def near(array):
    return pltpu.with_memory_space_constraint(array, pltpu.VMEM)


def owner_kernel(turns, ids_ref, down_ref, mine_ref, other_ref, *refs):
    amount = len(turns)
    hidden_refs, (delta_refs, scratch) = refs[:amount], (refs[-3 - amount : -3], refs[-3:])
    state_ref, sum_ref, row_ref = scratch
    count, rank, width = down_ref.shape
    rows = state_ref.shape[1]
    heads = row_ref.shape[0]
    me, core = lax.axis_index("store"), lax.axis_index("tensor")

    def slot_of(partners, row, shared):
        source = me ^ jnp.where(core == 0, partners[0], partners[1])
        slot = ids_ref[source * rows + row] - me * count
        mine = jnp.logical_not(shared) | (core == lax.rem(row, len(TURNS)))
        return slot, mine & (slot >= 0) & (slot < count)

    owned = {}
    for i, turn in enumerate(turns):
        for row in range(rows):
            owned[i, row] = slot_of([steps[turn] for steps in TURNS], row, SHARED[turn])[1]

            @pl.when(owned[i, row])
            def _():
                state_ref[i, row : row + 1] = hidden_refs[i][row : row + 1, :].astype(jnp.float32)

        delta_refs[i][...] = jnp.zeros(delta_refs[i].shape, delta_refs[i].dtype)

    packed = [sum(steps[turn] << (4 * i) for i, turn in enumerate(turns)) for steps in TURNS]
    both = sum(SHARED[turn] << i for i, turn in enumerate(turns))

    def one_request(index, carry):
        i, row = lax.div(index, rows), lax.rem(index, rows)
        partners = [(jnp.int32(value) >> (4 * i)) & 15 for value in packed]
        slot, here = slot_of(partners, row, ((jnp.int32(both) >> i) & 1) == 1)

        @pl.when(here)
        def _():
            total = jnp.zeros((rank, CHUNK), jnp.float32)
            for start in range(0, width, CHUNK):
                down = down_ref[slot, :, start : start + CHUNK].astype(jnp.float32)
                total = total + down * state_ref[i, pl.ds(row, 1), start : start + CHUNK]
            low = jnp.sum(total, axis=1, keepdims=True)
            low = low.astype(jnp.bfloat16).astype(jnp.float32)
            for half, up_ref in ((core, mine_ref), (1 - core, other_ref)):
                for head in range(heads):
                    up = up_ref[slot, :, head * LANES : (head + 1) * LANES]
                    row_ref[head : head + 1, :] = jnp.sum(
                        up.astype(jnp.float32) * low, axis=0, keepdims=True
                    )
                sum_ref[i, row, half] = row_ref[...].astype(sum_ref.dtype)

        return carry

    lax.fori_loop(0, amount * rows, one_request, 0)
    for (i, row), here in owned.items():

        @pl.when(here)
        def _():
            delta_refs[i][row] = sum_ref[i, row]


def merge_kernel(own_ref, *refs):
    came_refs, (kept_ref, sent_ref) = refs[:-2], refs[-2:]
    core = lax.axis_index("tensor")
    for half, out_ref in ((core, kept_ref), (1 - core, sent_ref)):
        total = own_ref[:, half].astype(jnp.float32)
        for came_ref in came_refs:
            total = total + came_ref[:, half].astype(jnp.float32)
        out_ref[...] = total.astype(out_ref.dtype)


def turn_kernel(key_ref, turned_ref):
    for row in range(key_ref.shape[0]):
        for kv in range(key_ref.shape[1]):
            turned_ref[row, kv] = key_ref[row, kv].T


def attend_kernel(parts, live_ref, base_ref, *refs):
    delta_refs, (key_ref, value_ref, out_ref, rows_ref) = refs[:parts], refs[parts:]
    rows, kv_heads, slots, head_size = value_ref.shape
    heads = base_ref.shape[1]
    group = heads // kv_heads
    scale = 1.0 / (float(head_size) ** 0.5)
    scores = []
    for row in range(rows):
        query = base_ref[row].astype(jnp.float32)
        delta = delta_refs[0][row].astype(jnp.float32)
        for ref in delta_refs[1:]:
            delta = delta + ref[row].astype(jnp.float32)
        query = query + delta
        live = live_ref[row] > 0
        for kv in range(kv_heads):
            mine = query[kv * group : (kv + 1) * group].astype(jnp.bfloat16)
            score = lax.dot_general(
                mine,
                key_ref[row, kv],
                (((1,), (0,)), ((), ())),
                preferred_element_type=jnp.float32,
            )
            scores.append(jnp.where(live, score * scale, jnp.float32(-1e30)))
    scores = jnp.concatenate(scores, axis=0)
    grown = jnp.exp(scores - jnp.max(scores, axis=1, keepdims=True))
    weights = grown * (1.0 / jnp.sum(grown, axis=1, keepdims=True))
    for row in range(rows):
        for kv in range(kv_heads):
            at = (row * kv_heads + kv) * group
            rows_ref[row, kv * group : (kv + 1) * group, :] = jnp.dot(
                weights[at : at + group].astype(jnp.bfloat16),
                value_ref[row, kv],
                preferred_element_type=jnp.float32,
            )
    for head in range(heads):
        out_ref[:, head * LANES : (head + 1) * LANES] = rows_ref[:, head, :].astype(out_ref.dtype)


def shared_deltas(hidden, adapter_down, adapter_up, adapter_ids, block):
    rows, heads, head_size = block
    owners, cores = lax.axis_size("store"), len(TURNS)

    def turn_pairs(turn):
        return [
            (i * cores + core, (i ^ TURNS[core][turn]) * cores + core)
            for i in range(owners)
            for core in range(cores)
        ]

    def visit(array, turn):
        return lax.ppermute(array, ("store", "tensor"), turn_pairs(turn))

    def swap(array):
        return lax.ppermute(array, "tensor", [(0, 1), (1, 0)])

    states = [visit(hidden, turn) for turn in range(SENT)]
    other = swap(adapter_up)
    ids = scalars(adapter_ids, adapter_down, adapter_up)
    down, up, other = near(adapter_down), near(adapter_up), near(other)
    wide = (rows, cores, heads, head_size)

    def work(name, after, *turns):
        amount = len(turns)
        return pl.pallas_call(
            functools.partial(owner_kernel, turns),
            out_shape=[jax.ShapeDtypeStruct(wide, jnp.bfloat16)] * amount,
            in_specs=[SMEM] + [VMEM] * (amount + 3) + [pl.BlockSpec(memory_space=pl.ANY)] * len(after),
            out_specs=[VMEM] * amount,
            scratch_shapes=[
                pltpu.VMEM((amount,) + hidden.shape, jnp.float32),
                pltpu.VMEM((amount,) + wide, jnp.bfloat16),
                pltpu.VMEM((heads, head_size), jnp.float32),
            ],
            compiler_params=PARAMS,
            name=name,
        )(ids, down, up, other, *[states[turn] for turn in turns], *after)

    states.append(near(hidden))
    deltas = []
    for group in GROUPS:
        after = [deltas[others[0]] for others in GROUPS if others[0] < group[0]][-1:]
        deltas += work("owner%d" % group[0], after, *group)
    came = [visit(delta, turn) for turn, delta in enumerate(deltas[:SENT])]
    kept, sent = pl.pallas_call(
        merge_kernel,
        out_shape=[jax.ShapeDtypeStruct(block, jnp.bfloat16)] * 2,
        in_specs=[VMEM] * (SENT + 1),
        out_specs=[VMEM] * 2,
        compiler_params=PARAMS,
        name="merge",
    )(deltas[-1], *came)
    return [kept, swap(sent)]


def exchanged_deltas(hidden, adapter_down, adapter_up, adapter_ids, block):
    count, rank, width = adapter_down.shape
    owners, rows = lax.axis_size("store"), hidden.shape[0]
    copies = jnp.broadcast_to(hidden[None], (owners,) + hidden.shape)
    everyone = lax.all_to_all(copies, "store", 0, 0, tiled=True).reshape(owners * rows, width)
    slot = adapter_ids - lax.axis_index("store") * count
    owned = slot[:, None] == jnp.arange(count, dtype=jnp.int32)[None, :]
    low = jnp.einsum(
        "rd,kd->rk",
        everyone,
        adapter_down.reshape(count * rank, width),
        preferred_element_type=jnp.float32,
    ).reshape(owners * rows, count, rank)
    low = (low * owned[:, :, None].astype(jnp.float32)).astype(jnp.bfloat16)
    parts = jnp.dot(
        low.reshape(owners * rows, count * rank),
        adapter_up.reshape(count * rank, -1),
        preferred_element_type=jnp.float32,
    )
    came = lax.all_to_all(parts.reshape((owners,) + block), "store", 0, 0, tiled=True)
    return [jnp.sum(came, axis=0)]


def per_device(
    hidden, query_base, adapter_down, adapter_up, adapter_ids, key_cache, value_cache, kv_lengths
):
    features = adapter_up.shape[2]
    rows, kv_heads, slots, head_size = key_cache.shape
    block = (rows, features // head_size, head_size)
    shared = (lax.axis_size("store"), lax.axis_size("tensor")) == (8, len(TURNS))
    deltas = (shared_deltas if shared else exchanged_deltas)(
        hidden, adapter_down, adapter_up, adapter_ids, block
    )
    turned = pl.pallas_call(
        turn_kernel,
        out_shape=jax.ShapeDtypeStruct((rows, kv_heads, head_size, slots), key_cache.dtype),
        in_specs=[VMEM],
        out_specs=VMEM,
        compiler_params=PARAMS,
        name="turn",
    )(near(key_cache))
    live = jnp.arange(slots, dtype=jnp.int32)[None, None, :] < kv_lengths[:, None, None]
    return pl.pallas_call(
        functools.partial(attend_kernel, len(deltas)),
        out_shape=jax.ShapeDtypeStruct((rows, features), jnp.bfloat16),
        in_specs=[VMEM] * (len(deltas) + 4),
        out_specs=VMEM,
        scratch_shapes=[pltpu.VMEM(block, jnp.float32)],
        compiler_params=PARAMS,
        name="attend",
    )(
        near(live.astype(jnp.float32)),
        near(query_base.reshape(block)),
        *deltas,
        near(turned),
        near(value_cache),
    )


def solution(mesh):
    in_specs = (
        P(("groups", "store"), None),
        P(("groups", "store"), "tensor"),
        P(("groups", "store"), None, None),
        P(("groups", "store"), None, "tensor"),
        P("groups"),
        P(("groups", "store"), "tensor", None, None),
        P(("groups", "store"), "tensor", None, None),
        P(("groups", "store")),
    )
    out_specs = P(("groups", "store"), "tensor")
    return jax.shard_map(
        per_device, mesh=mesh, in_specs=in_specs, out_specs=out_specs, check_vma=False
    )
```
